512 devices in a mesh: bins: 64 (over y, x, z_hi), lon: 8 (over z_lo, core).
Axes of the slice: x: 4, y: 8, z: 8 (z_hi: 2, z_lo: 4; z = z_hi * 4 + z_lo), core: 2. Of those that a mesh axis runs over, the one named last changes fastest.
Arguments:
- spectrum: float32 [1152, 512, 128], P('bins', 'lon'), may hold values from 0.05 to 2
- wind_speed: float32 [512, 128], P('lon'), may hold values from 2 to 20
- wind_dir: float32 [512, 128], P('lon'), may hold values from -3.140625 to 3.140625
- flags: int32 [512, 128], P('lon'), may hold values from 0 to 2
Outputs:
- spectrum_out: float32 [1152, 512, 128], P('bins', 'lon')
The draws below stay inside these ranges and needn't reach their ends.
Inputs may be any that keep to these rules, and one draw needn't show every extreme that they name: `flags`: 0 marks land, 1 open sea, 2 sea ice.
All inputs are finite; a program needn't handle non-finite values.
Results may differ from the reference program's by a relative error of at most 0.0003.
Values sent between devices are 32-bit elements; how exact they have to be, the bound alone decides.
A program may use at most 64 MiB of HBM per device.

```python
import math
import jax
import jax.numpy as jnp
from jax import lax

NF = 32
ND = 36
LAT = 128
LON_DEV = 64
STEPS = 2
NB = 1152
NLON = 512
N_LON = 8


def place_ends(result, stream_key, smallest, top_value):
    longest = result.shape.index(max(result.shape))
    spots = []
    for shift in (0, 1):
        where = [jax.random.randint(jax.random.fold_in(stream_key, axis), (), 0, length) for axis, length in enumerate(result.shape)]
        where[longest] = (where[longest] + shift) % result.shape[longest]
        spots.append(tuple(where))
    return result.at[spots[0]].set(smallest).at[spots[1]].set(top_value)


def steps_of(own_key, extent, pieces, smallest, top_value):
    level = 1.0
    for dim, parts in pieces:
        draws = jax.random.uniform(jax.random.fold_in(jax.random.fold_in(own_key, 6), dim), (parts,), jnp.float32, smallest / len(pieces), top_value / len(pieces))
        level = level * jnp.repeat(jnp.exp(draws), extent[dim] // parts).reshape((-1,) + (1,) * (len(extent) - 1 - dim))
    return level


def setup_inputs(seed: int = 0) -> dict:
    streams_of = jax.random.split(jax.random.key(seed), 5)
    return {
        "spectrum": jnp.clip(jnp.exp(math.log(2.0) - 3.6888794 * jax.random.uniform(streams_of[0], (NB, NLON, LAT), jnp.float32) ** steps_of(streams_of[0], (NB, NLON, LAT), ((0, 64), (1, 8)), -0.2, 0.2)), 0.05, 2.0),
        "wind_speed": jnp.clip(jnp.exp(math.log(20.0) - 2.3025851 * jax.random.uniform(streams_of[1], (NLON, LAT), jnp.float32) ** steps_of(streams_of[1], (NLON, LAT), ((0, 8),), -0.2, 0.2)), 2.0, 20.0),
        "wind_dir": jnp.clip(jax.random.uniform(streams_of[2], (NLON, LAT), jnp.float32, -3.140625, 3.140625), -3.140625, 3.140625),
        "flags": place_ends(jax.random.randint(streams_of[3], (NLON, LAT), 0, 3), jax.random.fold_in(streams_of[3], 1), 0, 2).astype(jnp.int32),
    }


wind_gain = 0.5
quad_gain = 0.3
break_gain = 0.3
ice_loss = 1.0
courant = 0.6


def spectral_tables(index, nfreq, ndir):
    direction = (index // nfreq).astype(jnp.float32)
    level = (index % nfreq).astype(jnp.float32)
    theta = direction * (2.0 * math.pi / ndir)
    ratio = jnp.power(1.05, level - nfreq // 2)
    group = jnp.power(1.1, -level)
    return theta, ratio, group, index % nfreq


def courants(theta, group, rows):
    lines = jnp.arange(rows).astype(jnp.float32)
    coslat = jnp.cos((lines - rows / 2 + 0.5) * (0.25 * math.pi / 180.0))
    east = courant * group * jnp.cos(theta) / coslat
    north = courant * group * jnp.sin(theta)
    return east, north


def sources(field, upper, lower, spread, theta, ratio, speed, heading, kinds):
    forcing = wind_gain * (speed * 0.1) * ratio * jnp.maximum(jnp.cos(theta - heading), 0.0) * field
    quad = quad_gain * ratio * (field * field * (upper + lower) - 2.0 * field * upper * lower)
    damping = break_gain * ratio * ratio * spread
    grown = (field + forcing + quad) / (1.0 + damping)
    frozen = field / (1.0 + damping + ice_loss)
    return jnp.where(kinds == 1, grown, jnp.where(kinds == 2, frozen, 0.0))


def upwind(padded, axis, length):
    def cells(offset):
        return lax.slice_in_dim(padded, 3 + offset, 3 + offset + length, axis=axis)
    plus = (-2.0 * cells(-3) + 15.0 * cells(-2) - 60.0 * cells(-1) + 20.0 * cells(0) + 30.0 * cells(1) - 3.0 * cells(2)) / 60.0
    minus = (3.0 * cells(-2) - 30.0 * cells(-1) - 20.0 * cells(0) + 60.0 * cells(1) - 15.0 * cells(2) + 2.0 * cells(3)) / 60.0
    return plus, minus


def tendency(extended, east, north):
    width = extended.shape[1] - 6
    inner = extended[:, 3:-3, :]
    east_plus, east_minus = upwind(extended, 1, width)
    padded = jnp.pad(inner, ((0, 0), (0, 0), (3, 3)))
    north_plus, north_minus = upwind(padded, 2, inner.shape[2])
    return -(east * jnp.where(east >= 0.0, east_plus, east_minus) + north * jnp.where(north >= 0.0, north_plus, north_minus))


def wrapped(field):
    return jnp.concatenate([field[:, -3:], field, field[:, :3]], axis=1)


def reference(spectrum, wind_speed, wind_dir, flags):
    total = NF * ND
    nlon = N_LON * LON_DEV
    index = jnp.arange(total, dtype=jnp.int32)
    theta, ratio, group, level = spectral_tables(index, NF, ND)
    column = (total, 1, 1)
    theta_c = theta.reshape(column)
    ratio_c = ratio.reshape(column)
    upper_ok = (level + 2 < NF).reshape(column)
    lower_ok = (level >= 2).reshape(column)
    speed_blocks = wind_speed.reshape(N_LON, LON_DEV, LAT)
    heading_blocks = wind_dir.reshape(N_LON, LON_DEV, LAT)
    kind_blocks = flags.reshape(N_LON, LON_DEV, LAT)

    def source_block(args):
        block, speed, heading, kinds = args
        upper = jnp.where(upper_ok, jnp.roll(block, -(NF + 2), axis=0), 0.0)
        lower = jnp.where(lower_ok, jnp.roll(block, 3 * NF + 2, axis=0), 0.0)
        spread = jnp.sum(ratio_c * ratio_c * block * block, axis=0) / total
        return sources(block, upper, lower, spread, theta_c, ratio_c, speed, heading, kinds)

    def advect(args):
        group_field, direction = args
        local = direction * NF + jnp.arange(NF, dtype=jnp.int32)
        local_theta, local_ratio, local_group, local_level = spectral_tables(local, NF, ND)
        east, north = courants(local_theta.reshape(NF, 1, 1), local_group.reshape(NF, 1, 1), LAT)

        def rate(current):
            return tendency(wrapped(current), east, north)
        one = group_field + rate(group_field)
        two = 0.75 * group_field + 0.25 * (one + rate(one))
        return group_field / 3.0 + (2.0 / 3.0) * (two + rate(two))

    field = spectrum
    for step in range(STEPS):
        blocks = field.reshape(total, N_LON, LON_DEV, LAT).transpose(1, 0, 2, 3)
        blocks = lax.map(source_block, (blocks, speed_blocks, heading_blocks, kind_blocks))
        field = blocks.transpose(1, 0, 2, 3).reshape(total, nlon, LAT)
        field = lax.map(advect, (field.reshape(ND, NF, nlon, LAT), jnp.arange(ND, dtype=jnp.int32)))
        field = field.reshape(total, nlon, LAT)
        field = jnp.where(flags != 0, field, 0.0)
    return field
```

```python
import functools
import math

import jax
import jax.numpy as jnp
from jax import lax
from jax.experimental import pallas as pl
from jax.experimental.pallas import tpu as pltpu
from jax.sharding import PartitionSpec as P

NF = 32
ND = 36
STEPS = 2

wind_gain = 0.5
quad_gain = 0.3
break_gain = 0.3
ice_loss = 1.0
courant = 0.6

RING = 8
HALO = 9
BASE = 16
GROUP = 3
GROUPS = 6
LAG = 2
LEG = 2
PLUS = (-2.0, 15.0, -60.0, 20.0, 30.0, -3.0, 0.0)
MINUS = (0.0, 3.0, -30.0, -20.0, 60.0, -15.0, 2.0)

DIRECT = (
    (0, 0, 3, 2, -2), (0, 3, 3, 5, -2), (0, 6, 3, 8, -2), (0, 9, 3, 11, -2), (0, 12, 3, 14, -2), (0, 15, 1, 17, -2),
    (1, 16, 2, 6, 6),
)
SHARED = ((3, 12, 2, 0), (4, 14, 3, 2), (5, 17, 1, 5))
FAR = ((0, 16, 2, 0, -1), (1, 0, 3, 8, 1), (1, 3, 3, 11, -1), (1, 6, 3, 14, 1), (1, 9, 1, 17, -1))
KEPT_BACK = (1, 2)
S0, F0 = len(DIRECT), len(DIRECT) + len(SHARED)
PIECES = F0 + len(FAR)
NEEDS = (
    ((F0, 0, S0, S0 + 1), (1, S0 + 2), (2, 6, F0 + 1), (F0 + 2,), (F0 + 3,), (F0 + 4,)),
    ((F0, S0), (0, 1, S0 + 1, S0 + 2), (2, 6, F0 + 1), (F0 + 2,), (F0 + 3,), (F0 + 4,)),
)
FIRST_GROUP = (0, 1)

RATIO, COS, SIN, DAMP, UPPER, LOWER, EAST, WEST, NORTH, SOUTH = range(10)


def bin_table(index):
    direction = (index // NF).astype(jnp.float32)
    level = (index % NF).astype(jnp.float32)
    theta = direction * (2.0 * math.pi / ND)
    ratio = jnp.power(1.05, level - NF // 2)
    group = jnp.power(1.1, -level)
    east = courant * group * jnp.cos(theta)
    north = courant * group * jnp.sin(theta)
    ratio, theta, east, north, level = (v[:, None] for v in (ratio, theta, east, north, level))
    return jnp.concatenate(
        [
            ratio,
            jnp.cos(theta),
            jnp.sin(theta),
            break_gain * ratio * ratio / (NF * ND),
            (level + 2 < NF).astype(jnp.float32),
            (level >= 2).astype(jnp.float32),
            jnp.where(east >= 0.0, east / -60.0, 0.0),
            jnp.where(east >= 0.0, 0.0, east / -60.0),
            jnp.where(north >= 0.0, north / -60.0, 0.0),
            jnp.where(north >= 0.0, 0.0, north / -60.0),
        ],
        axis=1,
    )


def row_table(rows):
    lines = jnp.arange(rows)
    coslat = jnp.cos((lines.astype(jnp.float32) - rows / 2 + 0.5) * (0.25 * math.pi / 180.0))
    masks = [((lines + j >= 0) & (lines + j < rows)).astype(jnp.float32) for j in range(-3, 4)]
    return jnp.stack([1.0 / coslat] + masks, axis=0)


def kernel(
    field_hbm, speed_hbm, heading_hbm, flags_hbm, bins_ref, rows_ref, out_ref,
    first, later, last, got, relay, wide, one, two, speed, heading, flags, gain_x, gain_y, open_sea, ice,
    part, part_in, mid, mid_in, total,
    send_sem, got_sem, leg_send, leg_recv, halo_send, halo_recv,
    a_send, a_recv, b_send, b_recv, c_send, c_recv, in_sem, out_sem,
):
    here, columns, rows = field_hbm.shape
    count, sectors = lax.axis_size("bins"), lax.axis_size("lon")
    place, sector = lax.axis_index("bins"), lax.axis_index("lon")
    line, spot = place // RING, place % RING
    chunk = columns // RING
    def in_row(turn):
        return line * RING + (spot + turn) % RING

    def in_column(turn):
        return (line + turn) % RING * RING + spot

    def across(offset):
        return (place + offset + count) % count

    pair, far, core = place // 2, place % 2, sector % 2
    height = far * (sectors // 2) + sector // 2
    around_z = sectors

    def at(pair_offset, climb):
        new = (height + climb + around_z) % around_z
        new_pair = (pair + pair_offset + count // 2) % (count // 2)
        return {"bins": new_pair * 2 + new // (sectors // 2), "lon": new % (sectors // 2) * 2 + core}

    barrier = pltpu.get_barrier_semaphore()
    partners = [{"bins": across(s * o)} for o in (2, 6, 8) for s in (1, -1)]
    partners += [at(o, s * LEG) for o in (-3, -1, 0, 1, 3) for s in (1, -1)]
    partners += [{"bins": in_row(t)} for t in range(1, RING)]
    partners += [{"bins": in_column(t)} for t in range(1, RING)]
    partners += [{"lon": (sector + s + sectors) % sectors} for s in (1, -1)]
    for partner in partners:
        pl.semaphore_signal(barrier, inc=1, device_id=partner, device_id_type=pl.DeviceIdType.MESH)

    def send(src, dst, send_sem, recv_sem, device):
        return pltpu.make_async_remote_copy(
            src_ref=src, dst_ref=dst, send_sem=send_sem, recv_sem=recv_sem,
            device_id=device, device_id_type=pl.DeviceIdType.MESH,
        )

    def source_of(step):
        return field_hbm if step == 0 else later

    def field_of(step):
        return first if step == 0 else later

    def direct(step, piece):
        kind, b, bins, slot, places = DIRECT[piece]
        return send(
            source_of(step).at[pl.ds(b, bins)], got.at[step, kind, pl.ds(slot, bins)],
            send_sem.at[step, piece], got_sem.at[step, piece], {"bins": across(places)},
        )

    def shared(step, piece):
        _, slot, bins, new_slot = SHARED[piece]
        return send(
            got.at[step, 0, pl.ds(slot, bins)], got.at[step, 1, pl.ds(new_slot, bins)],
            send_sem.at[step, S0 + piece], got_sem.at[step, S0 + piece], {"bins": across(8)},
        )

    def leg(step, piece):
        kind, b, bins, _, way = FAR[piece]
        offset = 1 + 2 * far if kind else far - 1
        return send(
            source_of(step).at[pl.ds(b, bins)], relay.at[step, pl.ds(b, bins)],
            leg_send.at[step, piece], leg_recv.at[step, piece], at(offset, way * LEG),
        )

    def second_leg(step, piece):
        kind, b, bins, slot, way = FAR[piece]
        source_far = (height - way * LEG + around_z) % around_z // (sectors // 2)
        return send(
            relay.at[step, pl.ds(b, bins)], got.at[step, kind, pl.ds(slot, bins)],
            send_sem.at[step, F0 + piece], got_sem.at[step, F0 + piece], at(1 - source_far if kind else 0, way * LEG),
        )

    def arrival(step, piece):
        if piece < S0:
            return direct(step, piece)
        if piece < F0:
            return shared(step, piece - S0)
        return second_leg(step, piece - F0)

    def pass_on_far(step, pieces):
        for piece in pieces:
            leg(step, piece).wait_recv()
            second_leg(step, piece).start()

    def pass_on_shared(step):
        for piece, (before, *_) in enumerate(SHARED):
            direct(step, before).wait_recv()
            shared(step, piece).start()

    def halo_copy(step, group, side):
        if side == 0:
            src, dst, turn = BASE + columns - HALO, BASE - HALO, 1
        else:
            src, dst, turn = BASE, BASE + columns, -1
        ext = wide.at[step, pl.ds(group * GROUP, GROUP)]
        return send(
            ext.at[:, pl.ds(src, HALO)], ext.at[:, pl.ds(dst, HALO)],
            halo_send.at[step, side, group], halo_recv.at[step, side, group],
            {"lon": (sector + turn + sectors) % sectors},
        )

    def a_copy(step, turn):
        start = pl.multiple_of((spot + turn) % RING * chunk, chunk)
        return send(part.at[step, pl.ds(start, chunk)], part_in.at[step, turn], a_send.at[step, turn], a_recv.at[step, turn], {"bins": in_row(turn)})

    def b_copy(step, turn):
        return send(mid.at[step], mid_in.at[step, turn], b_send.at[step, turn], b_recv.at[step, turn], {"bins": in_column(turn)})

    def c_copy(step, turn):
        start = pl.multiple_of(spot * chunk, chunk)
        mine = total.at[step, pl.ds(start, chunk)]
        return send(mine, mine, c_send.at[step, turn], c_recv.at[step, turn], {"bins": in_row(turn)})

    def c_from(step, turn):
        start = pl.multiple_of((spot + RING - turn) % RING * chunk, chunk)
        theirs = total.at[step, pl.ds(start, chunk)]
        return send(theirs, theirs, c_send.at[step, turn], c_recv.at[step, turn], {"bins": in_row(turn)})

    def square(b, values):
        scaled = bins_ref[b, RATIO] * values
        return scaled * scaled

    def spread_a(step):
        for turn in range(1, RING):
            a_copy(step, turn).start()

    def spread_b(step):
        start = pl.multiple_of(spot * chunk, chunk)
        so_far = part[step, pl.ds(start, chunk)]
        for turn in range(1, RING):
            a_copy(step, turn).wait_recv()
            so_far += part_in[step, turn]
        mid[step] = so_far
        for turn in range(1, RING):
            b_copy(step, turn).start()

    def spread_c(step):
        start = pl.multiple_of(spot * chunk, chunk)
        so_far = mid[step]
        for turn in range(1, RING):
            b_copy(step, turn).wait_recv()
            so_far += mid_in[step, turn]
        total[step, pl.ds(start, chunk)] = so_far
        for turn in range(1, RING):
            c_copy(step, turn).start()

    def spread_end(step):
        for turn in range(1, RING):
            c_from(step, turn).wait_recv()

    def source(step, b):
        energy = field_of(step)[b]
        above = got[step, 0, b] * bins_ref[b, UPPER]
        below = got[step, 1, b] * bins_ref[b, LOWER]
        ratio = bins_ref[b, RATIO]
        wind = jnp.maximum(bins_ref[b, COS] * gain_x[...] + bins_ref[b, SIN] * gain_y[...], 0.0)
        quad = quad_gain * (energy * (above + below) - 2.0 * above * below)
        grown = energy + energy * (ratio * (wind + quad))
        top = jnp.where(open_sea[...] > 0.0, grown, energy)
        bottom = 1.0 + bins_ref[b, DAMP] * total[step] + ice[...]
        wide[step, b, pl.ds(BASE, columns)] = jnp.where(flags[...] == 0, 0.0, top / bottom)

    def rate(ref, start, length, lon, lat):
        centre = ref[pl.ds(start, length)]
        result = centre * (1.0 + lon[3] + lat[3])
        for j in (-3, -2, -1, 1, 2, 3):
            result += ref[pl.ds(start + j, length)] * lon[j + 3]
            result += pltpu.roll(centre, (-j) % rows, 1) * lat[j + 3]
        return result

    def advance(step, b, slot):
        lon = [(PLUS[j] * bins_ref[b, EAST] + MINUS[j] * bins_ref[b, WEST]) * rows_ref[0:1] for j in range(7)]
        lat = [(PLUS[j] * bins_ref[b, NORTH] + MINUS[j] * bins_ref[b, SOUTH]) * rows_ref[1 + j : 2 + j] for j in range(7)]
        ext, one_b, two_b = wide.at[step, b], one.at[slot], two.at[slot]
        around, wider = pl.ds(BASE - 8, columns + 16), columns + 16
        one_b[around] = rate(ext, BASE - 8, wider, lon, lat)
        two_b[around] = 0.75 * ext[around] + 0.25 * rate(one_b, BASE - 8, wider, lon, lat)
        moved = ext[pl.ds(BASE, columns)] / 3.0 + (2.0 / 3.0) * rate(two_b, BASE, columns, lon, lat)
        moved = jnp.where(flags[...] == 0, 0.0, moved)
        if step < STEPS - 1:
            later[b] = moved
            part[step + 1] += square(b, moved)
        else:
            last[b] = moved

    def result_copy(group):
        some = pl.ds(group * GROUP, GROUP)
        return pltpu.make_async_copy(last.at[some], out_ref.at[some], out_sem.at[group])

    def send_group(step, group):
        for k in range(GROUPS):
            @pl.when(group == k)
            def _(k=k):
                mine = range(k * GROUP, (k + 1) * GROUP)
                for piece, (_, b, *_) in enumerate(FAR):
                    if b in mine:
                        leg(step, piece).start()
                for piece, (_, b, *_) in enumerate(DIRECT):
                    if b in mine and piece not in KEPT_BACK:
                        direct(step, piece).start()

    inputs = [(field_hbm, first), (speed_hbm, speed), (heading_hbm, heading), (flags_hbm, flags)]
    inputs = [pltpu.make_async_copy(src, dst, in_sem.at[i]) for i, (src, dst) in enumerate(inputs)]
    for copy in inputs:
        copy.start()
    for step in range(1, STEPS):
        part[step] = jnp.zeros((columns, rows), jnp.float32)
    inputs[0].wait()
    part[0] = lax.fori_loop(0, here, lambda b, so_far: so_far + square(b, first[b]), jnp.zeros((columns, rows), jnp.float32))
    pl.semaphore_wait(barrier, len(partners))

    spread_a(0)
    for piece in range(len(FAR)):
        leg(0, piece).start()
    for piece in (3, 4, 5, 6, 0):
        direct(0, piece).start()
    for copy in inputs[1:]:
        copy.wait()
    gain = wind_gain * 0.1 * speed[...]
    gain_x[...] = gain * jnp.cos(heading[...])
    gain_y[...] = gain * jnp.sin(heading[...])
    open_sea[...] = jnp.where(flags[...] == 1, 1.0, 0.0)
    ice[...] = jnp.where(flags[...] == 2, ice_loss, 0.0)
    spread_b(0)
    direct(0, 1).start()
    pass_on_far(0, (0, 1, 2))
    spread_c(0)
    direct(0, 2).start()
    pass_on_far(0, (3, 4))
    pass_on_shared(0)
    spread_end(0)

    for step in range(STEPS):
        if step > 0:
            spread_a(step)
            direct(step, 1).start()
            pass_on_far(step, (1, 2))
            spread_b(step)
            direct(step, 2).start()
            pass_on_far(step, (3, 4))
            pass_on_shared(step)
            spread_c(step)
            pass_on_far(step, (0,))
            spread_end(step)

        @pl.loop(0, GROUPS + LAG)
        def _(g, step=step):
            @pl.when(g < GROUPS)
            def _():
                group = (g + FIRST_GROUP[step]) % GROUPS
                for k in range(GROUPS):
                    @pl.when(group == k)
                    def _(k=k):
                        for piece in NEEDS[step][k]:
                            arrival(step, piece).wait_recv()

                for j in range(GROUP):
                    source(step, group * GROUP + j)
                for side in range(2):
                    halo_copy(step, group, side).start()

            @pl.when(g >= LAG)
            def _():
                group = (g - LAG + FIRST_GROUP[step]) % GROUPS
                for side in range(2):
                    halo_copy(step, group, side).wait_recv()
                for j in range(GROUP):
                    advance(step, group * GROUP + j, j)
                if step < STEPS - 1:
                    send_group(step + 1, group)
                else:
                    result_copy(group).start()

    for step in range(STEPS):
        for turn in range(1, RING):
            a_copy(step, turn).wait_send()
            b_copy(step, turn).wait_send()
            c_copy(step, turn).wait_send()
        for piece in range(PIECES):
            arrival(step, piece).wait_send()
        for piece in range(len(FAR)):
            leg(step, piece).wait_send()

        @pl.loop(0, GROUPS)
        def _(group, step=step):
            for side in range(2):
                halo_copy(step, group, side).wait_send()

    @pl.loop(0, GROUPS)
    def _(group):
        result_copy(group).wait()


def shards(spectrum, wind_speed, wind_dir, flags):
    here, columns, rows = spectrum.shape
    index = lax.axis_index("bins") * here + jnp.arange(here, dtype=jnp.int32)
    whole = (columns, rows)
    chunk = columns // RING
    ext = columns + 2 * BASE
    hbm = pl.BlockSpec(memory_space=pl.ANY)
    dma = pltpu.SemaphoreType.DMA

    def buffer(*shape):
        return pltpu.VMEM(shape, jnp.float32)

    return pl.pallas_call(
        kernel,
        out_shape=jax.ShapeDtypeStruct(spectrum.shape, jnp.float32),
        in_specs=[hbm] * 4 + [pl.BlockSpec(memory_space=pltpu.SMEM), pl.BlockSpec(memory_space=pltpu.VMEM)],
        out_specs=hbm,
        scratch_shapes=[
            buffer(here, *whole),
            buffer(here, *whole),
            buffer(here, *whole),
            buffer(STEPS, 2, here, *whole),
            buffer(STEPS, here, *whole),
            buffer(STEPS, here, ext, rows),
            buffer(GROUP, ext, rows),
            buffer(GROUP, ext, rows),
            buffer(*whole),
            buffer(*whole),
            pltpu.VMEM(whole, jnp.int32),
            buffer(*whole),
            buffer(*whole),
            buffer(*whole),
            buffer(*whole),
            buffer(STEPS, *whole),
            buffer(STEPS, RING, chunk, rows),
            buffer(STEPS, chunk, rows),
            buffer(STEPS, RING, chunk, rows),
            buffer(STEPS, *whole),
        ]
        + [dma((STEPS, PIECES))] * 2
        + [dma((STEPS, len(FAR)))] * 2
        + [dma((STEPS, 2, GROUPS))] * 2
        + [dma((STEPS, RING))] * 6
        + [dma((4,)), dma((GROUPS,))],
        compiler_params=pltpu.CompilerParams(
            collective_id=0, has_side_effects=True, vmem_limit_bytes=24 * 1024 * 1024
        ),
    )(spectrum, wind_speed, wind_dir, flags, bin_table(index), row_table(rows))


def solution(mesh):
    return jax.shard_map(
        shards,
        mesh=mesh,
        in_specs=(P("bins", "lon", None), P("lon", None), P("lon", None), P("lon", None)),
        out_specs=P("bins", "lon", None),
        check_vma=False,
    )
```

```python
import functools
import math

import jax
import jax.numpy as jnp
from jax import lax
from jax.experimental import pallas as pl
from jax.experimental.pallas import tpu as pltpu
from jax.sharding import PartitionSpec as P

NF = 32
ND = 36
STEPS = 2

wind_gain = 0.5
quad_gain = 0.3
break_gain = 0.3
ice_loss = 1.0
courant = 0.6

RING = 8
HALO = 9
BASE = 16
GROUP = 3
GROUPS = 6
LAG = 2
LEG = 2
PLUS = (-2.0, 15.0, -60.0, 20.0, 30.0, -3.0, 0.0)
MINUS = (0.0, 3.0, -30.0, -20.0, 60.0, -15.0, 2.0)

DIRECT = (
    (0, 0, 3, 2, -2), (0, 3, 3, 5, -2), (0, 6, 3, 8, -2), (0, 9, 3, 11, -2), (0, 12, 3, 14, -2), (0, 15, 1, 17, -2),
    (1, 16, 2, 6, 6),
)
SHARED = ((3, 12, 2, 0), (4, 14, 3, 2), (5, 17, 1, 5))
FAR = ((0, 16, 2, 0, -1), (1, 0, 3, 8, 1), (1, 3, 3, 11, -1), (1, 6, 3, 14, 1), (1, 9, 1, 17, -1))
KEPT_BACK = (1, 2)
S0, F0 = len(DIRECT), len(DIRECT) + len(SHARED)
PIECES = F0 + len(FAR)
NEEDS = (
    ((F0, 0, S0, S0 + 1), (1, S0 + 2), (2, 6, F0 + 1), (F0 + 2,), (F0 + 3,), (F0 + 4,)),
    ((F0, S0), (0, 1, S0 + 1, S0 + 2), (2, 6, F0 + 1), (F0 + 2,), (F0 + 3,), (F0 + 4,)),
)
FIRST_GROUP = (0, 1)

RATIO, COS, SIN, DAMP, UPPER, LOWER, EAST, WEST, NORTH, SOUTH = range(10)


def bin_table(index):
    direction = (index // NF).astype(jnp.float32)
    level = (index % NF).astype(jnp.float32)
    theta = direction * (2.0 * math.pi / ND)
    ratio = jnp.power(1.05, level - NF // 2)
    group = jnp.power(1.1, -level)
    east = courant * group * jnp.cos(theta)
    north = courant * group * jnp.sin(theta)
    ratio, theta, east, north, level = (v[:, None] for v in (ratio, theta, east, north, level))
    return jnp.concatenate(
        [
            ratio,
            jnp.cos(theta),
            jnp.sin(theta),
            break_gain * ratio * ratio / (NF * ND),
            (level + 2 < NF).astype(jnp.float32),
            (level >= 2).astype(jnp.float32),
            jnp.where(east >= 0.0, east / -60.0, 0.0),
            jnp.where(east >= 0.0, 0.0, east / -60.0),
            jnp.where(north >= 0.0, north / -60.0, 0.0),
            jnp.where(north >= 0.0, 0.0, north / -60.0),
        ],
        axis=1,
    )


def row_table(rows):
    lines = jnp.arange(rows).astype(jnp.float32)
    coslat = jnp.cos((lines - rows / 2 + 0.5) * (0.25 * math.pi / 180.0))
    return (1.0 / coslat).reshape(1, rows)


def kernel(
    field_hbm, speed_hbm, heading_hbm, flags_hbm, bins_ref, rows_ref, out_ref,
    first, later, last, got, relay, wide, one, two, lon_taps, lat_taps, speed, heading, flags, gain_x, gain_y, open_sea, ice,
    part, part_in, mid, mid_in, total,
    send_sem, got_sem, leg_send, leg_recv, halo_send, halo_recv,
    a_send, a_recv, b_send, b_recv, c_send, c_recv, in_sem, out_sem,
):
    here, columns, rows = field_hbm.shape
    count, sectors = lax.axis_size("bins"), lax.axis_size("lon")
    place, sector = lax.axis_index("bins"), lax.axis_index("lon")
    ext = columns + 2 * BASE
    line, spot = place // RING, place % RING
    chunk = columns // RING
    def in_row(turn):
        return line * RING + (spot + turn) % RING

    def in_column(turn):
        return (line + turn) % RING * RING + spot

    def across(offset):
        return (place + offset + count) % count

    pair, far, core = place // 2, place % 2, sector % 2
    height = far * (sectors // 2) + sector // 2
    around_z = sectors

    def at(pair_offset, climb):
        new = (height + climb + around_z) % around_z
        new_pair = (pair + pair_offset + count // 2) % (count // 2)
        return {"bins": new_pair * 2 + new // (sectors // 2), "lon": new % (sectors // 2) * 2 + core}

    for step in range(STEPS):
        for rows_of in (pl.ds(0, BASE), pl.ds(BASE + columns, BASE)):
            wide[step, :, rows_of] = jnp.zeros((here, BASE, rows), jnp.float32)

    barrier = pltpu.get_barrier_semaphore()
    partners = [{"bins": across(s * o)} for o in (2, 6, 8) for s in (1, -1)]
    partners += [at(o, s * LEG) for o in (-3, -1, 0, 1, 3) for s in (1, -1)]
    partners += [{"bins": in_row(t)} for t in range(1, RING)]
    partners += [{"bins": in_column(t)} for t in range(1, RING)]
    partners += [{"lon": (sector + s + sectors) % sectors} for s in (1, -1)]
    for partner in partners:
        pl.semaphore_signal(barrier, inc=1, device_id=partner, device_id_type=pl.DeviceIdType.MESH)

    def send(src, dst, send_sem, recv_sem, device):
        return pltpu.make_async_remote_copy(
            src_ref=src, dst_ref=dst, send_sem=send_sem, recv_sem=recv_sem,
            device_id=device, device_id_type=pl.DeviceIdType.MESH,
        )

    def source_of(step):
        return field_hbm if step == 0 else later

    def field_of(step):
        return first if step == 0 else later

    def direct(step, piece):
        kind, b, bins, slot, places = DIRECT[piece]
        return send(
            source_of(step).at[pl.ds(b, bins)], got.at[step, kind, pl.ds(slot, bins)],
            send_sem.at[step, piece], got_sem.at[step, piece], {"bins": across(places)},
        )

    def shared(step, piece):
        _, slot, bins, new_slot = SHARED[piece]
        return send(
            got.at[step, 0, pl.ds(slot, bins)], got.at[step, 1, pl.ds(new_slot, bins)],
            send_sem.at[step, S0 + piece], got_sem.at[step, S0 + piece], {"bins": across(8)},
        )

    def leg(step, piece):
        kind, b, bins, _, way = FAR[piece]
        offset = 1 + 2 * far if kind else far - 1
        return send(
            source_of(step).at[pl.ds(b, bins)], relay.at[step, pl.ds(b, bins)],
            leg_send.at[step, piece], leg_recv.at[step, piece], at(offset, way * LEG),
        )

    def second_leg(step, piece):
        kind, b, bins, slot, way = FAR[piece]
        source_far = (height - way * LEG + around_z) % around_z // (sectors // 2)
        return send(
            relay.at[step, pl.ds(b, bins)], got.at[step, kind, pl.ds(slot, bins)],
            send_sem.at[step, F0 + piece], got_sem.at[step, F0 + piece], at(1 - source_far if kind else 0, way * LEG),
        )

    def arrival(step, piece):
        if piece < S0:
            return direct(step, piece)
        if piece < F0:
            return shared(step, piece - S0)
        return second_leg(step, piece - F0)

    def pass_on_far(step, pieces):
        for piece in pieces:
            leg(step, piece).wait_recv()
            second_leg(step, piece).start()

    def pass_on_shared(step):
        for piece, (before, *_) in enumerate(SHARED):
            direct(step, before).wait_recv()
            shared(step, piece).start()

    def halo_copy(step, group, side):
        if side == 0:
            src, dst, turn = BASE + columns - HALO, BASE - HALO, 1
        else:
            src, dst, turn = BASE, BASE + columns, -1
        ext = wide.at[step, pl.ds(group * GROUP, GROUP)]
        return send(
            ext.at[:, pl.ds(src, HALO)], ext.at[:, pl.ds(dst, HALO)],
            halo_send.at[step, side, group], halo_recv.at[step, side, group],
            {"lon": (sector + turn + sectors) % sectors},
        )

    def a_copy(step, turn):
        start = pl.multiple_of((spot + turn) % RING * chunk, chunk)
        return send(part.at[step, pl.ds(start, chunk)], part_in.at[step, turn], a_send.at[step, turn], a_recv.at[step, turn], {"bins": in_row(turn)})

    def b_copy(step, turn):
        return send(mid.at[step], mid_in.at[step, turn], b_send.at[step, turn], b_recv.at[step, turn], {"bins": in_column(turn)})

    def c_copy(step, turn):
        start = pl.multiple_of(spot * chunk, chunk)
        mine = total.at[step, pl.ds(start, chunk)]
        return send(mine, mine, c_send.at[step, turn], c_recv.at[step, turn], {"bins": in_row(turn)})

    def c_from(step, turn):
        start = pl.multiple_of((spot + RING - turn) % RING * chunk, chunk)
        theirs = total.at[step, pl.ds(start, chunk)]
        return send(theirs, theirs, c_send.at[step, turn], c_recv.at[step, turn], {"bins": in_row(turn)})

    def square(b, values):
        scaled = bins_ref[b, RATIO] * values
        return scaled * scaled

    def spread_a(step):
        for turn in range(1, RING):
            a_copy(step, turn).start()

    def spread_b(step):
        start = pl.multiple_of(spot * chunk, chunk)
        so_far = part[step, pl.ds(start, chunk)]
        for turn in range(1, RING):
            a_copy(step, turn).wait_recv()
            so_far += part_in[step, turn]
        mid[step] = so_far
        for turn in range(1, RING):
            b_copy(step, turn).start()

    def spread_c(step):
        start = pl.multiple_of(spot * chunk, chunk)
        so_far = mid[step]
        for turn in range(1, RING):
            b_copy(step, turn).wait_recv()
            so_far += mid_in[step, turn]
        total[step, pl.ds(start, chunk)] = so_far
        for turn in range(1, RING):
            c_copy(step, turn).start()

    def spread_end(step):
        for turn in range(1, RING):
            c_from(step, turn).wait_recv()

    def source(step, b):
        energy = field_of(step)[b]
        above = got[step, 0, b] * bins_ref[b, UPPER]
        below = got[step, 1, b] * bins_ref[b, LOWER]
        ratio = bins_ref[b, RATIO]
        wind = jnp.maximum(bins_ref[b, COS] * gain_x[...] + bins_ref[b, SIN] * gain_y[...], 0.0)
        quad = quad_gain * (energy * (above + below) - 2.0 * above * below)
        grown = energy + energy * (ratio * (wind + quad))
        top = jnp.where(open_sea[...] > 0.0, grown, energy)
        bottom = 1.0 + bins_ref[b, DAMP] * total[step] + ice[...]
        wide[step, b, pl.ds(BASE, columns)] = jnp.where(flags[...] == 0, 0.0, top / bottom)

    def halves(values):
        high = values.astype(jnp.bfloat16)
        return high, (values - high.astype(jnp.float32)).astype(jnp.bfloat16)

    def rates(fields, bins, signs, rows_out):
        parts = [halves(field) for field in fields]
        along_lat = jnp.dot(
            jnp.concatenate([jnp.concatenate(pair_of, axis=1) for pair_of in parts], axis=0),
            lat_taps[...], preferred_element_type=jnp.float32,
        )
        results = []
        for i, (field, pair_of, b) in enumerate(zip(fields, parts, bins)):
            along_lon = jnp.dot(
                lon_taps[signs[i], rows_out], jnp.concatenate(pair_of, axis=0), preferred_element_type=jnp.float32
            )
            start, end = i * ext + rows_out.start, i * ext + rows_out.start + rows_out.size
            east = (bins_ref[b, EAST] + bins_ref[b, WEST]) * rows_ref[...]
            results.append(
                field[rows_out.start : rows_out.start + rows_out.size]
                + along_lon * east
                + along_lat[start:end, :rows] * bins_ref[b, NORTH]
                + along_lat[start:end, rows:] * bins_ref[b, SOUTH]
            )
        return results

    def advance(step, group):
        bins = [group * GROUP + j for j in range(GROUP)]
        directions = [(place * here + b) // NF for b in bins]
        signs = [(d + ND // 4) // (ND // 2) % 2 for d in directions]
        every, inner = pl.ds(0, ext), pl.ds(BASE, columns)
        for j, values in enumerate(rates([wide[step, b] for b in bins], bins, signs, every)):
            one[j] = values
        for j, values in enumerate(rates([one[j] for j in range(GROUP)], bins, signs, every)):
            two[j] = 0.75 * wide[step, bins[j]] + 0.25 * values
        for j, values in enumerate(rates([two[j] for j in range(GROUP)], bins, signs, inner)):
            moved = wide[step, bins[j], inner] * (1.0 / 3.0) + (2.0 / 3.0) * values
            moved = jnp.where(flags[...] == 0, 0.0, moved)
            if step < STEPS - 1:
                later[bins[j]] = moved
                part[step + 1] += square(bins[j], moved)
            else:
                last[bins[j]] = moved

    def result_copy(group):
        some = pl.ds(group * GROUP, GROUP)
        return pltpu.make_async_copy(last.at[some], out_ref.at[some], out_sem.at[group])

    def send_group(step, group):
        for k in range(GROUPS):
            @pl.when(group == k)
            def _(k=k):
                mine = range(k * GROUP, (k + 1) * GROUP)
                for piece, (_, b, *_) in enumerate(FAR):
                    if b in mine:
                        leg(step, piece).start()
                for piece, (_, b, *_) in enumerate(DIRECT):
                    if b in mine and piece not in KEPT_BACK:
                        direct(step, piece).start()

    inputs = [(field_hbm, first), (speed_hbm, speed), (heading_hbm, heading), (flags_hbm, flags)]
    inputs = [pltpu.make_async_copy(src, dst, in_sem.at[i]) for i, (src, dst) in enumerate(inputs)]
    for copy in inputs:
        copy.start()

    def band(shape, along, across_it, taps):
        offset = lax.broadcasted_iota(jnp.int32, shape, along) - lax.broadcasted_iota(jnp.int32, shape, across_it)
        matrix = jnp.zeros(shape, jnp.float32)
        for j, tap in enumerate(taps):
            matrix = jnp.where(offset == j - 3, tap, matrix)
        return matrix.astype(jnp.bfloat16)

    for sign, taps in enumerate((PLUS, MINUS)):
        lon_band, lat_band = band((ext, ext), 1, 0, taps), band((rows, rows), 0, 1, taps)
        lon_taps[sign] = jnp.concatenate([lon_band, lon_band], axis=1)
        for half in range(2):
            lat_taps[pl.ds(half * rows, rows), pl.ds(sign * rows, rows)] = lat_band
    for step in range(1, STEPS):
        part[step] = jnp.zeros((columns, rows), jnp.float32)
    inputs[0].wait()
    part[0] = lax.fori_loop(0, here, lambda b, so_far: so_far + square(b, first[b]), jnp.zeros((columns, rows), jnp.float32))
    pl.semaphore_wait(barrier, len(partners))

    spread_a(0)
    for piece in range(len(FAR)):
        leg(0, piece).start()
    for piece in (3, 4, 5, 6, 0):
        direct(0, piece).start()
    for copy in inputs[1:]:
        copy.wait()
    gain = wind_gain * 0.1 * speed[...]
    gain_x[...] = gain * jnp.cos(heading[...])
    gain_y[...] = gain * jnp.sin(heading[...])
    open_sea[...] = jnp.where(flags[...] == 1, 1.0, 0.0)
    ice[...] = jnp.where(flags[...] == 2, ice_loss, 0.0)
    spread_b(0)
    direct(0, 1).start()
    pass_on_far(0, (0, 1, 2))
    spread_c(0)
    direct(0, 2).start()
    pass_on_far(0, (3, 4))
    pass_on_shared(0)
    spread_end(0)

    for step in range(STEPS):
        if step > 0:
            spread_a(step)
            direct(step, 1).start()
            pass_on_far(step, (1, 2))
            spread_b(step)
            direct(step, 2).start()
            pass_on_far(step, (3, 4))
            pass_on_shared(step)
            spread_c(step)
            pass_on_far(step, (0,))
            spread_end(step)

        @pl.loop(0, GROUPS + LAG)
        def _(g, step=step):
            @pl.when(g < GROUPS)
            def _():
                group = (g + FIRST_GROUP[step]) % GROUPS
                for k in range(GROUPS):
                    @pl.when(group == k)
                    def _(k=k):
                        for piece in NEEDS[step][k]:
                            arrival(step, piece).wait_recv()

                for j in range(GROUP):
                    source(step, group * GROUP + j)
                for side in range(2):
                    halo_copy(step, group, side).start()

            @pl.when(g >= LAG)
            def _():
                group = (g - LAG + FIRST_GROUP[step]) % GROUPS
                for side in range(2):
                    halo_copy(step, group, side).wait_recv()
                advance(step, group)
                if step < STEPS - 1:
                    send_group(step + 1, group)
                else:
                    result_copy(group).start()

    for step in range(STEPS):
        for turn in range(1, RING):
            a_copy(step, turn).wait_send()
            b_copy(step, turn).wait_send()
            c_copy(step, turn).wait_send()
        for piece in range(PIECES):
            arrival(step, piece).wait_send()
        for piece in range(len(FAR)):
            leg(step, piece).wait_send()

        @pl.loop(0, GROUPS)
        def _(group, step=step):
            for side in range(2):
                halo_copy(step, group, side).wait_send()

    @pl.loop(0, GROUPS)
    def _(group):
        result_copy(group).wait()


def shards(spectrum, wind_speed, wind_dir, flags):
    here, columns, rows = spectrum.shape
    index = lax.axis_index("bins") * here + jnp.arange(here, dtype=jnp.int32)
    whole = (columns, rows)
    chunk = columns // RING
    ext = columns + 2 * BASE
    hbm = pl.BlockSpec(memory_space=pl.ANY)
    dma = pltpu.SemaphoreType.DMA

    def buffer(*shape):
        return pltpu.VMEM(shape, jnp.float32)

    return pl.pallas_call(
        kernel,
        out_shape=jax.ShapeDtypeStruct(spectrum.shape, jnp.float32),
        in_specs=[hbm] * 4 + [pl.BlockSpec(memory_space=pltpu.SMEM), pl.BlockSpec(memory_space=pltpu.VMEM)],
        out_specs=hbm,
        scratch_shapes=[
            buffer(here, *whole),
            buffer(here, *whole),
            buffer(here, *whole),
            buffer(STEPS, 2, here, *whole),
            buffer(STEPS, here, *whole),
            buffer(STEPS, here, ext, rows),
            buffer(GROUP, ext, rows),
            buffer(GROUP, ext, rows),
            pltpu.VMEM((2, ext, 2 * ext), jnp.bfloat16),
            pltpu.VMEM((2 * rows, 2 * rows), jnp.bfloat16),
            buffer(*whole),
            buffer(*whole),
            pltpu.VMEM(whole, jnp.int32),
            buffer(*whole),
            buffer(*whole),
            buffer(*whole),
            buffer(*whole),
            buffer(STEPS, *whole),
            buffer(STEPS, RING, chunk, rows),
            buffer(STEPS, chunk, rows),
            buffer(STEPS, RING, chunk, rows),
            buffer(STEPS, *whole),
        ]
        + [dma((STEPS, PIECES))] * 2
        + [dma((STEPS, len(FAR)))] * 2
        + [dma((STEPS, 2, GROUPS))] * 2
        + [dma((STEPS, RING))] * 6
        + [dma((4,)), dma((GROUPS,))],
        compiler_params=pltpu.CompilerParams(
            collective_id=0, has_side_effects=True, vmem_limit_bytes=56 * 1024 * 1024
        ),
    )(spectrum, wind_speed, wind_dir, flags, bin_table(index), row_table(rows))


def solution(mesh):
    return jax.shard_map(
        shards,
        mesh=mesh,
        in_specs=(P("bins", "lon", None), P("lon", None), P("lon", None), P("lon", None)),
        out_specs=P("bins", "lon", None),
        check_vma=False,
    )
```

```python
import functools
import math

import jax
import jax.numpy as jnp
from jax import lax
from jax.experimental import pallas as pl
from jax.experimental.pallas import tpu as pltpu
from jax.sharding import PartitionSpec as P

NF = 32
ND = 36
STEPS = 2

wind_gain = 0.5
quad_gain = 0.3
break_gain = 0.3
ice_loss = 1.0
courant = 0.6

RING = 8
HALO = 9
BASE = 16
GROUP = 3
GROUPS = 6
LAG = 2
LEG = 2
PLUS = (-2.0, 15.0, -60.0, 20.0, 30.0, -3.0, 0.0)
MINUS = (0.0, 3.0, -30.0, -20.0, 60.0, -15.0, 2.0)

DIRECT = (
    (0, 0, 3, 2, -2), (0, 3, 3, 5, -2), (0, 6, 3, 8, -2), (0, 9, 3, 11, -2), (0, 12, 3, 14, -2), (0, 15, 1, 17, -2),
    (1, 16, 2, 6, 6),
)
SHARED = ((3, 12, 2, 0), (4, 14, 3, 2), (5, 17, 1, 5))
FAR = ((0, 16, 2, 0, -1), (1, 0, 3, 8, 1), (1, 3, 3, 11, -1), (1, 6, 3, 14, 1), (1, 9, 1, 17, -1))
KEPT_BACK = (1, 2)
S0, F0 = len(DIRECT), len(DIRECT) + len(SHARED)
PIECES = F0 + len(FAR)
NEEDS = (
    ((F0, 0, S0, S0 + 1), (1, S0 + 2), (2, 6, F0 + 1), (F0 + 2,), (F0 + 3,), (F0 + 4,)),
    ((F0, S0), (0, 1, S0 + 1, S0 + 2), (2, 6, F0 + 1), (F0 + 2,), (F0 + 3,), (F0 + 4,)),
)
FIRST_GROUP = (0, 1)

RATIO, COS, SIN, DAMP, UPPER, LOWER, EAST, WEST, NORTH, SOUTH = range(10)


def bin_table(index):
    direction = (index // NF).astype(jnp.float32)
    level = (index % NF).astype(jnp.float32)
    theta = direction * (2.0 * math.pi / ND)
    ratio = jnp.power(1.05, level - NF // 2)
    group = jnp.power(1.1, -level)
    east = courant * group * jnp.cos(theta)
    north = courant * group * jnp.sin(theta)
    ratio, theta, east, north, level = (v[:, None] for v in (ratio, theta, east, north, level))
    return jnp.concatenate(
        [
            ratio,
            jnp.cos(theta),
            jnp.sin(theta),
            break_gain * ratio * ratio / (NF * ND),
            (level + 2 < NF).astype(jnp.float32),
            (level >= 2).astype(jnp.float32),
            jnp.where(east >= 0.0, east / -60.0, 0.0),
            jnp.where(east >= 0.0, 0.0, east / -60.0),
            jnp.where(north >= 0.0, north / -60.0, 0.0),
            jnp.where(north >= 0.0, 0.0, north / -60.0),
        ],
        axis=1,
    )


def row_table(rows):
    lines = jnp.arange(rows).astype(jnp.float32)
    coslat = jnp.cos((lines - rows / 2 + 0.5) * (0.25 * math.pi / 180.0))
    return (1.0 / coslat).reshape(1, rows)


def halves(values):
    high = values.astype(jnp.bfloat16)
    return high, (values - high.astype(jnp.float32)).astype(jnp.bfloat16)

def rates(fields, bins, signs, rows_out, lon_taps, lat_taps, bins_ref, rows_ref):
    ext, rows = fields[0].shape
    parts = [halves(field) for field in fields]
    along_lat = jnp.dot(
        jnp.concatenate([jnp.concatenate(pair_of, axis=1) for pair_of in parts], axis=0),
        lat_taps[...], preferred_element_type=jnp.float32,
    )
    results = []
    for i, (field, pair_of, b) in enumerate(zip(fields, parts, bins)):
        along_lon = jnp.dot(
            lon_taps[signs[i], rows_out], jnp.concatenate(pair_of, axis=0), preferred_element_type=jnp.float32
        )
        start, end = i * ext + rows_out.start, i * ext + rows_out.start + rows_out.size
        east = (bins_ref[b, EAST] + bins_ref[b, WEST]) * rows_ref[...]
        results.append(
            field[rows_out.start : rows_out.start + rows_out.size]
            + along_lon * east
            + along_lat[start:end, :rows] * bins_ref[b, NORTH]
            + along_lat[start:end, rows:] * bins_ref[b, SOUTH]
        )
    return results


def sections(place, here, start, bins, lon_taps, lat_taps, bins_ref, rows_ref, one, two):
    ext, rows = one.shape[1:]
    count = len(bins)
    directions = [(place * here + b) // NF for b in bins]
    signs = [(d + ND // 4) // (ND // 2) % 2 for d in directions]
    every, inner = pl.ds(0, ext), pl.ds(BASE, ext - 2 * BASE)
    tables = lon_taps, lat_taps, bins_ref, rows_ref
    for j, values in enumerate(rates([start(j) for j in range(count)], bins, signs, every, *tables)):
        one[j] = values
    for j, values in enumerate(rates([one[j] for j in range(count)], bins, signs, every, *tables)):
        two[j] = 0.75 * start(j) + 0.25 * values
    results = rates([two[j] for j in range(count)], bins, signs, inner, *tables)
    return [
        start(j)[BASE : ext - BASE] * (1.0 / 3.0) + (2.0 / 3.0) * values for j, values in enumerate(results)
    ]


def fill_taps(lon_taps, lat_taps):
    ext, rows = lon_taps.shape[1], lat_taps.shape[0] // 2

    def band(shape, along, across_it, taps):
        offset = lax.broadcasted_iota(jnp.int32, shape, along) - lax.broadcasted_iota(jnp.int32, shape, across_it)
        matrix = jnp.zeros(shape, jnp.float32)
        for j, tap in enumerate(taps):
            matrix = jnp.where(offset == j - 3, tap, matrix)
        return matrix.astype(jnp.bfloat16)

    for sign, taps in enumerate((PLUS, MINUS)):
        lon_band, lat_band = band((ext, ext), 1, 0, taps), band((rows, rows), 0, 1, taps)
        lon_taps[sign] = jnp.concatenate([lon_band, lon_band], axis=1)
        for half in range(2):
            lat_taps[pl.ds(half * rows, rows), pl.ds(sign * rows, rows)] = lat_band


def last_kernel(wide, flags, bins_ref, rows_ref, out_ref, one, two, lon_taps, lat_taps):
    step = pl.program_id(0)
    place = lax.axis_index("bins")

    @pl.when(step == 0)
    def _():
        fill_taps(lon_taps, lat_taps)

    bins = [step * GROUP + j for j in range(GROUP)]
    results = sections(
        place, GROUP * GROUPS, lambda j: wide[j], bins, lon_taps, lat_taps, bins_ref, rows_ref, one, two
    )
    for j, moved in enumerate(results):
        out_ref[j] = jnp.where(flags[...] == 0, 0.0, moved)


def kernel(
    field_hbm, speed_hbm, heading_hbm, flags_hbm, bins_ref, rows_ref, out_ref,
    first, later, got, relay, wide, one, two, lon_taps, lat_taps, speed, heading, flags, gain_x, gain_y, open_sea, ice,
    part, part_in, mid, mid_in, total,
    send_sem, got_sem, leg_send, leg_recv, halo_send, halo_recv,
    a_send, a_recv, b_send, b_recv, c_send, c_recv, in_sem, out_sem,
):
    here, columns, rows = field_hbm.shape
    count, sectors = lax.axis_size("bins"), lax.axis_size("lon")
    place, sector = lax.axis_index("bins"), lax.axis_index("lon")
    ext = columns + 2 * BASE
    line, spot = place // RING, place % RING
    chunk = columns // RING
    def in_row(turn):
        return line * RING + (spot + turn) % RING

    def in_column(turn):
        return (line + turn) % RING * RING + spot

    def across(offset):
        return (place + offset + count) % count

    pair, far, core = place // 2, place % 2, sector % 2
    height = far * (sectors // 2) + sector // 2
    around_z = sectors

    def at(pair_offset, climb):
        new = (height + climb + around_z) % around_z
        new_pair = (pair + pair_offset + count // 2) % (count // 2)
        return {"bins": new_pair * 2 + new // (sectors // 2), "lon": new % (sectors // 2) * 2 + core}

    for step in range(STEPS):
        for rows_of in (pl.ds(0, BASE), pl.ds(BASE + columns, BASE)):
            wide[step, :, rows_of] = jnp.zeros((here, BASE, rows), jnp.float32)

    barrier = pltpu.get_barrier_semaphore()
    partners = [{"bins": across(s * o)} for o in (2, 6, 8) for s in (1, -1)]
    partners += [at(o, s * LEG) for o in (-3, -1, 0, 1, 3) for s in (1, -1)]
    partners += [{"bins": in_row(t)} for t in range(1, RING)]
    partners += [{"bins": in_column(t)} for t in range(1, RING)]
    partners += [{"lon": (sector + s + sectors) % sectors} for s in (1, -1)]
    for partner in partners:
        pl.semaphore_signal(barrier, inc=1, device_id=partner, device_id_type=pl.DeviceIdType.MESH)

    def send(src, dst, send_sem, recv_sem, device):
        return pltpu.make_async_remote_copy(
            src_ref=src, dst_ref=dst, send_sem=send_sem, recv_sem=recv_sem,
            device_id=device, device_id_type=pl.DeviceIdType.MESH,
        )

    def source_of(step):
        return field_hbm if step == 0 else later

    def field_of(step):
        return first if step == 0 else later

    def direct(step, piece):
        kind, b, bins, slot, places = DIRECT[piece]
        return send(
            source_of(step).at[pl.ds(b, bins)], got.at[step, kind, pl.ds(slot, bins)],
            send_sem.at[step, piece], got_sem.at[step, piece], {"bins": across(places)},
        )

    def shared(step, piece):
        _, slot, bins, new_slot = SHARED[piece]
        return send(
            got.at[step, 0, pl.ds(slot, bins)], got.at[step, 1, pl.ds(new_slot, bins)],
            send_sem.at[step, S0 + piece], got_sem.at[step, S0 + piece], {"bins": across(8)},
        )

    def leg(step, piece):
        kind, b, bins, _, way = FAR[piece]
        offset = 1 + 2 * far if kind else far - 1
        return send(
            source_of(step).at[pl.ds(b, bins)], relay.at[step, pl.ds(b, bins)],
            leg_send.at[step, piece], leg_recv.at[step, piece], at(offset, way * LEG),
        )

    def second_leg(step, piece):
        kind, b, bins, slot, way = FAR[piece]
        source_far = (height - way * LEG + around_z) % around_z // (sectors // 2)
        return send(
            relay.at[step, pl.ds(b, bins)], got.at[step, kind, pl.ds(slot, bins)],
            send_sem.at[step, F0 + piece], got_sem.at[step, F0 + piece], at(1 - source_far if kind else 0, way * LEG),
        )

    def arrival(step, piece):
        if piece < S0:
            return direct(step, piece)
        if piece < F0:
            return shared(step, piece - S0)
        return second_leg(step, piece - F0)

    def pass_on_far(step, pieces):
        for piece in pieces:
            leg(step, piece).wait_recv()
            second_leg(step, piece).start()

    def pass_on_shared(step):
        for piece, (before, *_) in enumerate(SHARED):
            direct(step, before).wait_recv()
            shared(step, piece).start()

    def halo_copy(step, group, side):
        if side == 0:
            src, dst, turn = BASE + columns - HALO, BASE - HALO, 1
        else:
            src, dst, turn = BASE, BASE + columns, -1
        ext = wide.at[step, pl.ds(group * GROUP, GROUP)]
        return send(
            ext.at[:, pl.ds(src, HALO)], ext.at[:, pl.ds(dst, HALO)],
            halo_send.at[step, side, group], halo_recv.at[step, side, group],
            {"lon": (sector + turn + sectors) % sectors},
        )

    def a_copy(step, turn):
        start = pl.multiple_of((spot + turn) % RING * chunk, chunk)
        return send(part.at[step, pl.ds(start, chunk)], part_in.at[step, turn], a_send.at[step, turn], a_recv.at[step, turn], {"bins": in_row(turn)})

    def b_copy(step, turn):
        return send(mid.at[step], mid_in.at[step, turn], b_send.at[step, turn], b_recv.at[step, turn], {"bins": in_column(turn)})

    def c_copy(step, turn):
        start = pl.multiple_of(spot * chunk, chunk)
        mine = total.at[step, pl.ds(start, chunk)]
        return send(mine, mine, c_send.at[step, turn], c_recv.at[step, turn], {"bins": in_row(turn)})

    def c_from(step, turn):
        start = pl.multiple_of((spot + RING - turn) % RING * chunk, chunk)
        theirs = total.at[step, pl.ds(start, chunk)]
        return send(theirs, theirs, c_send.at[step, turn], c_recv.at[step, turn], {"bins": in_row(turn)})

    def square(b, values):
        scaled = bins_ref[b, RATIO] * values
        return scaled * scaled

    def spread_a(step):
        for turn in range(1, RING):
            a_copy(step, turn).start()

    def spread_b(step):
        start = pl.multiple_of(spot * chunk, chunk)
        so_far = part[step, pl.ds(start, chunk)]
        for turn in range(1, RING):
            a_copy(step, turn).wait_recv()
            so_far += part_in[step, turn]
        mid[step] = so_far
        for turn in range(1, RING):
            b_copy(step, turn).start()

    def spread_c(step):
        start = pl.multiple_of(spot * chunk, chunk)
        so_far = mid[step]
        for turn in range(1, RING):
            b_copy(step, turn).wait_recv()
            so_far += mid_in[step, turn]
        total[step, pl.ds(start, chunk)] = so_far
        for turn in range(1, RING):
            c_copy(step, turn).start()

    def spread_end(step):
        for turn in range(1, RING):
            c_from(step, turn).wait_recv()

    def source(step, b):
        energy = field_of(step)[b]
        above = got[step, 0, b] * bins_ref[b, UPPER]
        below = got[step, 1, b] * bins_ref[b, LOWER]
        ratio = bins_ref[b, RATIO]
        wind = jnp.maximum(bins_ref[b, COS] * gain_x[...] + bins_ref[b, SIN] * gain_y[...], 0.0)
        quad = quad_gain * (energy * (above + below) - 2.0 * above * below)
        grown = energy + energy * (ratio * (wind + quad))
        top = jnp.where(open_sea[...] > 0.0, grown, energy)
        bottom = 1.0 + bins_ref[b, DAMP] * total[step] + ice[...]
        wide[step, b, pl.ds(BASE, columns)] = jnp.where(flags[...] == 0, 0.0, top / bottom)

    def advance(step, group):
        bins = [group * GROUP + j for j in range(GROUP)]
        results = sections(
            place, here, lambda j: wide[step, bins[j]], bins, lon_taps, lat_taps, bins_ref, rows_ref, one, two
        )
        for j, moved in enumerate(results):
            moved = jnp.where(flags[...] == 0, 0.0, moved)
            later[bins[j]] = moved
            part[step + 1] += square(bins[j], moved)

    def result_copy(group):
        some = pl.ds(group * GROUP, GROUP)
        return pltpu.make_async_copy(wide.at[STEPS - 1, some], out_ref.at[some], out_sem.at[group])

    def send_group(step, group):
        for k in range(GROUPS):
            @pl.when(group == k)
            def _(k=k):
                mine = range(k * GROUP, (k + 1) * GROUP)
                for piece, (_, b, *_) in enumerate(FAR):
                    if b in mine:
                        leg(step, piece).start()
                for piece, (_, b, *_) in enumerate(DIRECT):
                    if b in mine and piece not in KEPT_BACK:
                        direct(step, piece).start()

    inputs = [(field_hbm, first), (speed_hbm, speed), (heading_hbm, heading), (flags_hbm, flags)]
    inputs = [pltpu.make_async_copy(src, dst, in_sem.at[i]) for i, (src, dst) in enumerate(inputs)]
    for copy in inputs:
        copy.start()

    fill_taps(lon_taps, lat_taps)
    for step in range(1, STEPS):
        part[step] = jnp.zeros((columns, rows), jnp.float32)
    inputs[0].wait()
    part[0] = lax.fori_loop(0, here, lambda b, so_far: so_far + square(b, first[b]), jnp.zeros((columns, rows), jnp.float32))
    pl.semaphore_wait(barrier, len(partners))

    spread_a(0)
    for piece in range(len(FAR)):
        leg(0, piece).start()
    for piece in (3, 4, 5, 6, 0):
        direct(0, piece).start()
    for copy in inputs[1:]:
        copy.wait()
    gain = wind_gain * 0.1 * speed[...]
    gain_x[...] = gain * jnp.cos(heading[...])
    gain_y[...] = gain * jnp.sin(heading[...])
    open_sea[...] = jnp.where(flags[...] == 1, 1.0, 0.0)
    ice[...] = jnp.where(flags[...] == 2, ice_loss, 0.0)
    spread_b(0)
    direct(0, 1).start()
    pass_on_far(0, (0, 1, 2))
    spread_c(0)
    direct(0, 2).start()
    pass_on_far(0, (3, 4))
    pass_on_shared(0)
    spread_end(0)

    for step in range(STEPS):
        if step > 0:
            spread_a(step)
            direct(step, 1).start()
            pass_on_far(step, (1, 2))
            spread_b(step)
            direct(step, 2).start()
            pass_on_far(step, (3, 4))
            pass_on_shared(step)
            spread_c(step)
            pass_on_far(step, (0,))
            spread_end(step)

        @pl.loop(0, GROUPS + LAG)
        def _(g, step=step):
            @pl.when(g < GROUPS)
            def _():
                group = (g + FIRST_GROUP[step]) % GROUPS
                for k in range(GROUPS):
                    @pl.when(group == k)
                    def _(k=k):
                        for piece in NEEDS[step][k]:
                            arrival(step, piece).wait_recv()

                for j in range(GROUP):
                    source(step, group * GROUP + j)
                for side in range(2):
                    halo_copy(step, group, side).start()

            @pl.when(g >= LAG)
            def _():
                group = (g - LAG + FIRST_GROUP[step]) % GROUPS
                for side in range(2):
                    halo_copy(step, group, side).wait_recv()
                if step < STEPS - 1:
                    advance(step, group)
                    send_group(step + 1, group)
                else:
                    result_copy(group).start()

    for step in range(STEPS):
        for turn in range(1, RING):
            a_copy(step, turn).wait_send()
            b_copy(step, turn).wait_send()
            c_copy(step, turn).wait_send()
        for piece in range(PIECES):
            arrival(step, piece).wait_send()
        for piece in range(len(FAR)):
            leg(step, piece).wait_send()

        @pl.loop(0, GROUPS)
        def _(group, step=step):
            for side in range(2):
                halo_copy(step, group, side).wait_send()

    @pl.loop(0, GROUPS)
    def _(group):
        result_copy(group).wait()


def shards(spectrum, wind_speed, wind_dir, flags):
    here, columns, rows = spectrum.shape
    index = lax.axis_index("bins") * here + jnp.arange(here, dtype=jnp.int32)
    whole = (columns, rows)
    chunk = columns // RING
    ext = columns + 2 * BASE
    hbm = pl.BlockSpec(memory_space=pl.ANY)
    dma = pltpu.SemaphoreType.DMA

    def buffer(*shape):
        return pltpu.VMEM(shape, jnp.float32)

    bins_of, rows_of = bin_table(index), row_table(rows)
    sourced = pl.pallas_call(
        kernel,
        out_shape=jax.ShapeDtypeStruct((here, ext, rows), jnp.float32),
        in_specs=[hbm] * 4 + [pl.BlockSpec(memory_space=pltpu.SMEM), pl.BlockSpec(memory_space=pltpu.VMEM)],
        out_specs=hbm,
        scratch_shapes=[
            buffer(here, *whole),
            buffer(here, *whole),
            buffer(STEPS, 2, here, *whole),
            buffer(STEPS, here, *whole),
            buffer(STEPS, here, ext, rows),
            buffer(GROUP, ext, rows),
            buffer(GROUP, ext, rows),
            pltpu.VMEM((2, ext, 2 * ext), jnp.bfloat16),
            pltpu.VMEM((2 * rows, 2 * rows), jnp.bfloat16),
            buffer(*whole),
            buffer(*whole),
            pltpu.VMEM(whole, jnp.int32),
            buffer(*whole),
            buffer(*whole),
            buffer(*whole),
            buffer(*whole),
            buffer(STEPS, *whole),
            buffer(STEPS, RING, chunk, rows),
            buffer(STEPS, chunk, rows),
            buffer(STEPS, RING, chunk, rows),
            buffer(STEPS, *whole),
        ]
        + [dma((STEPS, PIECES))] * 2
        + [dma((STEPS, len(FAR)))] * 2
        + [dma((STEPS, 2, GROUPS))] * 2
        + [dma((STEPS, RING))] * 6
        + [dma((4,)), dma((GROUPS,))],
        compiler_params=pltpu.CompilerParams(
            collective_id=0, has_side_effects=True, vmem_limit_bytes=56 * 1024 * 1024
        ),
    )(spectrum, wind_speed, wind_dir, flags, bins_of, rows_of)
    return pl.pallas_call(
        last_kernel,
        grid=(GROUPS,),
        out_shape=jax.ShapeDtypeStruct(spectrum.shape, jnp.float32),
        in_specs=[
            pl.BlockSpec((GROUP, ext, rows), lambda i: (i, 0, 0)),
            pl.BlockSpec(whole, lambda i: (0, 0)),
            pl.BlockSpec(memory_space=pltpu.SMEM),
            pl.BlockSpec((1, rows), lambda i: (0, 0)),
        ],
        out_specs=pl.BlockSpec((GROUP, *whole), lambda i: (i, 0, 0)),
        scratch_shapes=[
            buffer(GROUP, ext, rows),
            buffer(GROUP, ext, rows),
            pltpu.VMEM((2, ext, 2 * ext), jnp.bfloat16),
            pltpu.VMEM((2 * rows, 2 * rows), jnp.bfloat16),
        ],
        compiler_params=pltpu.CompilerParams(vmem_limit_bytes=56 * 1024 * 1024),
    )(sourced, flags, bins_of, rows_of)


def solution(mesh):
    return jax.shard_map(
        shards,
        mesh=mesh,
        in_specs=(P("bins", "lon", None), P("lon", None), P("lon", None), P("lon", None)),
        out_specs=P("bins", "lon", None),
        check_vma=False,
    )
```

```python
import functools
import math

import jax
import jax.numpy as jnp
from jax import lax
from jax.experimental import pallas as pl
from jax.experimental.pallas import tpu as pltpu
from jax.sharding import PartitionSpec as P

NF = 32
ND = 36
STEPS = 2

wind_gain = 0.5
quad_gain = 0.3
break_gain = 0.3
ice_loss = 1.0
courant = 0.6

RING = 8
HALO = 9
BASE = 16
GROUP = 3
GROUPS = 6
LAG = 2
LEG = 2
PLUS = (-2.0, 15.0, -60.0, 20.0, 30.0, -3.0, 0.0)
MINUS = (0.0, 3.0, -30.0, -20.0, 60.0, -15.0, 2.0)

DIRECT = (
    (0, 0, 3, 2, -2), (0, 3, 3, 5, -2), (0, 6, 3, 8, -2), (0, 9, 3, 11, -2), (0, 12, 3, 14, -2), (0, 15, 1, 17, -2),
    (1, 16, 2, 6, 6),
)
SHARED = ((3, 12, 2, 0), (4, 14, 3, 2), (5, 17, 1, 5))
FAR = ((0, 16, 2, 0, -1), (1, 0, 3, 8, 1), (1, 3, 3, 11, -1), (1, 6, 3, 14, 1), (1, 9, 1, 17, -1))
S0, F0 = len(DIRECT), len(DIRECT) + len(SHARED)
PIECES = F0 + len(FAR)
NEEDS = (
    ((F0, 0, S0, S0 + 1), (1, S0 + 2), (2, 6, F0 + 1), (F0 + 2,), (F0 + 3,), (F0 + 4,)),
    ((F0, S0), (0, 1, S0 + 1, S0 + 2), (2, 6, F0 + 1), (F0 + 2,), (F0 + 3,), (F0 + 4,)),
)
FIRST_GROUP = (0, 1)

RATIO, COS, SIN, DAMP, UPPER, LOWER, EAST, WEST, NORTH, SOUTH = range(10)


def bin_table(index):
    direction = (index // NF).astype(jnp.float32)
    level = (index % NF).astype(jnp.float32)
    theta = direction * (2.0 * math.pi / ND)
    ratio = jnp.power(1.05, level - NF // 2)
    group = jnp.power(1.1, -level)
    east = courant * group * jnp.cos(theta)
    north = courant * group * jnp.sin(theta)
    ratio, theta, east, north, level = (v[:, None] for v in (ratio, theta, east, north, level))
    return jnp.concatenate(
        [
            ratio,
            jnp.cos(theta),
            jnp.sin(theta),
            break_gain * ratio * ratio / (NF * ND),
            (level + 2 < NF).astype(jnp.float32),
            (level >= 2).astype(jnp.float32),
            jnp.where(east >= 0.0, east / -60.0, 0.0),
            jnp.where(east >= 0.0, 0.0, east / -60.0),
            jnp.where(north >= 0.0, north / -60.0, 0.0),
            jnp.where(north >= 0.0, 0.0, north / -60.0),
        ],
        axis=1,
    )


def row_table(rows):
    lines = jnp.arange(rows).astype(jnp.float32)
    coslat = jnp.cos((lines - rows / 2 + 0.5) * (0.25 * math.pi / 180.0))
    return (1.0 / coslat).reshape(1, rows)


def kernel(
    field_hbm, speed_hbm, heading_hbm, flags_hbm, bins_ref, rows_ref, out_ref,
    first, later, last, got, relay, wide, one, two, lon_taps, lat_taps, speed, heading, flags, gain_x, gain_y, open_sea, ice,
    part, part_in, mid, mid_in, total,
    send_sem, got_sem, leg_send, leg_recv, halo_send, halo_recv,
    a_send, a_recv, b_send, b_recv, c_send, c_recv, in_sem, out_sem,
):
    here, columns, rows = field_hbm.shape
    count, sectors = lax.axis_size("bins"), lax.axis_size("lon")
    place, sector = lax.axis_index("bins"), lax.axis_index("lon")
    ext = columns + 2 * BASE
    line, spot = place // RING, place % RING
    chunk = columns // RING
    def in_row(turn):
        return line * RING + (spot + turn) % RING

    def in_column(turn):
        return (line + turn) % RING * RING + spot

    def across(offset):
        return (place + offset + count) % count

    pair, far, core = place // 2, place % 2, sector % 2
    height = far * (sectors // 2) + sector // 2
    around_z = sectors

    def at(pair_offset, climb):
        new = (height + climb + around_z) % around_z
        new_pair = (pair + pair_offset + count // 2) % (count // 2)
        return {"bins": new_pair * 2 + new // (sectors // 2), "lon": new % (sectors // 2) * 2 + core}

    for step in range(STEPS):
        for rows_of in (pl.ds(0, BASE), pl.ds(BASE + columns, BASE)):
            wide[step, :, rows_of] = jnp.zeros((here, BASE, rows), jnp.float32)

    barrier = pltpu.get_barrier_semaphore()
    partners = [{"bins": across(s * o)} for o in (2, 6, 8) for s in (1, -1)]
    partners += [at(o, s * LEG) for o in (-3, -1, 0, 1, 3) for s in (1, -1)]
    partners += [{"bins": in_row(t)} for t in range(1, RING)]
    partners += [{"bins": in_column(t)} for t in range(1, RING)]
    partners += [{"lon": (sector + s + sectors) % sectors} for s in (1, -1)]
    for partner in partners:
        pl.semaphore_signal(barrier, inc=1, device_id=partner, device_id_type=pl.DeviceIdType.MESH)

    def send(src, dst, send_sem, recv_sem, device):
        return pltpu.make_async_remote_copy(
            src_ref=src, dst_ref=dst, send_sem=send_sem, recv_sem=recv_sem,
            device_id=device, device_id_type=pl.DeviceIdType.MESH,
        )

    def source_of(step):
        return field_hbm if step == 0 else later

    def field_of(step):
        return first if step == 0 else later

    def direct(step, piece):
        kind, b, bins, slot, places = DIRECT[piece]
        return send(
            source_of(step).at[pl.ds(b, bins)], got.at[step, kind, pl.ds(slot, bins)],
            send_sem.at[step, piece], got_sem.at[step, piece], {"bins": across(places)},
        )

    def shared(step, piece):
        _, slot, bins, new_slot = SHARED[piece]
        return send(
            got.at[step, 0, pl.ds(slot, bins)], got.at[step, 1, pl.ds(new_slot, bins)],
            send_sem.at[step, S0 + piece], got_sem.at[step, S0 + piece], {"bins": across(8)},
        )

    def leg(step, piece):
        kind, b, bins, _, way = FAR[piece]
        offset = 1 + 2 * far if kind else far - 1
        return send(
            source_of(step).at[pl.ds(b, bins)], relay.at[step, pl.ds(b, bins)],
            leg_send.at[step, piece], leg_recv.at[step, piece], at(offset, way * LEG),
        )

    def second_leg(step, piece):
        kind, b, bins, slot, way = FAR[piece]
        source_far = (height - way * LEG + around_z) % around_z // (sectors // 2)
        return send(
            relay.at[step, pl.ds(b, bins)], got.at[step, kind, pl.ds(slot, bins)],
            send_sem.at[step, F0 + piece], got_sem.at[step, F0 + piece], at(1 - source_far if kind else 0, way * LEG),
        )

    def arrival(step, piece):
        if piece < S0:
            return direct(step, piece)
        if piece < F0:
            return shared(step, piece - S0)
        return second_leg(step, piece - F0)

    def pass_on_far(step, pieces):
        for piece in pieces:
            leg(step, piece).wait_recv()
            second_leg(step, piece).start()

    def pass_on_shared(step, pieces):
        for piece in pieces:
            direct(step, SHARED[piece][0]).wait_recv()
            shared(step, piece).start()

    def halo_copy(step, group, side):
        if side == 0:
            src, dst, turn = BASE + columns - HALO, BASE - HALO, 1
        else:
            src, dst, turn = BASE, BASE + columns, -1
        ext = wide.at[step, pl.ds(group * GROUP, GROUP)]
        return send(
            ext.at[:, pl.ds(src, HALO)], ext.at[:, pl.ds(dst, HALO)],
            halo_send.at[step, side, group], halo_recv.at[step, side, group],
            {"lon": (sector + turn + sectors) % sectors},
        )

    def chunk_of(owner):
        return pl.ds(pl.multiple_of(owner * chunk, chunk), chunk)

    def a_copy(step, turn):
        return send(part.at[step, chunk_of((line + turn) % RING)], part_in.at[step, turn], a_send.at[step, turn], a_recv.at[step, turn], {"bins": in_column(turn)})

    def b_copy(step, turn):
        return send(mid.at[step], mid_in.at[step, turn], b_send.at[step, turn], b_recv.at[step, turn], {"bins": in_row(turn)})

    def c_copy(step, turn):
        mine = total.at[step, chunk_of(line)]
        return send(mine, mine, c_send.at[step, turn], c_recv.at[step, turn], {"bins": in_column(turn)})

    def c_from(step, turn):
        theirs = total.at[step, chunk_of((line + RING - turn) % RING)]
        return send(theirs, theirs, c_send.at[step, turn], c_recv.at[step, turn], {"bins": in_column(turn)})

    def square(b, values):
        scaled = bins_ref[b, RATIO] * values
        return scaled * scaled

    def spread_a(step):
        for turn in range(1, RING):
            a_copy(step, turn).start()

    def spread_b(step):
        so_far = part[step, chunk_of(line)]
        for turn in range(1, RING):
            a_copy(step, turn).wait_recv()
            so_far += part_in[step, turn]
        mid[step] = so_far
        for turn in range(1, RING):
            b_copy(step, turn).start()

    def spread_c(step):
        so_far = mid[step]
        for turn in range(1, RING):
            b_copy(step, turn).wait_recv()
            so_far += mid_in[step, turn]
        total[step, chunk_of(line)] = so_far
        for turn in range(1, RING):
            c_copy(step, turn).start()

    def spread_end(step):
        for turn in range(1, RING):
            c_from(step, turn).wait_recv()

    def source(step, b):
        energy = field_of(step)[b]
        above = got[step, 0, b] * bins_ref[b, UPPER]
        below = got[step, 1, b] * bins_ref[b, LOWER]
        ratio = bins_ref[b, RATIO]
        wind = jnp.maximum(bins_ref[b, COS] * gain_x[...] + bins_ref[b, SIN] * gain_y[...], 0.0)
        quad = quad_gain * (energy * (above + below) - 2.0 * above * below)
        grown = energy + energy * (ratio * (wind + quad))
        top = jnp.where(open_sea[...] > 0.0, grown, energy)
        bottom = 1.0 + bins_ref[b, DAMP] * total[step] + ice[...]
        wide[step, b, pl.ds(BASE, columns)] = jnp.where(flags[...] == 0, 0.0, top / bottom)

    def halves(values):
        high = values.astype(jnp.bfloat16)
        return high, (values - high.astype(jnp.float32)).astype(jnp.bfloat16)

    def rates(fields, bins, signs, rows_out):
        parts = [halves(field) for field in fields]
        along_lat = jnp.dot(
            jnp.concatenate([jnp.concatenate(pair_of, axis=1) for pair_of in parts], axis=0),
            lat_taps[...], preferred_element_type=jnp.float32,
        )
        results = []
        for i, (field, pair_of, b) in enumerate(zip(fields, parts, bins)):
            along_lon = jnp.dot(
                lon_taps[signs[i], rows_out], jnp.concatenate(pair_of, axis=0), preferred_element_type=jnp.float32
            )
            start, end = i * ext + rows_out.start, i * ext + rows_out.start + rows_out.size
            east = (bins_ref[b, EAST] + bins_ref[b, WEST]) * rows_ref[...]
            results.append(
                field[rows_out.start : rows_out.start + rows_out.size]
                + along_lon * east
                + along_lat[start:end, :rows] * bins_ref[b, NORTH]
                + along_lat[start:end, rows:] * bins_ref[b, SOUTH]
            )
        return results

    def advance(step, group):
        bins = [group * GROUP + j for j in range(GROUP)]
        directions = [(place * here + b) // NF for b in bins]
        signs = [(d + ND // 4) // (ND // 2) % 2 for d in directions]
        every, inner = pl.ds(0, ext), pl.ds(BASE, columns)
        for j, values in enumerate(rates([wide[step, b] for b in bins], bins, signs, every)):
            one[j] = values
        for j, values in enumerate(rates([one[j] for j in range(GROUP)], bins, signs, every)):
            two[j] = 0.75 * wide[step, bins[j]] + 0.25 * values
        for j, values in enumerate(rates([two[j] for j in range(GROUP)], bins, signs, inner)):
            moved = wide[step, bins[j], inner] * (1.0 / 3.0) + (2.0 / 3.0) * values
            moved = jnp.where(flags[...] == 0, 0.0, moved)
            if step < STEPS - 1:
                later[bins[j]] = moved
                part[step + 1] += square(bins[j], moved)
            else:
                last[bins[j]] = moved

    def result_copy(group):
        some = pl.ds(group * GROUP, GROUP)
        return pltpu.make_async_copy(last.at[some], out_ref.at[some], out_sem.at[group])

    def send_group(step, group):
        for k in range(GROUPS):
            @pl.when(group == k)
            def _(k=k):
                mine = range(k * GROUP, (k + 1) * GROUP)
                for piece, (_, b, *_) in enumerate(FAR):
                    if b in mine:
                        leg(step, piece).start()
                for piece, (_, b, *_) in enumerate(DIRECT):
                    if b in mine:
                        direct(step, piece).start()

    inputs = [(field_hbm, first), (speed_hbm, speed), (heading_hbm, heading), (flags_hbm, flags)]
    inputs = [pltpu.make_async_copy(src, dst, in_sem.at[i]) for i, (src, dst) in enumerate(inputs)]
    for copy in inputs:
        copy.start()

    def band(shape, along, across_it, taps):
        offset = lax.broadcasted_iota(jnp.int32, shape, along) - lax.broadcasted_iota(jnp.int32, shape, across_it)
        matrix = jnp.zeros(shape, jnp.float32)
        for j, tap in enumerate(taps):
            matrix = jnp.where(offset == j - 3, tap, matrix)
        return matrix.astype(jnp.bfloat16)

    for sign, taps in enumerate((PLUS, MINUS)):
        lon_band, lat_band = band((ext, ext), 1, 0, taps), band((rows, rows), 0, 1, taps)
        lon_taps[sign] = jnp.concatenate([lon_band, lon_band], axis=1)
        for half in range(2):
            lat_taps[pl.ds(half * rows, rows), pl.ds(sign * rows, rows)] = lat_band
    for step in range(1, STEPS):
        part[step] = jnp.zeros((columns, rows), jnp.float32)
    inputs[0].wait()
    part[0] = lax.fori_loop(0, here, lambda b, so_far: so_far + square(b, first[b]), jnp.zeros((columns, rows), jnp.float32))
    pl.semaphore_wait(barrier, len(partners))

    spread_a(0)
    for piece in range(len(FAR)):
        leg(0, piece).start()
    for piece in (3, 4, 5, 6, 0, 1, 2):
        direct(0, piece).start()
    for copy in inputs[1:]:
        copy.wait()
    gain = wind_gain * 0.1 * speed[...]
    gain_x[...] = gain * jnp.cos(heading[...])
    gain_y[...] = gain * jnp.sin(heading[...])
    open_sea[...] = jnp.where(flags[...] == 1, 1.0, 0.0)
    ice[...] = jnp.where(flags[...] == 2, ice_loss, 0.0)
    spread_b(0)
    pass_on_far(0, (0, 1, 2))
    pass_on_shared(0, range(len(SHARED)))
    pass_on_far(0, (3, 4))
    spread_c(0)
    spread_end(0)

    for step in range(STEPS):
        if step > 0:
            spread_a(step)
            pass_on_far(step, (4,))
            pass_on_shared(step, (0,))
            spread_b(step)
            pass_on_shared(step, (1, 2))
            pass_on_far(step, (0,))
            spread_c(step)
            spread_end(step)

        @pl.loop(0, GROUPS + LAG)
        def _(g, step=step):
            @pl.when(g < GROUPS)
            def _():
                group = (g + FIRST_GROUP[step]) % GROUPS
                for k in range(GROUPS):
                    @pl.when(group == k)
                    def _(k=k):
                        for piece in NEEDS[step][k]:
                            arrival(step, piece).wait_recv()

                for j in range(GROUP):
                    source(step, group * GROUP + j)
                for side in range(2):
                    halo_copy(step, group, side).start()

            if step < STEPS - 1:
                for piece in (1, 2, 3):
                    @pl.when(g == piece + 4)
                    def _(piece=piece):
                        pass_on_far(step + 1, (piece,))

            @pl.when(g >= LAG)
            def _():
                group = (g - LAG + FIRST_GROUP[step]) % GROUPS
                for side in range(2):
                    halo_copy(step, group, side).wait_recv()
                advance(step, group)
                if step < STEPS - 1:
                    send_group(step + 1, group)
                else:
                    result_copy(group).start()

    for step in range(STEPS):
        for turn in range(1, RING):
            a_copy(step, turn).wait_send()
            b_copy(step, turn).wait_send()
            c_copy(step, turn).wait_send()
        for piece in range(PIECES):
            arrival(step, piece).wait_send()
        for piece in range(len(FAR)):
            leg(step, piece).wait_send()

        @pl.loop(0, GROUPS)
        def _(group, step=step):
            for side in range(2):
                halo_copy(step, group, side).wait_send()

    @pl.loop(0, GROUPS)
    def _(group):
        result_copy(group).wait()


def shards(spectrum, wind_speed, wind_dir, flags):
    here, columns, rows = spectrum.shape
    index = lax.axis_index("bins") * here + jnp.arange(here, dtype=jnp.int32)
    whole = (columns, rows)
    chunk = columns // RING
    ext = columns + 2 * BASE
    hbm = pl.BlockSpec(memory_space=pl.ANY)
    dma = pltpu.SemaphoreType.DMA

    def buffer(*shape):
        return pltpu.VMEM(shape, jnp.float32)

    return pl.pallas_call(
        kernel,
        out_shape=jax.ShapeDtypeStruct(spectrum.shape, jnp.float32),
        in_specs=[hbm] * 4 + [pl.BlockSpec(memory_space=pltpu.SMEM), pl.BlockSpec(memory_space=pltpu.VMEM)],
        out_specs=hbm,
        scratch_shapes=[
            buffer(here, *whole),
            buffer(here, *whole),
            buffer(here, *whole),
            buffer(STEPS, 2, here, *whole),
            buffer(STEPS, here, *whole),
            buffer(STEPS, here, ext, rows),
            buffer(GROUP, ext, rows),
            buffer(GROUP, ext, rows),
            pltpu.VMEM((2, ext, 2 * ext), jnp.bfloat16),
            pltpu.VMEM((2 * rows, 2 * rows), jnp.bfloat16),
            buffer(*whole),
            buffer(*whole),
            pltpu.VMEM(whole, jnp.int32),
            buffer(*whole),
            buffer(*whole),
            buffer(*whole),
            buffer(*whole),
            buffer(STEPS, *whole),
            buffer(STEPS, RING, chunk, rows),
            buffer(STEPS, chunk, rows),
            buffer(STEPS, RING, chunk, rows),
            buffer(STEPS, *whole),
        ]
        + [dma((STEPS, PIECES))] * 2
        + [dma((STEPS, len(FAR)))] * 2
        + [dma((STEPS, 2, GROUPS))] * 2
        + [dma((STEPS, RING))] * 6
        + [dma((4,)), dma((GROUPS,))],
        compiler_params=pltpu.CompilerParams(
            collective_id=0, has_side_effects=True, vmem_limit_bytes=56 * 1024 * 1024
        ),
    )(spectrum, wind_speed, wind_dir, flags, bin_table(index), row_table(rows))


def solution(mesh):
    return jax.shard_map(
        shards,
        mesh=mesh,
        in_specs=(P("bins", "lon", None), P("lon", None), P("lon", None), P("lon", None)),
        out_specs=P("bins", "lon", None),
        check_vma=False,
    )
```

```python
import math

import jax
import jax.numpy as jnp
import numpy as np
from jax import lax
from jax.experimental import pallas as pl
from jax.experimental.pallas import tpu as pltpu
from jax.sharding import PartitionSpec as P

NF = 32
ND = 36
STEPS = 2

wind_gain = 0.5
quad_gain = 0.3
break_gain = 0.3
ice_loss = 1.0
courant = 0.6

LINES, ROW = 8, 4
HALO = 9
BASE = 16
GROUP = 3
GROUPS = 6
LAG = 2
LEG = 2
PLUS = (-2.0, 15.0, -60.0, 20.0, 30.0, -3.0, 0.0)
MINUS = (0.0, 3.0, -30.0, -20.0, 60.0, -15.0, 2.0)

DIRECT = (
    (0, 0, 3, 2, -2), (0, 3, 3, 5, -2), (0, 6, 3, 8, -2), (0, 9, 3, 11, -2), (0, 12, 3, 14, -2), (0, 15, 1, 17, -2),
    (1, 16, 2, 6, 6),
)
SHARED = ((3, 12, 2, 0), (4, 14, 3, 2), (5, 17, 1, 5))
FAR = ((0, 16, 2, 0, -1), (1, 0, 3, 8, 1), (1, 3, 3, 11, -1), (1, 6, 3, 14, 1), (1, 9, 1, 17, -1))
KEPT_BACK = (1, 2)
S0, F0 = len(DIRECT), len(DIRECT) + len(SHARED)
PIECES = F0 + len(FAR)
NEEDS = (
    ((F0, 0, S0, S0 + 1), (1, S0 + 2), (2, 6, F0 + 1), (F0 + 2,), (F0 + 3,), (F0 + 4,)),
    ((F0, S0), (0, 1, S0 + 1, S0 + 2), (2, 6, F0 + 1), (F0 + 2,), (F0 + 3,), (F0 + 4,)),
)
FIRST_GROUP = (0, 1)

RATIO, COS, SIN, DAMP, UPPER, LOWER, EAST, WEST, NORTH, SOUTH = range(10)


def bin_table(places, here):
    index = np.arange(places * here).reshape(places, here)
    theta = (index // NF).astype(np.float32) * np.float32(2.0 * math.pi / ND)
    theta = theta.astype(np.float64)
    level = index % NF
    ratio = 1.05 ** (level - NF // 2.0)
    east = courant * 1.1 ** (-level.astype(np.float64)) * np.cos(theta)
    north = courant * 1.1 ** (-level.astype(np.float64)) * np.sin(theta)
    table = np.zeros((places, 16, 128), np.float32)
    values = (
        ratio,
        np.cos(theta),
        np.sin(theta),
        break_gain * ratio * ratio / (NF * ND),
        level + 2 < NF,
        level >= 2,
        np.maximum(east, 0.0) / -60.0,
        np.minimum(east, 0.0) / -60.0,
        np.maximum(north, 0.0) / -60.0,
        np.minimum(north, 0.0) / -60.0,
    )
    for quantity, value in enumerate(values):
        table[:, quantity, :here] = value
    return table


def row_table(rows):
    lines = np.arange(rows)
    coslat = np.cos((lines - rows / 2 + 0.5) * (0.25 * math.pi / 180.0))
    return np.broadcast_to(1.0 / coslat, (8, rows)).astype(np.float32)


def kernel(
    field_hbm, speed_hbm, heading_hbm, flags_hbm, bins_hbm, rows_hbm, out_ref,
    first, later, last, got, relay, wide, one, two, lon_taps, lat_taps, bins_ref, rows_ref, speed, heading, flags, gain_x, gain_y, open_sea, ice,
    part, part_in, half, half_in, mid, mid_in, total,
    send_sem, got_sem, leg_send, leg_recv, halo_send, halo_recv,
    a_send, a_recv, z_send, z_recv, b_send, b_recv, c_send, c_recv, in_sem, out_sem,
):
    here, columns, rows = field_hbm.shape
    count, sectors = lax.axis_size("bins"), lax.axis_size("lon")
    place, sector = lax.axis_index("bins"), lax.axis_index("lon")
    ext = columns + 2 * BASE
    line, spot = place // (2 * ROW), place // 2 % ROW
    chunk = columns // ROW

    def in_row(turn):
        return (line * ROW + (spot + turn) % ROW) * 2 + place % 2

    def in_column(turn):
        return ((line + turn) % LINES * ROW + spot) * 2 + place % 2

    def opposite():
        return place + 1 - 2 * (place % 2)

    def across(offset):
        return (place + offset + count) % count

    pair, far, core = place // 2, place % 2, sector % 2
    height = far * (sectors // 2) + sector // 2
    around_z = sectors

    def at(pair_offset, climb):
        new = (height + climb + around_z) % around_z
        new_pair = (pair + pair_offset + count // 2) % (count // 2)
        return {"bins": new_pair * 2 + new // (sectors // 2), "lon": new % (sectors // 2) * 2 + core}

    for step in range(STEPS):
        for rows_of in (pl.ds(0, BASE), pl.ds(BASE + columns, BASE)):
            wide[step, :, rows_of] = jnp.zeros((here, BASE, rows), jnp.float32)

    barrier = pltpu.get_barrier_semaphore()
    partners = [{"bins": across(s * o)} for o in (2, 6) for s in (1, -1)]
    partners += [at(o, s * LEG) for o in (-3, -1, 0, 1, 3) for s in (1, -1)]
    partners += [{"bins": in_row(t)} for t in range(1, ROW)]
    partners += [{"bins": in_column(t)} for t in range(1, LINES)]
    partners += [{"bins": opposite()}]
    partners += [{"lon": (sector + s + sectors) % sectors} for s in (1, -1)]
    for partner in partners:
        pl.semaphore_signal(barrier, inc=1, device_id=partner, device_id_type=pl.DeviceIdType.MESH)

    def send(src, dst, send_sem, recv_sem, device):
        return pltpu.make_async_remote_copy(
            src_ref=src, dst_ref=dst, send_sem=send_sem, recv_sem=recv_sem,
            device_id=device, device_id_type=pl.DeviceIdType.MESH,
        )

    def source_of(step):
        return field_hbm if step == 0 else later

    def field_of(step):
        return first if step == 0 else later

    def direct(step, piece):
        kind, b, bins, slot, places = DIRECT[piece]
        return send(
            source_of(step).at[pl.ds(b, bins)], got.at[step, kind, pl.ds(slot, bins)],
            send_sem.at[step, piece], got_sem.at[step, piece], {"bins": across(places)},
        )

    def shared(step, piece):
        _, slot, bins, new_slot = SHARED[piece]
        return send(
            got.at[step, 0, pl.ds(slot, bins)], got.at[step, 1, pl.ds(new_slot, bins)],
            send_sem.at[step, S0 + piece], got_sem.at[step, S0 + piece], {"bins": across(8)},
        )

    def leg(step, piece):
        kind, b, bins, _, way = FAR[piece]
        offset = 1 + 2 * far if kind else far - 1
        return send(
            source_of(step).at[pl.ds(b, bins)], relay.at[step, pl.ds(b, bins)],
            leg_send.at[step, piece], leg_recv.at[step, piece], at(offset, way * LEG),
        )

    def second_leg(step, piece):
        kind, b, bins, slot, way = FAR[piece]
        source_far = (height - way * LEG + around_z) % around_z // (sectors // 2)
        return send(
            relay.at[step, pl.ds(b, bins)], got.at[step, kind, pl.ds(slot, bins)],
            send_sem.at[step, F0 + piece], got_sem.at[step, F0 + piece], at(1 - source_far if kind else 0, way * LEG),
        )

    def arrival(step, piece):
        if piece < S0:
            return direct(step, piece)
        if piece < F0:
            return shared(step, piece - S0)
        return second_leg(step, piece - F0)

    def pass_on_far(step, pieces):
        for piece in pieces:
            leg(step, piece).wait_recv()
            second_leg(step, piece).start()

    def pass_on_shared(step):
        for piece, (before, *_) in enumerate(SHARED):
            direct(step, before).wait_recv()
            shared(step, piece).start()

    def halo_copy(step, group, side):
        if side == 0:
            src, dst, turn = BASE + columns - HALO, BASE - HALO, 1
        else:
            src, dst, turn = BASE, BASE + columns, -1
        ext = wide.at[step, pl.ds(group * GROUP, GROUP)]
        return send(
            ext.at[:, pl.ds(src, HALO)], ext.at[:, pl.ds(dst, HALO)],
            halo_send.at[step, side, group], halo_recv.at[step, side, group],
            {"lon": (sector + turn + sectors) % sectors},
        )

    def chunk_of(owner):
        return pl.ds(pl.multiple_of(owner * chunk, chunk), chunk)

    def a_copy(step, turn):
        return send(part.at[step, chunk_of((spot + turn) % ROW)], part_in.at[step, turn], a_send.at[step, turn], a_recv.at[step, turn], {"bins": in_row(turn)})

    def z_copy(step):
        return send(half.at[step], half_in.at[step], z_send.at[step], z_recv.at[step], {"bins": opposite()})

    def b_copy(step, turn):
        return send(mid.at[step], mid_in.at[step, turn], b_send.at[step, turn], b_recv.at[step, turn], {"bins": in_column(turn)})

    def c_copy(step, turn):
        mine = total.at[step, chunk_of(spot)]
        return send(mine, mine, c_send.at[step, turn], c_recv.at[step, turn], {"bins": in_row(turn)})

    def c_from(step, turn):
        theirs = total.at[step, chunk_of((spot + ROW - turn) % ROW)]
        return send(theirs, theirs, c_send.at[step, turn], c_recv.at[step, turn], {"bins": in_row(turn)})

    def square(b, values):
        scaled = bins_ref[RATIO, b] * values
        return scaled * scaled

    def spread_a(step):
        for turn in range(1, ROW):
            a_copy(step, turn).start()

    def spread_z(step):
        so_far = part[step, chunk_of(spot)]
        for turn in range(1, ROW):
            a_copy(step, turn).wait_recv()
            so_far += part_in[step, turn]
        half[step] = so_far
        z_copy(step).start()

    def spread_b(step):
        z_copy(step).wait_recv()
        mid[step] = half[step] + half_in[step]
        for turn in range(1, LINES):
            b_copy(step, turn).start()

    def spread_c(step):
        so_far = mid[step]
        for turn in range(1, LINES):
            b_copy(step, turn).wait_recv()
            so_far += mid_in[step, turn]
        total[step, chunk_of(spot)] = so_far
        for turn in range(1, ROW):
            c_copy(step, turn).start()

    def spread_end(step):
        for turn in range(1, ROW):
            c_from(step, turn).wait_recv()

    def source(step, b):
        energy = field_of(step)[b]
        above = got[step, 0, b] * bins_ref[UPPER, b]
        below = got[step, 1, b] * bins_ref[LOWER, b]
        ratio = bins_ref[RATIO, b]
        wind = jnp.maximum(bins_ref[COS, b] * gain_x[...] + bins_ref[SIN, b] * gain_y[...], 0.0)
        quad = quad_gain * (energy * (above + below) - 2.0 * above * below)
        grown = energy + energy * (ratio * (wind + quad))
        top = jnp.where(open_sea[...] > 0.0, grown, energy)
        bottom = 1.0 + bins_ref[DAMP, b] * total[step] + ice[...]
        wide[step, b, pl.ds(BASE, columns)] = jnp.where(flags[...] == 0, 0.0, top / bottom)

    def halves(values):
        high = values.astype(jnp.bfloat16)
        return high, (values - high.astype(jnp.float32)).astype(jnp.bfloat16)

    def rates(fields, bins, signs, rows_out):
        parts = [halves(field) for field in fields]
        along_lat = jnp.dot(
            jnp.concatenate([jnp.concatenate(pair_of, axis=1) for pair_of in parts], axis=0),
            lat_taps[...], preferred_element_type=jnp.float32,
        )
        results = []
        for i, (field, pair_of, b) in enumerate(zip(fields, parts, bins)):
            along_lon = jnp.dot(
                lon_taps[signs[i], rows_out], jnp.concatenate(pair_of, axis=0), preferred_element_type=jnp.float32
            )
            start, end = i * ext + rows_out.start, i * ext + rows_out.start + rows_out.size
            east = (bins_ref[EAST, b] + bins_ref[WEST, b]) * rows_ref[0:1]
            results.append(
                field[rows_out.start : rows_out.start + rows_out.size]
                + along_lon * east
                + along_lat[start:end, :rows] * bins_ref[NORTH, b]
                + along_lat[start:end, rows:] * bins_ref[SOUTH, b]
            )
        return results

    def advance(step, group):
        bins = [group * GROUP + j for j in range(GROUP)]
        directions = [(place * here + b) // NF for b in bins]
        signs = [(d + ND // 4) // (ND // 2) % 2 for d in directions]
        every, inner = pl.ds(0, ext), pl.ds(BASE, columns)
        for j, values in enumerate(rates([wide[step, b] for b in bins], bins, signs, every)):
            one[j] = values
        for j, values in enumerate(rates([one[j] for j in range(GROUP)], bins, signs, every)):
            two[j] = 0.75 * wide[step, bins[j]] + 0.25 * values
        for j, values in enumerate(rates([two[j] for j in range(GROUP)], bins, signs, inner)):
            moved = wide[step, bins[j], inner] * (1.0 / 3.0) + (2.0 / 3.0) * values
            moved = jnp.where(flags[...] == 0, 0.0, moved)
            if step < STEPS - 1:
                later[bins[j]] = moved
                part[step + 1] += square(bins[j], moved)
            else:
                last[bins[j]] = moved

    def result_copy(group):
        some = pl.ds(group * GROUP, GROUP)
        return pltpu.make_async_copy(last.at[some], out_ref.at[some], out_sem.at[group])

    def send_group(step, group):
        for k in range(GROUPS):
            @pl.when(group == k)
            def _(k=k):
                mine = range(k * GROUP, (k + 1) * GROUP)
                for piece, (_, b, *_) in enumerate(FAR):
                    if b in mine:
                        leg(step, piece).start()
                for piece, (_, b, *_) in enumerate(DIRECT):
                    if b in mine and piece not in KEPT_BACK:
                        direct(step, piece).start()

    inputs = [(field_hbm, first), (speed_hbm, speed), (heading_hbm, heading), (flags_hbm, flags),
              (bins_hbm.at[place], bins_ref), (rows_hbm, rows_ref)]
    inputs = [pltpu.make_async_copy(src, dst, in_sem.at[i]) for i, (src, dst) in enumerate(inputs)]
    for copy in inputs:
        copy.start()

    def band(shape, along, across_it, taps):
        offset = lax.broadcasted_iota(jnp.int32, shape, along) - lax.broadcasted_iota(jnp.int32, shape, across_it)
        matrix = jnp.zeros(shape, jnp.float32)
        for j, tap in enumerate(taps):
            matrix = jnp.where(offset == j - 3, tap, matrix)
        return matrix.astype(jnp.bfloat16)

    for sign, taps in enumerate((PLUS, MINUS)):
        lon_band, lat_band = band((ext, ext), 1, 0, taps), band((rows, rows), 0, 1, taps)
        lon_taps[sign] = jnp.concatenate([lon_band, lon_band], axis=1)
        for part_of in range(2):
            lat_taps[pl.ds(part_of * rows, rows), pl.ds(sign * rows, rows)] = lat_band
    for step in range(1, STEPS):
        part[step] = jnp.zeros((columns, rows), jnp.float32)
    for copy in inputs[4:] + inputs[:1]:
        copy.wait()
    part[0] = lax.fori_loop(0, here, lambda b, so_far: so_far + square(b, first[b]), jnp.zeros((columns, rows), jnp.float32))
    pl.semaphore_wait(barrier, len(partners))

    spread_a(0)
    for piece in range(len(FAR)):
        leg(0, piece).start()
    for piece in (3, 4, 5, 6, 0):
        direct(0, piece).start()
    for copy in inputs[1:4]:
        copy.wait()
    gain = wind_gain * 0.1 * speed[...]
    gain_x[...] = gain * jnp.cos(heading[...])
    gain_y[...] = gain * jnp.sin(heading[...])
    open_sea[...] = jnp.where(flags[...] == 1, 1.0, 0.0)
    ice[...] = jnp.where(flags[...] == 2, ice_loss, 0.0)
    spread_z(0)
    direct(0, 1).start()
    spread_b(0)
    direct(0, 2).start()
    pass_on_far(0, (0, 1, 2))
    spread_c(0)
    pass_on_far(0, (3, 4))
    pass_on_shared(0)
    spread_end(0)

    for step in range(STEPS):
        if step > 0:
            spread_a(step)
            direct(step, 1).start()
            pass_on_far(step, (1,))
            spread_z(step)
            direct(step, 2).start()
            pass_on_far(step, (2, 3))
            spread_b(step)
            pass_on_far(step, (4,))
            pass_on_shared(step)
            spread_c(step)
            pass_on_far(step, (0,))
            spread_end(step)

        @pl.loop(0, GROUPS + LAG)
        def _(g, step=step):
            @pl.when(g < GROUPS)
            def _():
                group = (g + FIRST_GROUP[step]) % GROUPS
                for k in range(GROUPS):
                    @pl.when(group == k)
                    def _(k=k):
                        for piece in NEEDS[step][k]:
                            arrival(step, piece).wait_recv()

                for j in range(GROUP):
                    source(step, group * GROUP + j)
                for side in range(2):
                    halo_copy(step, group, side).start()

            @pl.when(g >= LAG)
            def _():
                group = (g - LAG + FIRST_GROUP[step]) % GROUPS
                for side in range(2):
                    halo_copy(step, group, side).wait_recv()
                advance(step, group)
                if step < STEPS - 1:
                    send_group(step + 1, group)
                else:
                    result_copy(group).start()

    for step in range(STEPS):
        z_copy(step).wait_send()
        for turn in range(1, ROW):
            a_copy(step, turn).wait_send()
            c_copy(step, turn).wait_send()
        for turn in range(1, LINES):
            b_copy(step, turn).wait_send()
        for piece in range(PIECES):
            arrival(step, piece).wait_send()
        for piece in range(len(FAR)):
            leg(step, piece).wait_send()

        @pl.loop(0, GROUPS)
        def _(group, step=step):
            for side in range(2):
                halo_copy(step, group, side).wait_send()

    @pl.loop(0, GROUPS)
    def _(group):
        result_copy(group).wait()


def shards(spectrum, wind_speed, wind_dir, flags):
    here, columns, rows = spectrum.shape
    whole = (columns, rows)
    chunk = columns // ROW
    ext = columns + 2 * BASE
    hbm = pl.BlockSpec(memory_space=pl.ANY)
    dma = pltpu.SemaphoreType.DMA

    def buffer(*shape):
        return pltpu.VMEM(shape, jnp.float32)

    return pl.pallas_call(
        kernel,
        out_shape=jax.ShapeDtypeStruct(spectrum.shape, jnp.float32),
        in_specs=[hbm] * 6,
        out_specs=hbm,
        scratch_shapes=[
            buffer(here, *whole),
            buffer(here, *whole),
            buffer(here, *whole),
            buffer(STEPS, 2, here, *whole),
            buffer(STEPS, here, *whole),
            buffer(STEPS, here, ext, rows),
            buffer(GROUP, ext, rows),
            buffer(GROUP, ext, rows),
            pltpu.VMEM((2, ext, 2 * ext), jnp.bfloat16),
            pltpu.VMEM((2 * rows, 2 * rows), jnp.bfloat16),
            pltpu.SMEM((16, 128), jnp.float32),
            buffer(8, rows),
            buffer(*whole),
            buffer(*whole),
            pltpu.VMEM(whole, jnp.int32),
            buffer(*whole),
            buffer(*whole),
            buffer(*whole),
            buffer(*whole),
            buffer(STEPS, *whole),
            buffer(STEPS, ROW, chunk, rows),
            buffer(STEPS, chunk, rows),
            buffer(STEPS, chunk, rows),
            buffer(STEPS, chunk, rows),
            buffer(STEPS, LINES, chunk, rows),
            buffer(STEPS, *whole),
        ]
        + [dma((STEPS, PIECES))] * 2
        + [dma((STEPS, len(FAR)))] * 2
        + [dma((STEPS, 2, GROUPS))] * 2
        + [dma((STEPS, ROW))] * 2
        + [dma((STEPS,))] * 2
        + [dma((STEPS, LINES))] * 2
        + [dma((STEPS, ROW))] * 2
        + [dma((6,)), dma((GROUPS,))],
        compiler_params=pltpu.CompilerParams(
            collective_id=0, has_side_effects=True, vmem_limit_bytes=56 * 1024 * 1024
        ),
    )(spectrum, wind_speed, wind_dir, flags, bin_table(lax.axis_size("bins"), here), row_table(rows))


def solution(mesh):
    return jax.shard_map(
        shards,
        mesh=mesh,
        in_specs=(P("bins", "lon", None), P("lon", None), P("lon", None), P("lon", None)),
        out_specs=P("bins", "lon", None),
        check_vma=False,
    )
```

```python
import math

import jax
import jax.numpy as jnp
import numpy as np
from jax import lax
from jax.experimental import pallas as pl
from jax.experimental.pallas import tpu as pltpu
from jax.sharding import PartitionSpec as P

NF = 32
ND = 36
STEPS = 2

wind_gain = 0.5
quad_gain = 0.3
break_gain = 0.3
ice_loss = 1.0
courant = 0.6

LINES, ROW = 8, 4
HALO = 9
BASE = 16
GROUP = 3
GROUPS = 6
LAG = 2
LEG = 2
PLUS = (-2.0, 15.0, -60.0, 20.0, 30.0, -3.0, 0.0)
MINUS = (0.0, 3.0, -30.0, -20.0, 60.0, -15.0, 2.0)

DIRECT = (
    (0, 0, 3, 2, -2), (0, 3, 3, 5, -2), (0, 6, 3, 8, -2), (0, 9, 3, 11, -2), (0, 12, 3, 14, -2), (0, 15, 1, 17, -2),
    (1, 16, 2, 6, 6),
)
SHARED = ((3, 12, 2, 0), (4, 14, 3, 2), (5, 17, 1, 5))
FAR = ((0, 16, 2, 0, -1), (1, 0, 3, 8, 1), (1, 3, 3, 11, -1), (1, 6, 3, 14, 1), (1, 9, 1, 17, -1))
S0, F0 = len(DIRECT), len(DIRECT) + len(SHARED)
PIECES = F0 + len(FAR)
NEEDS = (
    ((F0, 0, S0, S0 + 1), (1, S0 + 2), (2, 6, F0 + 1), (F0 + 2,), (F0 + 3,), (F0 + 4,)),
    ((F0, S0), (0, 1, S0 + 1, S0 + 2), (2, 6, F0 + 1), (F0 + 2,), (F0 + 3,), (F0 + 4,)),
)
FIRST_GROUP = (0, 1)

RATIO, COS, SIN, DAMP, UPPER, LOWER, EAST, WEST, NORTH, SOUTH = range(10)


def bin_table(places, here):
    index = np.arange(places * here).reshape(places, here)
    theta = (index // NF).astype(np.float32) * np.float32(2.0 * math.pi / ND)
    theta = theta.astype(np.float64)
    level = index % NF
    ratio = 1.05 ** (level - NF // 2.0)
    east = courant * 1.1 ** (-level.astype(np.float64)) * np.cos(theta)
    north = courant * 1.1 ** (-level.astype(np.float64)) * np.sin(theta)
    table = np.zeros((places, 16, 128), np.float32)
    values = (
        ratio,
        np.cos(theta),
        np.sin(theta),
        break_gain * ratio * ratio / (NF * ND),
        level + 2 < NF,
        level >= 2,
        np.maximum(east, 0.0) / -60.0,
        np.minimum(east, 0.0) / -60.0,
        np.maximum(north, 0.0) / -60.0,
        np.minimum(north, 0.0) / -60.0,
    )
    for quantity, value in enumerate(values):
        table[:, quantity, :here] = value
    return table


def row_table(rows):
    lines = np.arange(rows)
    coslat = np.cos((lines - rows / 2 + 0.5) * (0.25 * math.pi / 180.0))
    return np.broadcast_to(1.0 / coslat, (8, rows)).astype(np.float32)


def kernel(
    field_hbm, speed_hbm, heading_hbm, flags_hbm, bins_hbm, rows_hbm, out_ref,
    first, later, last, got, relay, wide, one, two, lon_taps, lat_taps, bins_ref, rows_ref, speed, heading, flags, gain_x, gain_y, open_sea, ice,
    part, part_in, half, half_in, mid, mid_in, total,
    send_sem, got_sem, leg_send, leg_recv, halo_send, halo_recv,
    a_send, a_recv, z_send, z_recv, b_send, b_recv, c_send, c_recv, in_sem, out_sem,
):
    here, columns, rows = field_hbm.shape
    count, sectors = lax.axis_size("bins"), lax.axis_size("lon")
    place, sector = lax.axis_index("bins"), lax.axis_index("lon")
    ext = columns + 2 * BASE
    line, spot = place // (2 * ROW), place // 2 % ROW
    chunk = columns // ROW

    def in_row(turn):
        return (line * ROW + (spot + turn) % ROW) * 2 + place % 2

    def in_column(turn):
        return ((line + turn) % LINES * ROW + spot) * 2 + place % 2

    def opposite():
        return place + 1 - 2 * (place % 2)

    def across(offset):
        return (place + offset + count) % count

    pair, far, core = place // 2, place % 2, sector % 2
    height = far * (sectors // 2) + sector // 2
    around_z = sectors

    def at(pair_offset, climb):
        new = (height + climb + around_z) % around_z
        new_pair = (pair + pair_offset + count // 2) % (count // 2)
        return {"bins": new_pair * 2 + new // (sectors // 2), "lon": new % (sectors // 2) * 2 + core}

    for step in range(STEPS):
        for rows_of in (pl.ds(0, BASE), pl.ds(BASE + columns, BASE)):
            wide[step, :, rows_of] = jnp.zeros((here, BASE, rows), jnp.float32)

    barrier = pltpu.get_barrier_semaphore()
    partners = [{"bins": across(s * o)} for o in (2, 6) for s in (1, -1)]
    partners += [at(o, s * LEG) for o in (-3, -1, 0, 1, 3) for s in (1, -1)]
    partners += [{"bins": in_row(t)} for t in range(1, ROW)]
    partners += [{"bins": in_column(t)} for t in range(1, LINES)]
    partners += [{"bins": opposite()}]
    partners += [{"lon": (sector + s + sectors) % sectors} for s in (1, -1)]
    for partner in partners:
        pl.semaphore_signal(barrier, inc=1, device_id=partner, device_id_type=pl.DeviceIdType.MESH)

    def send(src, dst, send_sem, recv_sem, device):
        return pltpu.make_async_remote_copy(
            src_ref=src, dst_ref=dst, send_sem=send_sem, recv_sem=recv_sem,
            device_id=device, device_id_type=pl.DeviceIdType.MESH,
        )

    def source_of(step):
        return field_hbm if step == 0 else later

    def field_of(step):
        return first if step == 0 else later

    def direct(step, piece):
        kind, b, bins, slot, places = DIRECT[piece]
        return send(
            source_of(step).at[pl.ds(b, bins)], got.at[step, kind, pl.ds(slot, bins)],
            send_sem.at[step, piece], got_sem.at[step, piece], {"bins": across(places)},
        )

    def shared(step, piece):
        _, slot, bins, new_slot = SHARED[piece]
        return send(
            got.at[step, 0, pl.ds(slot, bins)], got.at[step, 1, pl.ds(new_slot, bins)],
            send_sem.at[step, S0 + piece], got_sem.at[step, S0 + piece], {"bins": across(8)},
        )

    def leg(step, piece):
        kind, b, bins, _, way = FAR[piece]
        offset = 1 + 2 * far if kind else far - 1
        return send(
            source_of(step).at[pl.ds(b, bins)], relay.at[step, pl.ds(b, bins)],
            leg_send.at[step, piece], leg_recv.at[step, piece], at(offset, way * LEG),
        )

    def second_leg(step, piece):
        kind, b, bins, slot, way = FAR[piece]
        source_far = (height - way * LEG + around_z) % around_z // (sectors // 2)
        return send(
            relay.at[step, pl.ds(b, bins)], got.at[step, kind, pl.ds(slot, bins)],
            send_sem.at[step, F0 + piece], got_sem.at[step, F0 + piece], at(1 - source_far if kind else 0, way * LEG),
        )

    def arrival(step, piece):
        if piece < S0:
            return direct(step, piece)
        if piece < F0:
            return shared(step, piece - S0)
        return second_leg(step, piece - F0)

    def pass_on_far(step, pieces):
        for piece in pieces:
            leg(step, piece).wait_recv()
            second_leg(step, piece).start()

    def pass_on_shared(step, pieces):
        for piece in pieces:
            direct(step, SHARED[piece][0]).wait_recv()
            shared(step, piece).start()

    def halo_copy(step, group, side):
        if side == 0:
            src, dst, turn = BASE + columns - HALO, BASE - HALO, 1
        else:
            src, dst, turn = BASE, BASE + columns, -1
        ext = wide.at[step, pl.ds(group * GROUP, GROUP)]
        return send(
            ext.at[:, pl.ds(src, HALO)], ext.at[:, pl.ds(dst, HALO)],
            halo_send.at[step, side, group], halo_recv.at[step, side, group],
            {"lon": (sector + turn + sectors) % sectors},
        )

    def chunk_of(owner):
        return pl.ds(pl.multiple_of(owner * chunk, chunk), chunk)

    def a_copy(step, turn):
        return send(part.at[step, chunk_of((spot + turn) % ROW)], part_in.at[step, turn], a_send.at[step, turn], a_recv.at[step, turn], {"bins": in_row(turn)})

    def z_copy(step):
        return send(half.at[step], half_in.at[step], z_send.at[step], z_recv.at[step], {"bins": opposite()})

    def b_copy(step, turn):
        return send(mid.at[step], mid_in.at[step, turn], b_send.at[step, turn], b_recv.at[step, turn], {"bins": in_column(turn)})

    def c_copy(step, turn):
        mine = total.at[step, chunk_of(spot)]
        return send(mine, mine, c_send.at[step, turn], c_recv.at[step, turn], {"bins": in_row(turn)})

    def c_from(step, turn):
        theirs = total.at[step, chunk_of((spot + ROW - turn) % ROW)]
        return send(theirs, theirs, c_send.at[step, turn], c_recv.at[step, turn], {"bins": in_row(turn)})

    def square(b, values):
        scaled = bins_ref[RATIO, b] * values
        return scaled * scaled

    def spread_a(step):
        for turn in range(1, ROW):
            a_copy(step, turn).start()

    def spread_z(step):
        so_far = part[step, chunk_of(spot)]
        for turn in range(1, ROW):
            a_copy(step, turn).wait_recv()
            so_far += part_in[step, turn]
        half[step] = so_far
        z_copy(step).start()

    def spread_b(step):
        z_copy(step).wait_recv()
        mid[step] = half[step] + half_in[step]
        for turn in range(1, LINES):
            b_copy(step, turn).start()

    def spread_c(step):
        so_far = mid[step]
        for turn in range(1, LINES):
            b_copy(step, turn).wait_recv()
            so_far += mid_in[step, turn]
        total[step, chunk_of(spot)] = so_far
        for turn in range(1, ROW):
            c_copy(step, turn).start()

    def spread_end(step):
        for turn in range(1, ROW):
            c_from(step, turn).wait_recv()

    def source(step, b):
        energy = field_of(step)[b]
        above = got[step, 0, b] * bins_ref[UPPER, b]
        below = got[step, 1, b] * bins_ref[LOWER, b]
        ratio = bins_ref[RATIO, b]
        wind = jnp.maximum(bins_ref[COS, b] * gain_x[...] + bins_ref[SIN, b] * gain_y[...], 0.0)
        quad = quad_gain * (energy * (above + below) - 2.0 * above * below)
        grown = energy + energy * (ratio * (wind + quad))
        top = jnp.where(open_sea[...] > 0.0, grown, energy)
        bottom = 1.0 + bins_ref[DAMP, b] * total[step] + ice[...]
        wide[step, b, pl.ds(BASE, columns)] = jnp.where(flags[...] == 0, 0.0, top / bottom)

    def halves(values):
        high = values.astype(jnp.bfloat16)
        return high, (values - high.astype(jnp.float32)).astype(jnp.bfloat16)

    def rates(fields, bins, signs, rows_out):
        parts = [halves(field) for field in fields]
        along_lat = jnp.dot(
            jnp.concatenate([jnp.concatenate(pair_of, axis=1) for pair_of in parts], axis=0),
            lat_taps[...], preferred_element_type=jnp.float32,
        )
        results = []
        for i, (field, pair_of, b) in enumerate(zip(fields, parts, bins)):
            along_lon = jnp.dot(
                lon_taps[signs[i], rows_out], jnp.concatenate(pair_of, axis=0), preferred_element_type=jnp.float32
            )
            start, end = i * ext + rows_out.start, i * ext + rows_out.start + rows_out.size
            east = (bins_ref[EAST, b] + bins_ref[WEST, b]) * rows_ref[0:1]
            results.append(
                field[rows_out.start : rows_out.start + rows_out.size]
                + along_lon * east
                + along_lat[start:end, :rows] * bins_ref[NORTH, b]
                + along_lat[start:end, rows:] * bins_ref[SOUTH, b]
            )
        return results

    def advance(step, group):
        bins = [group * GROUP + j for j in range(GROUP)]
        directions = [(place * here + b) // NF for b in bins]
        signs = [(d + ND // 4) // (ND // 2) % 2 for d in directions]
        every, inner = pl.ds(0, ext), pl.ds(BASE, columns)
        for j, values in enumerate(rates([wide[step, b] for b in bins], bins, signs, every)):
            one[j] = values
        for j, values in enumerate(rates([one[j] for j in range(GROUP)], bins, signs, every)):
            two[j] = 0.75 * wide[step, bins[j]] + 0.25 * values
        for j, values in enumerate(rates([two[j] for j in range(GROUP)], bins, signs, inner)):
            moved = wide[step, bins[j], inner] * (1.0 / 3.0) + (2.0 / 3.0) * values
            moved = jnp.where(flags[...] == 0, 0.0, moved)
            if step < STEPS - 1:
                later[bins[j]] = moved
                part[step + 1] += square(bins[j], moved)
            else:
                last[bins[j]] = moved

    def result_copy(group):
        some = pl.ds(group * GROUP, GROUP)
        return pltpu.make_async_copy(last.at[some], out_ref.at[some], out_sem.at[group])

    def send_group(step, group):
        for k in range(GROUPS):
            @pl.when(group == k)
            def _(k=k):
                mine = range(k * GROUP, (k + 1) * GROUP)
                for piece, (_, b, *_) in enumerate(FAR):
                    if b in mine:
                        leg(step, piece).start()
                for piece, (_, b, *_) in enumerate(DIRECT):
                    if b in mine:
                        direct(step, piece).start()

    inputs = [(field_hbm, first), (speed_hbm, speed), (heading_hbm, heading), (flags_hbm, flags),
              (bins_hbm.at[place], bins_ref), (rows_hbm, rows_ref)]
    inputs = [pltpu.make_async_copy(src, dst, in_sem.at[i]) for i, (src, dst) in enumerate(inputs)]
    for copy in inputs:
        copy.start()

    def band(shape, along, across_it, taps):
        offset = lax.broadcasted_iota(jnp.int32, shape, along) - lax.broadcasted_iota(jnp.int32, shape, across_it)
        matrix = jnp.zeros(shape, jnp.float32)
        for j, tap in enumerate(taps):
            matrix = jnp.where(offset == j - 3, tap, matrix)
        return matrix.astype(jnp.bfloat16)

    for sign, taps in enumerate((PLUS, MINUS)):
        lon_band, lat_band = band((ext, ext), 1, 0, taps), band((rows, rows), 0, 1, taps)
        lon_taps[sign] = jnp.concatenate([lon_band, lon_band], axis=1)
        for part_of in range(2):
            lat_taps[pl.ds(part_of * rows, rows), pl.ds(sign * rows, rows)] = lat_band
    for step in range(1, STEPS):
        part[step] = jnp.zeros((columns, rows), jnp.float32)
    for copy in inputs[4:] + inputs[:1]:
        copy.wait()
    part[0] = lax.fori_loop(0, here, lambda b, so_far: so_far + square(b, first[b]), jnp.zeros((columns, rows), jnp.float32))
    pl.semaphore_wait(barrier, len(partners))

    spread_a(0)
    for piece in range(len(FAR)):
        leg(0, piece).start()
    for piece in (3, 4, 5, 0, 6, 1, 2):
        direct(0, piece).start()
    for copy in inputs[1:4]:
        copy.wait()
    gain = wind_gain * 0.1 * speed[...]
    gain_x[...] = gain * jnp.cos(heading[...])
    gain_y[...] = gain * jnp.sin(heading[...])
    open_sea[...] = jnp.where(flags[...] == 1, 1.0, 0.0)
    ice[...] = jnp.where(flags[...] == 2, ice_loss, 0.0)
    spread_z(0)
    pass_on_far(0, (0, 1))
    pass_on_shared(0, (0, 1, 2))
    spread_b(0)
    pass_on_far(0, (2, 3, 4))
    spread_c(0)
    spread_end(0)

    for step in range(STEPS):
        if step > 0:
            spread_a(step)
            pass_on_far(step, (1, 2, 3))
            spread_z(step)
            pass_on_far(step, (4,))
            pass_on_shared(step, (0, 1, 2))
            pass_on_far(step, (0,))
            spread_b(step)
            spread_c(step)
            spread_end(step)

        @pl.loop(0, GROUPS + LAG)
        def _(g, step=step):
            @pl.when(g < GROUPS)
            def _():
                group = (g + FIRST_GROUP[step]) % GROUPS
                for k in range(GROUPS):
                    @pl.when(group == k)
                    def _(k=k):
                        for piece in NEEDS[step][k]:
                            arrival(step, piece).wait_recv()

                for j in range(GROUP):
                    source(step, group * GROUP + j)
                for side in range(2):
                    halo_copy(step, group, side).start()

            @pl.when(g >= LAG)
            def _():
                group = (g - LAG + FIRST_GROUP[step]) % GROUPS
                for side in range(2):
                    halo_copy(step, group, side).wait_recv()
                advance(step, group)
                if step < STEPS - 1:
                    send_group(step + 1, group)
                else:
                    result_copy(group).start()

    for step in range(STEPS):
        z_copy(step).wait_send()
        for turn in range(1, ROW):
            a_copy(step, turn).wait_send()
            c_copy(step, turn).wait_send()
        for turn in range(1, LINES):
            b_copy(step, turn).wait_send()
        for piece in range(PIECES):
            arrival(step, piece).wait_send()
        for piece in range(len(FAR)):
            leg(step, piece).wait_send()

        @pl.loop(0, GROUPS)
        def _(group, step=step):
            for side in range(2):
                halo_copy(step, group, side).wait_send()

    @pl.loop(0, GROUPS)
    def _(group):
        result_copy(group).wait()


def shards(spectrum, wind_speed, wind_dir, flags):
    here, columns, rows = spectrum.shape
    whole = (columns, rows)
    chunk = columns // ROW
    ext = columns + 2 * BASE
    hbm = pl.BlockSpec(memory_space=pl.ANY)
    dma = pltpu.SemaphoreType.DMA

    def buffer(*shape):
        return pltpu.VMEM(shape, jnp.float32)

    return pl.pallas_call(
        kernel,
        out_shape=jax.ShapeDtypeStruct(spectrum.shape, jnp.float32),
        in_specs=[hbm] * 6,
        out_specs=hbm,
        scratch_shapes=[
            buffer(here, *whole),
            buffer(here, *whole),
            buffer(here, *whole),
            buffer(STEPS, 2, here, *whole),
            buffer(STEPS, here, *whole),
            buffer(STEPS, here, ext, rows),
            buffer(GROUP, ext, rows),
            buffer(GROUP, ext, rows),
            pltpu.VMEM((2, ext, 2 * ext), jnp.bfloat16),
            pltpu.VMEM((2 * rows, 2 * rows), jnp.bfloat16),
            pltpu.SMEM((16, 128), jnp.float32),
            buffer(8, rows),
            buffer(*whole),
            buffer(*whole),
            pltpu.VMEM(whole, jnp.int32),
            buffer(*whole),
            buffer(*whole),
            buffer(*whole),
            buffer(*whole),
            buffer(STEPS, *whole),
            buffer(STEPS, ROW, chunk, rows),
            buffer(STEPS, chunk, rows),
            buffer(STEPS, chunk, rows),
            buffer(STEPS, chunk, rows),
            buffer(STEPS, LINES, chunk, rows),
            buffer(STEPS, *whole),
        ]
        + [dma((STEPS, PIECES))] * 2
        + [dma((STEPS, len(FAR)))] * 2
        + [dma((STEPS, 2, GROUPS))] * 2
        + [dma((STEPS, ROW))] * 2
        + [dma((STEPS,))] * 2
        + [dma((STEPS, LINES))] * 2
        + [dma((STEPS, ROW))] * 2
        + [dma((6,)), dma((GROUPS,))],
        compiler_params=pltpu.CompilerParams(
            collective_id=0, has_side_effects=True, vmem_limit_bytes=56 * 1024 * 1024
        ),
    )(spectrum, wind_speed, wind_dir, flags, bin_table(lax.axis_size("bins"), here), row_table(rows))


def solution(mesh):
    return jax.shard_map(
        shards,
        mesh=mesh,
        in_specs=(P("bins", "lon", None), P("lon", None), P("lon", None), P("lon", None)),
        out_specs=P("bins", "lon", None),
        check_vma=False,
    )
```

```python
import math

import jax
import jax.numpy as jnp
import numpy as np
from jax import lax
from jax.experimental import pallas as pl
from jax.experimental.pallas import tpu as pltpu
from jax.sharding import PartitionSpec as P

NF = 32
ND = 36
STEPS = 2

wind_gain = 0.5
quad_gain = 0.3
break_gain = 0.3
ice_loss = 1.0
courant = 0.6

RING = 8
HALO = 9
BASE = 16
GROUP = 3
GROUPS = 6
LAG = 2
LEG = 2
PLUS = (-2.0, 15.0, -60.0, 20.0, 30.0, -3.0, 0.0)
MINUS = (0.0, 3.0, -30.0, -20.0, 60.0, -15.0, 2.0)

DIRECT = (
    (0, 0, 3, 2, -2), (0, 3, 3, 5, -2), (0, 6, 3, 8, -2), (0, 9, 3, 11, -2), (0, 12, 3, 14, -2), (0, 15, 1, 17, -2),
    (1, 16, 2, 6, 6),
)
SHARED = ((3, 12, 2, 0), (4, 14, 3, 2), (5, 17, 1, 5))
FAR = ((0, 16, 2, 0, -1), (1, 0, 3, 8, 1), (1, 3, 3, 11, -1), (1, 6, 3, 14, 1), (1, 9, 1, 17, -1))
KEPT_BACK = (1, 2)
S0, F0 = len(DIRECT), len(DIRECT) + len(SHARED)
PIECES = F0 + len(FAR)
NEEDS = (
    ((F0, 0, S0, S0 + 1), (1, S0 + 2), (2, 6, F0 + 1), (F0 + 2,), (F0 + 3,), (F0 + 4,)),
    ((F0, S0), (0, 1, S0 + 1, S0 + 2), (2, 6, F0 + 1), (F0 + 2,), (F0 + 3,), (F0 + 4,)),
)
FIRST_GROUP = (0, 1)

RATIO, COS, SIN, DAMP, UPPER, LOWER, EAST, WEST, NORTH, SOUTH = range(10)


def bin_table(places, here):
    index = np.arange(places * here).reshape(places, here)
    theta = (index // NF).astype(np.float32) * np.float32(2.0 * math.pi / ND)
    theta = theta.astype(np.float64)
    level = index % NF
    ratio = 1.05 ** (level - NF // 2.0)
    east = courant * 1.1 ** (-level.astype(np.float64)) * np.cos(theta)
    north = courant * 1.1 ** (-level.astype(np.float64)) * np.sin(theta)
    table = np.zeros((places, 16, 128), np.float32)
    values = (
        ratio,
        np.cos(theta),
        np.sin(theta),
        break_gain * ratio * ratio / (NF * ND),
        level + 2 < NF,
        level >= 2,
        np.maximum(east, 0.0) / -60.0,
        np.minimum(east, 0.0) / -60.0,
        np.maximum(north, 0.0) / -60.0,
        np.minimum(north, 0.0) / -60.0,
    )
    for quantity, value in enumerate(values):
        table[:, quantity, :here] = value
    return table


def row_table(rows):
    lines = np.arange(rows)
    coslat = np.cos((lines - rows / 2 + 0.5) * (0.25 * math.pi / 180.0))
    return np.broadcast_to(1.0 / coslat, (8, rows)).astype(np.float32)


def kernel(
    field_hbm, speed_hbm, heading_hbm, flags_hbm, bins_hbm, rows_hbm, out_ref,
    first, later, last, got, relay, wide, one, two, lon_taps, lat_taps, bins_ref, rows_ref, speed, heading, flags, gain_x, gain_y, open_sea, ice,
    part, part_in, mid, mid_in, total,
    send_sem, got_sem, leg_send, leg_recv, halo_send, halo_recv,
    a_send, a_recv, b_send, b_recv, c_send, c_recv, in_sem, out_sem,
):
    here, columns, rows = field_hbm.shape
    count, sectors = lax.axis_size("bins"), lax.axis_size("lon")
    place, sector = lax.axis_index("bins"), lax.axis_index("lon")
    ext = columns + 2 * BASE
    line, spot = place // RING, place % RING
    chunk = columns // RING
    def in_row(turn):
        return line * RING + (spot + turn) % RING

    def in_column(turn):
        return (line + turn) % RING * RING + spot

    def across(offset):
        return (place + offset + count) % count

    pair, far, core = place // 2, place % 2, sector % 2
    height = far * (sectors // 2) + sector // 2
    around_z = sectors

    def at(pair_offset, climb):
        new = (height + climb + around_z) % around_z
        new_pair = (pair + pair_offset + count // 2) % (count // 2)
        return {"bins": new_pair * 2 + new // (sectors // 2), "lon": new % (sectors // 2) * 2 + core}

    for step in range(STEPS):
        for rows_of in (pl.ds(0, BASE), pl.ds(BASE + columns, BASE)):
            wide[step, :, rows_of] = jnp.zeros((here, BASE, rows), jnp.float32)

    barrier = pltpu.get_barrier_semaphore()
    partners = [{"bins": across(s * o)} for o in (2, 6, 8) for s in (1, -1)]
    partners += [at(o, s * LEG) for o in (-3, -1, 0, 1, 3) for s in (1, -1)]
    partners += [{"bins": in_row(t)} for t in range(1, RING)]
    partners += [{"bins": in_column(t)} for t in range(1, RING)]
    partners += [{"lon": (sector + s + sectors) % sectors} for s in (1, -1)]
    for partner in partners:
        pl.semaphore_signal(barrier, inc=1, device_id=partner, device_id_type=pl.DeviceIdType.MESH)

    def send(src, dst, send_sem, recv_sem, device):
        return pltpu.make_async_remote_copy(
            src_ref=src, dst_ref=dst, send_sem=send_sem, recv_sem=recv_sem,
            device_id=device, device_id_type=pl.DeviceIdType.MESH,
        )

    def source_of(step):
        return field_hbm if step == 0 else later

    def field_of(step):
        return first if step == 0 else later

    def direct(step, piece):
        kind, b, bins, slot, places = DIRECT[piece]
        return send(
            source_of(step).at[pl.ds(b, bins)], got.at[step, kind, pl.ds(slot, bins)],
            send_sem.at[step, piece], got_sem.at[step, piece], {"bins": across(places)},
        )

    def shared(step, piece):
        _, slot, bins, new_slot = SHARED[piece]
        return send(
            got.at[step, 0, pl.ds(slot, bins)], got.at[step, 1, pl.ds(new_slot, bins)],
            send_sem.at[step, S0 + piece], got_sem.at[step, S0 + piece], {"bins": across(8)},
        )

    def leg(step, piece):
        kind, b, bins, _, way = FAR[piece]
        offset = 1 + 2 * far if kind else far - 1
        return send(
            source_of(step).at[pl.ds(b, bins)], relay.at[step, pl.ds(b, bins)],
            leg_send.at[step, piece], leg_recv.at[step, piece], at(offset, way * LEG),
        )

    def second_leg(step, piece):
        kind, b, bins, slot, way = FAR[piece]
        source_far = (height - way * LEG + around_z) % around_z // (sectors // 2)
        return send(
            relay.at[step, pl.ds(b, bins)], got.at[step, kind, pl.ds(slot, bins)],
            send_sem.at[step, F0 + piece], got_sem.at[step, F0 + piece], at(1 - source_far if kind else 0, way * LEG),
        )

    def arrival(step, piece):
        if piece < S0:
            return direct(step, piece)
        if piece < F0:
            return shared(step, piece - S0)
        return second_leg(step, piece - F0)

    def pass_on_far(step, pieces):
        for piece in pieces:
            leg(step, piece).wait_recv()
            second_leg(step, piece).start()

    def pass_on_shared(step):
        for piece, (before, *_) in enumerate(SHARED):
            direct(step, before).wait_recv()
            shared(step, piece).start()

    def halo_copy(step, group, side):
        if side == 0:
            src, dst, turn = BASE + columns - HALO, BASE - HALO, 1
        else:
            src, dst, turn = BASE, BASE + columns, -1
        ext = wide.at[step, pl.ds(group * GROUP, GROUP)]
        return send(
            ext.at[:, pl.ds(src, HALO)], ext.at[:, pl.ds(dst, HALO)],
            halo_send.at[step, side, group], halo_recv.at[step, side, group],
            {"lon": (sector + turn + sectors) % sectors},
        )

    def a_copy(step, turn):
        start = pl.multiple_of((spot + turn) % RING * chunk, chunk)
        return send(part.at[step, pl.ds(start, chunk)], part_in.at[step, turn], a_send.at[step, turn], a_recv.at[step, turn], {"bins": in_row(turn)})

    def b_copy(step, turn):
        return send(mid.at[step], mid_in.at[step, turn], b_send.at[step, turn], b_recv.at[step, turn], {"bins": in_column(turn)})

    def c_copy(step, turn):
        start = pl.multiple_of(spot * chunk, chunk)
        mine = total.at[step, pl.ds(start, chunk)]
        return send(mine, mine, c_send.at[step, turn], c_recv.at[step, turn], {"bins": in_row(turn)})

    def c_from(step, turn):
        start = pl.multiple_of((spot + RING - turn) % RING * chunk, chunk)
        theirs = total.at[step, pl.ds(start, chunk)]
        return send(theirs, theirs, c_send.at[step, turn], c_recv.at[step, turn], {"bins": in_row(turn)})

    def square(b, values):
        scaled = bins_ref[RATIO, b] * values
        return scaled * scaled

    def spread_a(step):
        for turn in range(1, RING):
            a_copy(step, turn).start()

    def spread_b(step):
        start = pl.multiple_of(spot * chunk, chunk)
        so_far = part[step, pl.ds(start, chunk)]
        for turn in range(1, RING):
            a_copy(step, turn).wait_recv()
            so_far += part_in[step, turn]
        mid[step] = so_far
        for turn in range(1, RING):
            b_copy(step, turn).start()

    def spread_c(step):
        start = pl.multiple_of(spot * chunk, chunk)
        so_far = mid[step]
        for turn in range(1, RING):
            b_copy(step, turn).wait_recv()
            so_far += mid_in[step, turn]
        total[step, pl.ds(start, chunk)] = so_far
        for turn in range(1, RING):
            c_copy(step, turn).start()

    def spread_end(step):
        for turn in range(1, RING):
            c_from(step, turn).wait_recv()

    def source(step, b):
        energy = field_of(step)[b]
        above = got[step, 0, b] * bins_ref[UPPER, b]
        below = got[step, 1, b] * bins_ref[LOWER, b]
        ratio = bins_ref[RATIO, b]
        wind = jnp.maximum(bins_ref[COS, b] * gain_x[...] + bins_ref[SIN, b] * gain_y[...], 0.0)
        quad = quad_gain * (energy * (above + below) - 2.0 * above * below)
        grown = energy + energy * (ratio * (wind + quad))
        top = jnp.where(open_sea[...] > 0.0, grown, energy)
        bottom = 1.0 + bins_ref[DAMP, b] * total[step] + ice[...]
        wide[step, b, pl.ds(BASE, columns)] = jnp.where(flags[...] == 0, 0.0, top / bottom)

    def halves(values):
        high = values.astype(jnp.bfloat16)
        return high, (values - high.astype(jnp.float32)).astype(jnp.bfloat16)

    def rates(fields, bins, signs, rows_out):
        parts = [halves(field) for field in fields]
        along_lat = jnp.dot(
            jnp.concatenate([jnp.concatenate(pair_of, axis=1) for pair_of in parts], axis=0),
            lat_taps[...], preferred_element_type=jnp.float32,
        )
        results = []
        for i, (field, pair_of, b) in enumerate(zip(fields, parts, bins)):
            along_lon = jnp.dot(
                lon_taps[signs[i], rows_out], jnp.concatenate(pair_of, axis=0), preferred_element_type=jnp.float32
            )
            start, end = i * ext + rows_out.start, i * ext + rows_out.start + rows_out.size
            east = (bins_ref[EAST, b] + bins_ref[WEST, b]) * rows_ref[0:1]
            results.append(
                field[rows_out.start : rows_out.start + rows_out.size]
                + along_lon * east
                + along_lat[start:end, :rows] * bins_ref[NORTH, b]
                + along_lat[start:end, rows:] * bins_ref[SOUTH, b]
            )
        return results

    def advance(step, group):
        bins = [group * GROUP + j for j in range(GROUP)]
        directions = [(place * here + b) // NF for b in bins]
        signs = [(d + ND // 4) // (ND // 2) % 2 for d in directions]
        every, inner = pl.ds(0, ext), pl.ds(BASE, columns)
        for j, values in enumerate(rates([wide[step, b] for b in bins], bins, signs, every)):
            one[j] = values
        for j, values in enumerate(rates([one[j] for j in range(GROUP)], bins, signs, every)):
            two[j] = 0.75 * wide[step, bins[j]] + 0.25 * values
        for j, values in enumerate(rates([two[j] for j in range(GROUP)], bins, signs, inner)):
            moved = wide[step, bins[j], inner] * (1.0 / 3.0) + (2.0 / 3.0) * values
            moved = jnp.where(flags[...] == 0, 0.0, moved)
            if step < STEPS - 1:
                later[bins[j]] = moved
                part[step + 1] += square(bins[j], moved)
            else:
                last[bins[j]] = moved

    def result_copy(group):
        some = pl.ds(group * GROUP, GROUP)
        return pltpu.make_async_copy(last.at[some], out_ref.at[some], out_sem.at[group])

    def send_group(step, group):
        for k in range(GROUPS):
            @pl.when(group == k)
            def _(k=k):
                mine = range(k * GROUP, (k + 1) * GROUP)
                for piece, (_, b, *_) in enumerate(FAR):
                    if b in mine:
                        leg(step, piece).start()
                for piece, (_, b, *_) in enumerate(DIRECT):
                    if b in mine and piece not in KEPT_BACK:
                        direct(step, piece).start()

    inputs = [(field_hbm, first), (speed_hbm, speed), (heading_hbm, heading), (flags_hbm, flags),
              (bins_hbm.at[place], bins_ref), (rows_hbm, rows_ref)]
    inputs = [pltpu.make_async_copy(src, dst, in_sem.at[i]) for i, (src, dst) in enumerate(inputs)]
    for copy in inputs:
        copy.start()

    def band(shape, along, across_it, taps):
        offset = lax.broadcasted_iota(jnp.int32, shape, along) - lax.broadcasted_iota(jnp.int32, shape, across_it)
        matrix = jnp.zeros(shape, jnp.float32)
        for j, tap in enumerate(taps):
            matrix = jnp.where(offset == j - 3, tap, matrix)
        return matrix.astype(jnp.bfloat16)

    for sign, taps in enumerate((PLUS, MINUS)):
        lon_band, lat_band = band((ext, ext), 1, 0, taps), band((rows, rows), 0, 1, taps)
        lon_taps[sign] = jnp.concatenate([lon_band, lon_band], axis=1)
        for half in range(2):
            lat_taps[pl.ds(half * rows, rows), pl.ds(sign * rows, rows)] = lat_band
    for step in range(1, STEPS):
        part[step] = jnp.zeros((columns, rows), jnp.float32)
    for copy in inputs[4:] + inputs[:1]:
        copy.wait()
    part[0] = lax.fori_loop(0, here, lambda b, so_far: so_far + square(b, first[b]), jnp.zeros((columns, rows), jnp.float32))
    pl.semaphore_wait(barrier, len(partners))

    spread_a(0)
    for piece in range(len(FAR)):
        leg(0, piece).start()
    for piece in (3, 4, 5, 6, 0):
        direct(0, piece).start()
    for copy in inputs[1:4]:
        copy.wait()
    gain = wind_gain * 0.1 * speed[...]
    gain_x[...] = gain * jnp.cos(heading[...])
    gain_y[...] = gain * jnp.sin(heading[...])
    open_sea[...] = jnp.where(flags[...] == 1, 1.0, 0.0)
    ice[...] = jnp.where(flags[...] == 2, ice_loss, 0.0)
    spread_b(0)
    direct(0, 1).start()
    pass_on_far(0, (0, 1, 2))
    spread_c(0)
    direct(0, 2).start()
    pass_on_far(0, (3, 4))
    pass_on_shared(0)
    spread_end(0)

    for step in range(STEPS):
        if step > 0:
            spread_a(step)
            direct(step, 1).start()
            pass_on_far(step, (1, 2))
            spread_b(step)
            direct(step, 2).start()
            pass_on_far(step, (3, 4))
            pass_on_shared(step)
            spread_c(step)
            pass_on_far(step, (0,))
            spread_end(step)

        @pl.loop(0, GROUPS + LAG)
        def _(g, step=step):
            @pl.when(g < GROUPS)
            def _():
                group = (g + FIRST_GROUP[step]) % GROUPS
                for k in range(GROUPS):
                    @pl.when(group == k)
                    def _(k=k):
                        for piece in NEEDS[step][k]:
                            arrival(step, piece).wait_recv()

                for j in range(GROUP):
                    source(step, group * GROUP + j)
                for side in range(2):
                    halo_copy(step, group, side).start()

            @pl.when(g >= LAG)
            def _():
                group = (g - LAG + FIRST_GROUP[step]) % GROUPS
                for side in range(2):
                    halo_copy(step, group, side).wait_recv()
                advance(step, group)
                if step < STEPS - 1:
                    send_group(step + 1, group)
                else:
                    result_copy(group).start()

    for step in range(STEPS):
        for turn in range(1, RING):
            a_copy(step, turn).wait_send()
            b_copy(step, turn).wait_send()
            c_copy(step, turn).wait_send()
        for piece in range(PIECES):
            arrival(step, piece).wait_send()
        for piece in range(len(FAR)):
            leg(step, piece).wait_send()

        @pl.loop(0, GROUPS)
        def _(group, step=step):
            for side in range(2):
                halo_copy(step, group, side).wait_send()

    @pl.loop(0, GROUPS)
    def _(group):
        result_copy(group).wait()


def shards(spectrum, wind_speed, wind_dir, flags):
    here, columns, rows = spectrum.shape
    whole = (columns, rows)
    chunk = columns // RING
    ext = columns + 2 * BASE
    hbm = pl.BlockSpec(memory_space=pl.ANY)
    dma = pltpu.SemaphoreType.DMA

    def buffer(*shape):
        return pltpu.VMEM(shape, jnp.float32)

    return pl.pallas_call(
        kernel,
        out_shape=jax.ShapeDtypeStruct(spectrum.shape, jnp.float32),
        in_specs=[hbm] * 6,
        out_specs=hbm,
        scratch_shapes=[
            buffer(here, *whole),
            buffer(here, *whole),
            buffer(here, *whole),
            buffer(STEPS, 2, here, *whole),
            buffer(STEPS, here, *whole),
            buffer(STEPS, here, ext, rows),
            buffer(GROUP, ext, rows),
            buffer(GROUP, ext, rows),
            pltpu.VMEM((2, ext, 2 * ext), jnp.bfloat16),
            pltpu.VMEM((2 * rows, 2 * rows), jnp.bfloat16),
            pltpu.SMEM((16, 128), jnp.float32),
            buffer(8, rows),
            buffer(*whole),
            buffer(*whole),
            pltpu.VMEM(whole, jnp.int32),
            buffer(*whole),
            buffer(*whole),
            buffer(*whole),
            buffer(*whole),
            buffer(STEPS, *whole),
            buffer(STEPS, RING, chunk, rows),
            buffer(STEPS, chunk, rows),
            buffer(STEPS, RING, chunk, rows),
            buffer(STEPS, *whole),
        ]
        + [dma((STEPS, PIECES))] * 2
        + [dma((STEPS, len(FAR)))] * 2
        + [dma((STEPS, 2, GROUPS))] * 2
        + [dma((STEPS, RING))] * 6
        + [dma((6,)), dma((GROUPS,))],
        compiler_params=pltpu.CompilerParams(
            collective_id=0, has_side_effects=True, vmem_limit_bytes=56 * 1024 * 1024
        ),
    )(spectrum, wind_speed, wind_dir, flags, bin_table(lax.axis_size("bins"), here), row_table(rows))


def solution(mesh):
    return jax.shard_map(
        shards,
        mesh=mesh,
        in_specs=(P("bins", "lon", None), P("lon", None), P("lon", None), P("lon", None)),
        out_specs=P("bins", "lon", None),
        check_vma=False,
    )
```

```python
import math

import jax
import jax.numpy as jnp
import numpy as np
from jax import lax
from jax.experimental import pallas as pl
from jax.experimental.pallas import tpu as pltpu
from jax.sharding import PartitionSpec as P

NF = 32
ND = 36
STEPS = 2

wind_gain = 0.5
quad_gain = 0.3
break_gain = 0.3
ice_loss = 1.0
courant = 0.6

RING = 8
HALO = 9
BASE = 16
GROUP = 3
GROUPS = 6
LAG = 2
LEG = 2
PLUS = (-2.0, 15.0, -60.0, 20.0, 30.0, -3.0, 0.0)
MINUS = (0.0, 3.0, -30.0, -20.0, 60.0, -15.0, 2.0)

DIRECT = (
    (0, 0, 3, 2, -2), (0, 3, 3, 5, -2), (0, 6, 3, 8, -2), (0, 9, 3, 11, -2), (0, 12, 3, 14, -2), (0, 15, 1, 17, -2),
    (1, 16, 2, 6, 6),
)
SHARED = ((3, 12, 2, 0), (4, 14, 3, 2), (5, 17, 1, 5))
FAR = ((0, 16, 2, 0, -1), (1, 0, 3, 8, 1), (1, 3, 3, 11, -1), (1, 6, 3, 14, 1), (1, 9, 1, 17, -1))
KEPT_BACK = (1, 2, 4, 5, 6)
KEPT_FAR = (0,)
S0, F0 = len(DIRECT), len(DIRECT) + len(SHARED)
PIECES = F0 + len(FAR)
NEEDS = (
    ((F0, 0, S0, S0 + 1), (1, S0 + 2), (2, 6, F0 + 1), (F0 + 2,), (F0 + 3,), (F0 + 4,)),
    ((F0, S0), (0, 1, S0 + 1, S0 + 2), (2, 6, F0 + 1), (F0 + 2,), (F0 + 3,), (F0 + 4,)),
)
FIRST_GROUP = (0, 1)

RATIO, COS, SIN, DAMP, UPPER, LOWER, EAST, WEST, NORTH, SOUTH = range(10)


def bin_table(places, here):
    index = np.arange(places * here).reshape(places, here)
    theta = (index // NF).astype(np.float32) * np.float32(2.0 * math.pi / ND)
    theta = theta.astype(np.float64)
    level = index % NF
    ratio = 1.05 ** (level - NF // 2.0)
    east = courant * 1.1 ** (-level.astype(np.float64)) * np.cos(theta)
    north = courant * 1.1 ** (-level.astype(np.float64)) * np.sin(theta)
    table = np.zeros((places, 16, 128), np.float32)
    values = (
        ratio,
        np.cos(theta),
        np.sin(theta),
        break_gain * ratio * ratio / (NF * ND),
        level + 2 < NF,
        level >= 2,
        np.maximum(east, 0.0) / -60.0,
        np.minimum(east, 0.0) / -60.0,
        np.maximum(north, 0.0) / -60.0,
        np.minimum(north, 0.0) / -60.0,
    )
    for quantity, value in enumerate(values):
        table[:, quantity, :here] = value
    return table


def row_table(rows):
    lines = np.arange(rows)
    coslat = np.cos((lines - rows / 2 + 0.5) * (0.25 * math.pi / 180.0))
    return np.broadcast_to(1.0 / coslat, (8, rows)).astype(np.float32)


def kernel(
    field_hbm, speed_hbm, heading_hbm, flags_hbm, bins_hbm, rows_hbm, out_ref,
    first, later, last, got, relay, wide, one, two, lon_taps, lat_taps, bins_ref, rows_ref, speed, heading, flags, gain_x, gain_y, open_sea, ice,
    part, part_in, mid, mid_in, total,
    send_sem, got_sem, leg_send, leg_recv, halo_send, halo_recv,
    a_send, a_recv, b_send, b_recv, c_send, c_recv, in_sem, out_sem,
):
    here, columns, rows = field_hbm.shape
    count, sectors = lax.axis_size("bins"), lax.axis_size("lon")
    place, sector = lax.axis_index("bins"), lax.axis_index("lon")
    ext = columns + 2 * BASE
    line, spot = place // RING, place % RING
    chunk = columns // RING
    def in_row(turn):
        return line * RING + (spot + turn) % RING

    def in_column(turn):
        return (line + turn) % RING * RING + spot

    def across(offset):
        return (place + offset + count) % count

    pair, far, core = place // 2, place % 2, sector % 2
    height = far * (sectors // 2) + sector // 2
    around_z = sectors

    def at(pair_offset, climb):
        new = (height + climb + around_z) % around_z
        new_pair = (pair + pair_offset + count // 2) % (count // 2)
        return {"bins": new_pair * 2 + new // (sectors // 2), "lon": new % (sectors // 2) * 2 + core}

    for step in range(STEPS):
        for rows_of in (pl.ds(0, BASE), pl.ds(BASE + columns, BASE)):
            wide[step, :, rows_of] = jnp.zeros((here, BASE, rows), jnp.float32)

    barrier = pltpu.get_barrier_semaphore()
    partners = [{"bins": across(s * o)} for o in (2, 6, 8) for s in (1, -1)]
    partners += [at(o, s * LEG) for o in (-3, -1, 0, 1, 3) for s in (1, -1)]
    partners += [{"bins": in_row(t)} for t in range(1, RING)]
    partners += [{"bins": in_column(t)} for t in range(1, RING)]
    partners += [{"lon": (sector + s + sectors) % sectors} for s in (1, -1)]
    for partner in partners:
        pl.semaphore_signal(barrier, inc=1, device_id=partner, device_id_type=pl.DeviceIdType.MESH)

    def send(src, dst, send_sem, recv_sem, device):
        return pltpu.make_async_remote_copy(
            src_ref=src, dst_ref=dst, send_sem=send_sem, recv_sem=recv_sem,
            device_id=device, device_id_type=pl.DeviceIdType.MESH,
        )

    def source_of(step):
        return field_hbm if step == 0 else later

    def field_of(step):
        return first if step == 0 else later

    def direct(step, piece):
        kind, b, bins, slot, places = DIRECT[piece]
        return send(
            source_of(step).at[pl.ds(b, bins)], got.at[step, kind, pl.ds(slot, bins)],
            send_sem.at[step, piece], got_sem.at[step, piece], {"bins": across(places)},
        )

    def shared(step, piece):
        _, slot, bins, new_slot = SHARED[piece]
        return send(
            got.at[step, 0, pl.ds(slot, bins)], got.at[step, 1, pl.ds(new_slot, bins)],
            send_sem.at[step, S0 + piece], got_sem.at[step, S0 + piece], {"bins": across(8)},
        )

    def leg(step, piece):
        kind, b, bins, _, way = FAR[piece]
        offset = 1 + 2 * far if kind else far - 1
        return send(
            source_of(step).at[pl.ds(b, bins)], relay.at[step, pl.ds(b, bins)],
            leg_send.at[step, piece], leg_recv.at[step, piece], at(offset, way * LEG),
        )

    def second_leg(step, piece):
        kind, b, bins, slot, way = FAR[piece]
        source_far = (height - way * LEG + around_z) % around_z // (sectors // 2)
        return send(
            relay.at[step, pl.ds(b, bins)], got.at[step, kind, pl.ds(slot, bins)],
            send_sem.at[step, F0 + piece], got_sem.at[step, F0 + piece], at(1 - source_far if kind else 0, way * LEG),
        )

    def arrival(step, piece):
        if piece < S0:
            return direct(step, piece)
        if piece < F0:
            return shared(step, piece - S0)
        return second_leg(step, piece - F0)

    def pass_on_far(step, pieces):
        for piece in pieces:
            leg(step, piece).wait_recv()
            second_leg(step, piece).start()

    def pass_on_shared(step):
        for piece, (before, *_) in enumerate(SHARED):
            direct(step, before).wait_recv()
            shared(step, piece).start()

    def halo_copy(step, group, side):
        if side == 0:
            src, dst, turn = BASE + columns - HALO, BASE - HALO, 1
        else:
            src, dst, turn = BASE, BASE + columns, -1
        ext = wide.at[step, pl.ds(group * GROUP, GROUP)]
        return send(
            ext.at[:, pl.ds(src, HALO)], ext.at[:, pl.ds(dst, HALO)],
            halo_send.at[step, side, group], halo_recv.at[step, side, group],
            {"lon": (sector + turn + sectors) % sectors},
        )

    def a_copy(step, turn):
        start = pl.multiple_of((spot + turn) % RING * chunk, chunk)
        return send(part.at[step, pl.ds(start, chunk)], part_in.at[step, turn], a_send.at[step, turn], a_recv.at[step, turn], {"bins": in_row(turn)})

    def b_copy(step, turn):
        return send(mid.at[step], mid_in.at[step, turn], b_send.at[step, turn], b_recv.at[step, turn], {"bins": in_column(turn)})

    def c_copy(step, turn):
        start = pl.multiple_of(spot * chunk, chunk)
        mine = total.at[step, pl.ds(start, chunk)]
        return send(mine, mine, c_send.at[step, turn], c_recv.at[step, turn], {"bins": in_row(turn)})

    def c_from(step, turn):
        start = pl.multiple_of((spot + RING - turn) % RING * chunk, chunk)
        theirs = total.at[step, pl.ds(start, chunk)]
        return send(theirs, theirs, c_send.at[step, turn], c_recv.at[step, turn], {"bins": in_row(turn)})

    def square(b, values):
        scaled = bins_ref[RATIO, b] * values
        return scaled * scaled

    def spread_a(step):
        for turn in range(1, RING):
            a_copy(step, turn).start()

    def spread_b(step):
        start = pl.multiple_of(spot * chunk, chunk)
        so_far = part[step, pl.ds(start, chunk)]
        for turn in range(1, RING):
            a_copy(step, turn).wait_recv()
            so_far += part_in[step, turn]
        mid[step] = so_far
        for turn in range(1, RING):
            b_copy(step, turn).start()

    def spread_c(step):
        start = pl.multiple_of(spot * chunk, chunk)
        so_far = mid[step]
        for turn in range(1, RING):
            b_copy(step, turn).wait_recv()
            so_far += mid_in[step, turn]
        total[step, pl.ds(start, chunk)] = so_far
        for turn in range(1, RING):
            c_copy(step, turn).start()

    def spread_end(step):
        for turn in range(1, RING):
            c_from(step, turn).wait_recv()

    def source(step, b):
        energy = field_of(step)[b]
        above = got[step, 0, b] * bins_ref[UPPER, b]
        below = got[step, 1, b] * bins_ref[LOWER, b]
        ratio = bins_ref[RATIO, b]
        wind = jnp.maximum(bins_ref[COS, b] * gain_x[...] + bins_ref[SIN, b] * gain_y[...], 0.0)
        quad = quad_gain * (energy * (above + below) - 2.0 * above * below)
        grown = energy + energy * (ratio * (wind + quad))
        top = jnp.where(open_sea[...] > 0.0, grown, energy)
        bottom = 1.0 + bins_ref[DAMP, b] * total[step] + ice[...]
        wide[step, b, pl.ds(BASE, columns)] = jnp.where(flags[...] == 0, 0.0, top / bottom)

    def halves(values):
        high = values.astype(jnp.bfloat16)
        return high, (values - high.astype(jnp.float32)).astype(jnp.bfloat16)

    def rates(fields, bins, signs, rows_out):
        parts = [halves(field) for field in fields]
        along_lat = jnp.dot(
            jnp.concatenate([jnp.concatenate(pair_of, axis=1) for pair_of in parts], axis=0),
            lat_taps[...], preferred_element_type=jnp.float32,
        )
        results = []
        for i, (field, pair_of, b) in enumerate(zip(fields, parts, bins)):
            along_lon = jnp.dot(
                lon_taps[signs[i], rows_out], jnp.concatenate(pair_of, axis=0), preferred_element_type=jnp.float32
            )
            start, end = i * ext + rows_out.start, i * ext + rows_out.start + rows_out.size
            east = (bins_ref[EAST, b] + bins_ref[WEST, b]) * rows_ref[0:1]
            results.append(
                field[rows_out.start : rows_out.start + rows_out.size]
                + along_lon * east
                + along_lat[start:end, :rows] * bins_ref[NORTH, b]
                + along_lat[start:end, rows:] * bins_ref[SOUTH, b]
            )
        return results

    def advance(step, group):
        bins = [group * GROUP + j for j in range(GROUP)]
        directions = [(place * here + b) // NF for b in bins]
        signs = [(d + ND // 4) // (ND // 2) % 2 for d in directions]
        every, inner = pl.ds(0, ext), pl.ds(BASE, columns)
        for j, values in enumerate(rates([wide[step, b] for b in bins], bins, signs, every)):
            one[j] = values
        for j, values in enumerate(rates([one[j] for j in range(GROUP)], bins, signs, every)):
            two[j] = 0.75 * wide[step, bins[j]] + 0.25 * values
        for j, values in enumerate(rates([two[j] for j in range(GROUP)], bins, signs, inner)):
            moved = wide[step, bins[j], inner] * (1.0 / 3.0) + (2.0 / 3.0) * values
            moved = jnp.where(flags[...] == 0, 0.0, moved)
            if step < STEPS - 1:
                later[bins[j]] = moved
                part[step + 1] += square(bins[j], moved)
            else:
                last[bins[j]] = moved

    def result_copy(group):
        some = pl.ds(group * GROUP, GROUP)
        return pltpu.make_async_copy(last.at[some], out_ref.at[some], out_sem.at[group])

    def send_group(step, group):
        for k in range(GROUPS):
            @pl.when(group == k)
            def _(k=k):
                mine = range(k * GROUP, (k + 1) * GROUP)
                for piece, (_, b, *_) in enumerate(FAR):
                    if b in mine and piece not in KEPT_FAR:
                        leg(step, piece).start()
                for piece, (_, b, *_) in enumerate(DIRECT):
                    if b in mine and piece not in KEPT_BACK:
                        direct(step, piece).start()

    inputs = [(field_hbm, first), (speed_hbm, speed), (heading_hbm, heading), (flags_hbm, flags),
              (bins_hbm.at[place], bins_ref), (rows_hbm, rows_ref)]
    inputs = [pltpu.make_async_copy(src, dst, in_sem.at[i]) for i, (src, dst) in enumerate(inputs)]
    for copy in inputs:
        copy.start()

    def band(shape, along, across_it, taps):
        offset = lax.broadcasted_iota(jnp.int32, shape, along) - lax.broadcasted_iota(jnp.int32, shape, across_it)
        matrix = jnp.zeros(shape, jnp.float32)
        for j, tap in enumerate(taps):
            matrix = jnp.where(offset == j - 3, tap, matrix)
        return matrix.astype(jnp.bfloat16)

    for sign, taps in enumerate((PLUS, MINUS)):
        lon_band, lat_band = band((ext, ext), 1, 0, taps), band((rows, rows), 0, 1, taps)
        lon_taps[sign] = jnp.concatenate([lon_band, lon_band], axis=1)
        for half in range(2):
            lat_taps[pl.ds(half * rows, rows), pl.ds(sign * rows, rows)] = lat_band
    for step in range(1, STEPS):
        part[step] = jnp.zeros((columns, rows), jnp.float32)
    for copy in inputs[4:] + inputs[:1]:
        copy.wait()
    part[0] = lax.fori_loop(0, here, lambda b, so_far: so_far + square(b, first[b]), jnp.zeros((columns, rows), jnp.float32))
    pl.semaphore_wait(barrier, len(partners))

    spread_a(0)
    for piece in range(len(FAR)):
        leg(0, piece).start()
    direct(0, 3).start()
    for copy in inputs[1:4]:
        copy.wait()
    gain = wind_gain * 0.1 * speed[...]
    gain_x[...] = gain * jnp.cos(heading[...])
    gain_y[...] = gain * jnp.sin(heading[...])
    open_sea[...] = jnp.where(flags[...] == 1, 1.0, 0.0)
    ice[...] = jnp.where(flags[...] == 2, ice_loss, 0.0)
    spread_b(0)
    for piece in (4, 5, 0, 6, 1):
        direct(0, piece).start()
    pass_on_far(0, (0, 1, 2))
    spread_c(0)
    direct(0, 2).start()
    pass_on_far(0, (3, 4))
    pass_on_shared(0)
    spread_end(0)

    for step in range(STEPS):
        if step > 0:
            spread_a(step)
            leg(step, 0).start()
            for piece in (4, 5, 6, 1):
                direct(step, piece).start()
            pass_on_far(step, (1, 2))
            spread_b(step)
            direct(step, 2).start()
            pass_on_far(step, (3, 4))
            pass_on_shared(step)
            spread_c(step)
            pass_on_far(step, (0,))
            spread_end(step)

        @pl.loop(0, GROUPS + LAG)
        def _(g, step=step):
            @pl.when(g < GROUPS)
            def _():
                group = (g + FIRST_GROUP[step]) % GROUPS
                for k in range(GROUPS):
                    @pl.when(group == k)
                    def _(k=k):
                        for piece in NEEDS[step][k]:
                            arrival(step, piece).wait_recv()

                for j in range(GROUP):
                    source(step, group * GROUP + j)
                for side in range(2):
                    halo_copy(step, group, side).start()

            @pl.when(g >= LAG)
            def _():
                group = (g - LAG + FIRST_GROUP[step]) % GROUPS
                for side in range(2):
                    halo_copy(step, group, side).wait_recv()
                advance(step, group)
                if step < STEPS - 1:
                    send_group(step + 1, group)
                else:
                    result_copy(group).start()

    for step in range(STEPS):
        for turn in range(1, RING):
            a_copy(step, turn).wait_send()
            b_copy(step, turn).wait_send()
            c_copy(step, turn).wait_send()
        for piece in range(PIECES):
            arrival(step, piece).wait_send()
        for piece in range(len(FAR)):
            leg(step, piece).wait_send()

        @pl.loop(0, GROUPS)
        def _(group, step=step):
            for side in range(2):
                halo_copy(step, group, side).wait_send()

    @pl.loop(0, GROUPS)
    def _(group):
        result_copy(group).wait()


def shards(spectrum, wind_speed, wind_dir, flags):
    here, columns, rows = spectrum.shape
    whole = (columns, rows)
    chunk = columns // RING
    ext = columns + 2 * BASE
    hbm = pl.BlockSpec(memory_space=pl.ANY)
    dma = pltpu.SemaphoreType.DMA

    def buffer(*shape):
        return pltpu.VMEM(shape, jnp.float32)

    return pl.pallas_call(
        kernel,
        out_shape=jax.ShapeDtypeStruct(spectrum.shape, jnp.float32),
        in_specs=[hbm] * 6,
        out_specs=hbm,
        scratch_shapes=[
            buffer(here, *whole),
            buffer(here, *whole),
            buffer(here, *whole),
            buffer(STEPS, 2, here, *whole),
            buffer(STEPS, here, *whole),
            buffer(STEPS, here, ext, rows),
            buffer(GROUP, ext, rows),
            buffer(GROUP, ext, rows),
            pltpu.VMEM((2, ext, 2 * ext), jnp.bfloat16),
            pltpu.VMEM((2 * rows, 2 * rows), jnp.bfloat16),
            pltpu.SMEM((16, 128), jnp.float32),
            buffer(8, rows),
            buffer(*whole),
            buffer(*whole),
            pltpu.VMEM(whole, jnp.int32),
            buffer(*whole),
            buffer(*whole),
            buffer(*whole),
            buffer(*whole),
            buffer(STEPS, *whole),
            buffer(STEPS, RING, chunk, rows),
            buffer(STEPS, chunk, rows),
            buffer(STEPS, RING, chunk, rows),
            buffer(STEPS, *whole),
        ]
        + [dma((STEPS, PIECES))] * 2
        + [dma((STEPS, len(FAR)))] * 2
        + [dma((STEPS, 2, GROUPS))] * 2
        + [dma((STEPS, RING))] * 6
        + [dma((6,)), dma((GROUPS,))],
        compiler_params=pltpu.CompilerParams(
            collective_id=0, has_side_effects=True, vmem_limit_bytes=56 * 1024 * 1024
        ),
    )(spectrum, wind_speed, wind_dir, flags, bin_table(lax.axis_size("bins"), here), row_table(rows))


def solution(mesh):
    return jax.shard_map(
        shards,
        mesh=mesh,
        in_specs=(P("bins", "lon", None), P("lon", None), P("lon", None), P("lon", None)),
        out_specs=P("bins", "lon", None),
        check_vma=False,
    )
```

```python
import math

import jax
import jax.numpy as jnp
import numpy as np
from jax import lax
from jax.experimental import pallas as pl
from jax.experimental.pallas import tpu as pltpu
from jax.sharding import PartitionSpec as P

NF = 32
ND = 36
STEPS = 2

wind_gain = 0.5
quad_gain = 0.3
break_gain = 0.3
ice_loss = 1.0
courant = 0.6

RING = 8
HALO = 9
BASE = 16
GROUP = 3
GROUPS = 6
LAG = 2
LEG = 2
PLUS = (-2.0, 15.0, -60.0, 20.0, 30.0, -3.0, 0.0)
MINUS = (0.0, 3.0, -30.0, -20.0, 60.0, -15.0, 2.0)

DIRECT = (
    (0, 0, 3, 2, -2), (0, 3, 3, 5, -2), (0, 6, 3, 8, -2), (0, 9, 3, 11, -2), (0, 12, 3, 14, -2), (0, 15, 1, 17, -2),
    (1, 16, 2, 6, 6),
)
SHARED = ((3, 12, 2, 0), (4, 14, 3, 2), (5, 17, 1, 5))
FAR = ((0, 16, 2, 0, -1), (1, 0, 3, 8, 1), (1, 3, 3, 11, -1), (1, 6, 3, 14, 1), (1, 9, 1, 17, -1))
KEPT_BACK = (1, 2, 4, 5, 6)
KEPT_FAR = (0,)
S0, F0 = len(DIRECT), len(DIRECT) + len(SHARED)
PIECES = F0 + len(FAR)
NEEDS = (
    ((F0, 0, S0, S0 + 1), (1, S0 + 2), (2, 6, F0 + 1), (F0 + 2,), (F0 + 3,), (F0 + 4,)),
    ((F0, S0), (0, 1, S0 + 1, S0 + 2), (2, 6, F0 + 1), (F0 + 2,), (F0 + 3,), (F0 + 4,)),
)

RATIO, COS, SIN, DAMP, UPPER, LOWER, EAST, WEST, NORTH, SOUTH = range(10)


def bin_table(places, here):
    index = np.arange(places * here).reshape(places, here)
    theta = (index // NF).astype(np.float32) * np.float32(2.0 * math.pi / ND)
    theta = theta.astype(np.float64)
    level = index % NF
    ratio = 1.05 ** (level - NF // 2.0)
    east = courant * 1.1 ** (-level.astype(np.float64)) * np.cos(theta)
    north = courant * 1.1 ** (-level.astype(np.float64)) * np.sin(theta)
    table = np.zeros((places, 16, 128), np.float32)
    values = (
        ratio,
        np.cos(theta),
        np.sin(theta),
        break_gain * ratio * ratio / (NF * ND),
        level + 2 < NF,
        level >= 2,
        np.maximum(east, 0.0) / -60.0,
        np.minimum(east, 0.0) / -60.0,
        np.maximum(north, 0.0) / -60.0,
        np.minimum(north, 0.0) / -60.0,
    )
    for quantity, value in enumerate(values):
        table[:, quantity, :here] = value
    return table


def row_table(rows):
    lines = np.arange(rows)
    coslat = np.cos((lines - rows / 2 + 0.5) * (0.25 * math.pi / 180.0))
    return np.broadcast_to(1.0 / coslat, (8, rows)).astype(np.float32)


def kernel(
    field_hbm, speed_hbm, heading_hbm, flags_hbm, bins_hbm, rows_hbm, out_ref,
    first, later, last, got, relay, wide, one, two, lon_taps, lat_taps, bins_ref, rows_ref, speed, heading, flags, gain_x, gain_y, open_sea, ice,
    part, part_in, mid, mid_in, total,
    send_sem, got_sem, leg_send, leg_recv, halo_send, halo_recv,
    a_send, a_recv, b_send, b_recv, c_send, c_recv, in_sem, out_sem,
):
    here, columns, rows = field_hbm.shape
    count, sectors = lax.axis_size("bins"), lax.axis_size("lon")
    place, sector = lax.axis_index("bins"), lax.axis_index("lon")
    ext = columns + 2 * BASE
    line, spot = place // RING, place % RING
    chunk = columns // RING
    def in_row(turn):
        return line * RING + (spot + turn) % RING

    def in_column(turn):
        return (line + turn) % RING * RING + spot

    def across(offset):
        return (place + offset + count) % count

    pair, far, core = place // 2, place % 2, sector % 2
    height = far * (sectors // 2) + sector // 2
    around_z = sectors

    def at(pair_offset, climb):
        new = (height + climb + around_z) % around_z
        new_pair = (pair + pair_offset + count // 2) % (count // 2)
        return {"bins": new_pair * 2 + new // (sectors // 2), "lon": new % (sectors // 2) * 2 + core}

    for step in range(STEPS):
        for rows_of in (pl.ds(0, BASE), pl.ds(BASE + columns, BASE)):
            wide[step, :, rows_of] = jnp.zeros((here, BASE, rows), jnp.float32)

    barrier = pltpu.get_barrier_semaphore()
    partners = [{"bins": across(s * o)} for o in (2, 6, 8) for s in (1, -1)]
    partners += [at(o, s * LEG) for o in (-3, -1, 0, 1, 3) for s in (1, -1)]
    partners += [{"bins": in_row(t)} for t in range(1, RING)]
    partners += [{"bins": in_column(t)} for t in range(1, RING)]
    partners += [{"lon": (sector + s + sectors) % sectors} for s in (1, -1)]
    for partner in partners:
        pl.semaphore_signal(barrier, inc=1, device_id=partner, device_id_type=pl.DeviceIdType.MESH)

    def send(src, dst, send_sem, recv_sem, device):
        return pltpu.make_async_remote_copy(
            src_ref=src, dst_ref=dst, send_sem=send_sem, recv_sem=recv_sem,
            device_id=device, device_id_type=pl.DeviceIdType.MESH,
        )

    def source_of(step):
        return field_hbm if step == 0 else later

    def field_of(step):
        return first if step == 0 else later

    def direct(step, piece):
        kind, b, bins, slot, places = DIRECT[piece]
        return send(
            source_of(step).at[pl.ds(b, bins)], got.at[step, kind, pl.ds(slot, bins)],
            send_sem.at[step, piece], got_sem.at[step, piece], {"bins": across(places)},
        )

    def shared(step, piece):
        _, slot, bins, new_slot = SHARED[piece]
        return send(
            got.at[step, 0, pl.ds(slot, bins)], got.at[step, 1, pl.ds(new_slot, bins)],
            send_sem.at[step, S0 + piece], got_sem.at[step, S0 + piece], {"bins": across(8)},
        )

    def leg(step, piece):
        kind, b, bins, _, way = FAR[piece]
        offset = 1 + 2 * far if kind else far - 1
        return send(
            source_of(step).at[pl.ds(b, bins)], relay.at[step, pl.ds(b, bins)],
            leg_send.at[step, piece], leg_recv.at[step, piece], at(offset, way * LEG),
        )

    def second_leg(step, piece):
        kind, b, bins, slot, way = FAR[piece]
        source_far = (height - way * LEG + around_z) % around_z // (sectors // 2)
        return send(
            relay.at[step, pl.ds(b, bins)], got.at[step, kind, pl.ds(slot, bins)],
            send_sem.at[step, F0 + piece], got_sem.at[step, F0 + piece], at(1 - source_far if kind else 0, way * LEG),
        )

    def arrival(step, piece):
        if piece < S0:
            return direct(step, piece)
        if piece < F0:
            return shared(step, piece - S0)
        return second_leg(step, piece - F0)

    def pass_on_far(step, pieces):
        for piece in pieces:
            leg(step, piece).wait_recv()
            second_leg(step, piece).start()

    def pass_on_shared(step):
        for piece, (before, *_) in enumerate(SHARED):
            direct(step, before).wait_recv()
            shared(step, piece).start()

    def halo_copy(step, group, side):
        if side == 0:
            src, dst, turn = BASE + columns - HALO, BASE - HALO, 1
        else:
            src, dst, turn = BASE, BASE + columns, -1
        ext = wide.at[step, pl.ds(group * GROUP, GROUP)]
        return send(
            ext.at[:, pl.ds(src, HALO)], ext.at[:, pl.ds(dst, HALO)],
            halo_send.at[step, side, group], halo_recv.at[step, side, group],
            {"lon": (sector + turn + sectors) % sectors},
        )

    def a_copy(step, turn):
        start = pl.multiple_of((spot + turn) % RING * chunk, chunk)
        return send(part.at[step, pl.ds(start, chunk)], part_in.at[step, turn], a_send.at[step, turn], a_recv.at[step, turn], {"bins": in_row(turn)})

    def b_copy(step, turn):
        return send(mid.at[step], mid_in.at[step, turn], b_send.at[step, turn], b_recv.at[step, turn], {"bins": in_column(turn)})

    def c_copy(step, turn):
        start = pl.multiple_of(spot * chunk, chunk)
        mine = total.at[step, pl.ds(start, chunk)]
        return send(mine, mine, c_send.at[step, turn], c_recv.at[step, turn], {"bins": in_row(turn)})

    def c_from(step, turn):
        start = pl.multiple_of((spot + RING - turn) % RING * chunk, chunk)
        theirs = total.at[step, pl.ds(start, chunk)]
        return send(theirs, theirs, c_send.at[step, turn], c_recv.at[step, turn], {"bins": in_row(turn)})

    def square(b, values):
        scaled = bins_ref[RATIO, b] * values
        return scaled * scaled

    def spread_a(step):
        for turn in range(1, RING):
            a_copy(step, turn).start()

    def spread_b(step):
        start = pl.multiple_of(spot * chunk, chunk)
        so_far = part[step, pl.ds(start, chunk)]
        for turn in range(1, RING):
            a_copy(step, turn).wait_recv()
            so_far += part_in[step, turn]
        mid[step] = so_far
        for turn in range(1, RING):
            b_copy(step, turn).start()

    def spread_c(step):
        start = pl.multiple_of(spot * chunk, chunk)
        so_far = mid[step]
        for turn in range(1, RING):
            b_copy(step, turn).wait_recv()
            so_far += mid_in[step, turn]
        total[step, pl.ds(start, chunk)] = so_far
        for turn in range(1, RING):
            c_copy(step, turn).start()

    def spread_end(step):
        for turn in range(1, RING):
            c_from(step, turn).wait_recv()

    def source(step, b):
        energy = field_of(step)[b]
        above = got[step, 0, b] * bins_ref[UPPER, b]
        below = got[step, 1, b] * bins_ref[LOWER, b]
        ratio = bins_ref[RATIO, b]
        wind = jnp.maximum(bins_ref[COS, b] * gain_x[...] + bins_ref[SIN, b] * gain_y[...], 0.0)
        quad = quad_gain * (energy * (above + below) - 2.0 * above * below)
        grown = energy + energy * (ratio * (wind + quad))
        top = jnp.where(open_sea[...] > 0.0, grown, energy)
        bottom = 1.0 + bins_ref[DAMP, b] * total[step] + ice[...]
        wide[step, b, pl.ds(BASE, columns)] = jnp.where(flags[...] == 0, 0.0, top / bottom)

    def halves(values):
        high = values.astype(jnp.bfloat16)
        return high, (values - high.astype(jnp.float32)).astype(jnp.bfloat16)

    def rates(fields, bins, signs, rows_out):
        parts = [halves(field) for field in fields]
        along_lat = jnp.dot(
            jnp.concatenate([jnp.concatenate(pair_of, axis=1) for pair_of in parts], axis=0),
            lat_taps[...], preferred_element_type=jnp.float32,
        )
        results = []
        for i, (field, pair_of, b) in enumerate(zip(fields, parts, bins)):
            along_lon = jnp.dot(
                lon_taps[signs[i], rows_out], jnp.concatenate(pair_of, axis=0), preferred_element_type=jnp.float32
            )
            start, end = i * ext + rows_out.start, i * ext + rows_out.start + rows_out.size
            east = (bins_ref[EAST, b] + bins_ref[WEST, b]) * rows_ref[0:1]
            results.append(
                field[rows_out.start : rows_out.start + rows_out.size]
                + along_lon * east
                + along_lat[start:end, :rows] * bins_ref[NORTH, b]
                + along_lat[start:end, rows:] * bins_ref[SOUTH, b]
            )
        return results

    def advance(step, groups_now):
        bins = [group * GROUP + j for group in groups_now for j in range(GROUP)]
        directions = [(place * here + b) // NF for b in bins]
        signs = [(d + ND // 4) // (ND // 2) % 2 for d in directions]
        every, inner = pl.ds(0, ext), pl.ds(BASE, columns)
        for j, values in enumerate(rates([wide[step, b] for b in bins], bins, signs, every)):
            one[j] = values
        for j, values in enumerate(rates([one[j] for j in range(len(bins))], bins, signs, every)):
            two[j] = 0.75 * wide[step, bins[j]] + 0.25 * values
        for j, values in enumerate(rates([two[j] for j in range(len(bins))], bins, signs, inner)):
            moved = wide[step, bins[j], inner] * (1.0 / 3.0) + (2.0 / 3.0) * values
            moved = jnp.where(flags[...] == 0, 0.0, moved)
            if step < STEPS - 1:
                later[bins[j]] = moved
                part[step + 1] += square(bins[j], moved)
            else:
                last[bins[j]] = moved

    def result_copy(group):
        some = pl.ds(group * GROUP, GROUP)
        return pltpu.make_async_copy(last.at[some], out_ref.at[some], out_sem.at[group])

    def send_group(step, group):
        for k in range(GROUPS):
            @pl.when(group == k)
            def _(k=k):
                mine = range(k * GROUP, (k + 1) * GROUP)
                for piece, (_, b, *_) in enumerate(FAR):
                    if b in mine and piece not in KEPT_FAR:
                        leg(step, piece).start()
                for piece, (_, b, *_) in enumerate(DIRECT):
                    if b in mine and piece not in KEPT_BACK:
                        direct(step, piece).start()

    inputs = [(field_hbm, first), (speed_hbm, speed), (heading_hbm, heading), (flags_hbm, flags),
              (bins_hbm.at[place], bins_ref), (rows_hbm, rows_ref)]
    inputs = [pltpu.make_async_copy(src, dst, in_sem.at[i]) for i, (src, dst) in enumerate(inputs)]
    for copy in inputs:
        copy.start()

    def band(shape, along, across_it, taps):
        offset = lax.broadcasted_iota(jnp.int32, shape, along) - lax.broadcasted_iota(jnp.int32, shape, across_it)
        matrix = jnp.zeros(shape, jnp.float32)
        for j, tap in enumerate(taps):
            matrix = jnp.where(offset == j - 3, tap, matrix)
        return matrix.astype(jnp.bfloat16)

    for sign, taps in enumerate((PLUS, MINUS)):
        lon_band, lat_band = band((ext, ext), 1, 0, taps), band((rows, rows), 0, 1, taps)
        lon_taps[sign] = jnp.concatenate([lon_band, lon_band], axis=1)
        for half in range(2):
            lat_taps[pl.ds(half * rows, rows), pl.ds(sign * rows, rows)] = lat_band
    for step in range(1, STEPS):
        part[step] = jnp.zeros((columns, rows), jnp.float32)
    for copy in inputs[4:] + inputs[:1]:
        copy.wait()
    part[0] = lax.fori_loop(0, here, lambda b, so_far: so_far + square(b, first[b]), jnp.zeros((columns, rows), jnp.float32))
    pl.semaphore_wait(barrier, len(partners))

    spread_a(0)
    for piece in range(len(FAR)):
        leg(0, piece).start()
    direct(0, 3).start()
    for copy in inputs[1:4]:
        copy.wait()
    gain = wind_gain * 0.1 * speed[...]
    gain_x[...] = gain * jnp.cos(heading[...])
    gain_y[...] = gain * jnp.sin(heading[...])
    open_sea[...] = jnp.where(flags[...] == 1, 1.0, 0.0)
    ice[...] = jnp.where(flags[...] == 2, ice_loss, 0.0)
    spread_b(0)
    for piece in (4, 5, 0, 6, 1):
        direct(0, piece).start()
    pass_on_far(0, (0, 1, 2))
    spread_c(0)
    direct(0, 2).start()
    pass_on_far(0, (3, 4))
    pass_on_shared(0)
    spread_end(0)

    def source_group(step, group):
        for k in range(GROUPS):
            @pl.when(group == k)
            def _(k=k):
                for piece in NEEDS[step][k]:
                    arrival(step, piece).wait_recv()

        for j in range(GROUP):
            source(step, group * GROUP + j)
        for side in range(2):
            halo_copy(step, group, side).start()

    def halos_there(step, group):
        for side in range(2):
            halo_copy(step, group, side).wait_recv()

    @pl.loop(0, GROUPS + LAG)
    def _(g):
        @pl.when(g >= LAG)
        def _():
            group = g - LAG
            halos_there(0, group)
            advance(0, (group,))
            send_group(1, group)

        @pl.when(g < GROUPS)
        def _():
            source_group(0, g)

    spread_a(1)
    leg(1, 0).start()
    for piece in (4, 5, 6, 1):
        direct(1, piece).start()
    pass_on_far(1, (1, 2))
    spread_b(1)
    direct(1, 2).start()
    pass_on_far(1, (3, 4))
    pass_on_shared(1)
    spread_c(1)
    pass_on_far(1, (0,))
    spread_end(1)


    @pl.loop(0, GROUPS // 2 + 1)
    def _(g):
        @pl.when(g < GROUPS // 2)
        def _():
            for j in range(2):
                source_group(1, (2 * g + j + 1) % GROUPS)

        @pl.when(g >= 1)
        def _():
            pair_now = [(2 * g + j - 1) % GROUPS for j in range(2)]
            for group in pair_now:
                halos_there(1, group)
            advance(1, pair_now)
            for group in pair_now:
                result_copy(group).start()

    for step in range(STEPS):
        for turn in range(1, RING):
            a_copy(step, turn).wait_send()
            b_copy(step, turn).wait_send()
            c_copy(step, turn).wait_send()
        for piece in range(PIECES):
            arrival(step, piece).wait_send()
        for piece in range(len(FAR)):
            leg(step, piece).wait_send()

        @pl.loop(0, GROUPS)
        def _(group, step=step):
            for side in range(2):
                halo_copy(step, group, side).wait_send()

    @pl.loop(0, GROUPS)
    def _(group):
        result_copy(group).wait()


def shards(spectrum, wind_speed, wind_dir, flags):
    here, columns, rows = spectrum.shape
    whole = (columns, rows)
    chunk = columns // RING
    ext = columns + 2 * BASE
    hbm = pl.BlockSpec(memory_space=pl.ANY)
    dma = pltpu.SemaphoreType.DMA

    def buffer(*shape):
        return pltpu.VMEM(shape, jnp.float32)

    return pl.pallas_call(
        kernel,
        out_shape=jax.ShapeDtypeStruct(spectrum.shape, jnp.float32),
        in_specs=[hbm] * 6,
        out_specs=hbm,
        scratch_shapes=[
            buffer(here, *whole),
            buffer(here, *whole),
            buffer(here, *whole),
            buffer(STEPS, 2, here, *whole),
            buffer(STEPS, here, *whole),
            buffer(STEPS, here, ext, rows),
            buffer(2 * GROUP, ext, rows),
            buffer(2 * GROUP, ext, rows),
            pltpu.VMEM((2, ext, 2 * ext), jnp.bfloat16),
            pltpu.VMEM((2 * rows, 2 * rows), jnp.bfloat16),
            pltpu.SMEM((16, 128), jnp.float32),
            buffer(8, rows),
            buffer(*whole),
            buffer(*whole),
            pltpu.VMEM(whole, jnp.int32),
            buffer(*whole),
            buffer(*whole),
            buffer(*whole),
            buffer(*whole),
            buffer(STEPS, *whole),
            buffer(STEPS, RING, chunk, rows),
            buffer(STEPS, chunk, rows),
            buffer(STEPS, RING, chunk, rows),
            buffer(STEPS, *whole),
        ]
        + [dma((STEPS, PIECES))] * 2
        + [dma((STEPS, len(FAR)))] * 2
        + [dma((STEPS, 2, GROUPS))] * 2
        + [dma((STEPS, RING))] * 6
        + [dma((6,)), dma((GROUPS,))],
        compiler_params=pltpu.CompilerParams(
            collective_id=0, has_side_effects=True, vmem_limit_bytes=56 * 1024 * 1024
        ),
    )(spectrum, wind_speed, wind_dir, flags, bin_table(lax.axis_size("bins"), here), row_table(rows))


def solution(mesh):
    return jax.shard_map(
        shards,
        mesh=mesh,
        in_specs=(P("bins", "lon", None), P("lon", None), P("lon", None), P("lon", None)),
        out_specs=P("bins", "lon", None),
        check_vma=False,
    )
```

```python
import math

import jax
import jax.numpy as jnp
import numpy as np
from jax import lax
from jax.experimental import pallas as pl
from jax.experimental.pallas import tpu as pltpu
from jax.sharding import PartitionSpec as P

NF = 32
ND = 36
STEPS = 2

wind_gain = 0.5
quad_gain = 0.3
break_gain = 0.3
ice_loss = 1.0
courant = 0.6

RING = 8
HALO = 9
BASE = 16
GROUP = 3
GROUPS = 6
LAG = 2
LEG = 2
PLUS = (-2.0, 15.0, -60.0, 20.0, 30.0, -3.0, 0.0)
MINUS = (0.0, 3.0, -30.0, -20.0, 60.0, -15.0, 2.0)

DIRECT = (
    (0, 0, 3, 2, -2), (0, 3, 3, 5, -2), (0, 6, 3, 8, -2), (0, 9, 3, 11, -2), (0, 12, 3, 14, -2), (0, 15, 1, 17, -2),
    (1, 16, 2, 6, 6),
)
SHARED = ((3, 12, 2, 0), (4, 14, 3, 2), (5, 17, 1, 5))
FAR = ((0, 16, 2, 0, -1), (1, 0, 3, 8, 1), (1, 3, 3, 11, -1), (1, 6, 3, 14, 1), (1, 9, 1, 17, -1))
KEPT_BACK = (1, 2, 4, 5, 6)
KEPT_FAR = (0,)
S0, F0 = len(DIRECT), len(DIRECT) + len(SHARED)
PIECES = F0 + len(FAR)
NEEDS = (
    ((F0, 0, S0, S0 + 1), (1, S0 + 2), (2, 6, F0 + 1), (F0 + 2,), (F0 + 3,), (F0 + 4,)),
    ((F0, S0), (0, 1, S0 + 1, S0 + 2), (2, 6, F0 + 1), (F0 + 2,), (F0 + 3,), (F0 + 4,)),
)

RATIO, COS, SIN, DAMP, UPPER, LOWER, EAST, WEST, NORTH, SOUTH = range(10)


def bin_table(places, here):
    index = np.arange(places * here).reshape(places, here)
    theta = (index // NF).astype(np.float32) * np.float32(2.0 * math.pi / ND)
    theta = theta.astype(np.float64)
    level = index % NF
    ratio = 1.05 ** (level - NF // 2.0)
    east = courant * 1.1 ** (-level.astype(np.float64)) * np.cos(theta)
    north = courant * 1.1 ** (-level.astype(np.float64)) * np.sin(theta)
    table = np.zeros((places, 16, 128), np.float32)
    values = (
        ratio,
        np.cos(theta),
        np.sin(theta),
        break_gain * ratio * ratio / (NF * ND),
        level + 2 < NF,
        level >= 2,
        np.maximum(east, 0.0) / -60.0,
        np.minimum(east, 0.0) / -60.0,
        np.maximum(north, 0.0) / -60.0,
        np.minimum(north, 0.0) / -60.0,
    )
    for quantity, value in enumerate(values):
        table[:, quantity, :here] = value
    return table


def row_table(rows):
    lines = np.arange(rows)
    coslat = np.cos((lines - rows / 2 + 0.5) * (0.25 * math.pi / 180.0))
    return np.broadcast_to(1.0 / coslat, (8, rows)).astype(np.float32)


def kernel(
    field_hbm, speed_hbm, heading_hbm, flags_hbm, bins_hbm, rows_hbm, out_ref,
    first, later, last, got, relay, wide, one, two, lon_taps, lat_taps, bins_ref, rows_ref, speed, heading, flags, gain_x, gain_y, open_sea, ice,
    part, part_in, mid, mid_in, total,
    send_sem, got_sem, leg_send, leg_recv, halo_send, halo_recv,
    a_send, a_recv, b_send, b_recv, c_send, c_recv, in_sem, out_sem,
):
    here, columns, rows = field_hbm.shape
    count, sectors = lax.axis_size("bins"), lax.axis_size("lon")
    place, sector = lax.axis_index("bins"), lax.axis_index("lon")
    ext = columns + 2 * BASE
    line, spot = place // RING, place % RING
    chunk = columns // RING
    def in_row(turn):
        return line * RING + (spot + turn) % RING

    def in_column(turn):
        return (line + turn) % RING * RING + spot

    def across(offset):
        return (place + offset + count) % count

    pair, far, core = place // 2, place % 2, sector % 2
    height = far * (sectors // 2) + sector // 2
    around_z = sectors

    def at(pair_offset, climb):
        new = (height + climb + around_z) % around_z
        new_pair = (pair + pair_offset + count // 2) % (count // 2)
        return {"bins": new_pair * 2 + new // (sectors // 2), "lon": new % (sectors // 2) * 2 + core}

    for step in range(STEPS):
        for rows_of in (pl.ds(0, BASE), pl.ds(BASE + columns, BASE)):
            wide[step, :, rows_of] = jnp.zeros((here, BASE, rows), jnp.float32)

    barrier = pltpu.get_barrier_semaphore()
    partners = [{"bins": across(s * o)} for o in (2, 6, 8) for s in (1, -1)]
    partners += [at(o, s * LEG) for o in (-3, -1, 0, 1, 3) for s in (1, -1)]
    partners += [{"bins": in_row(t)} for t in range(1, RING)]
    partners += [{"bins": in_column(t)} for t in range(1, RING)]
    partners += [{"lon": (sector + s + sectors) % sectors} for s in (1, -1)]
    for partner in partners:
        pl.semaphore_signal(barrier, inc=1, device_id=partner, device_id_type=pl.DeviceIdType.MESH)

    def send(src, dst, send_sem, recv_sem, device):
        return pltpu.make_async_remote_copy(
            src_ref=src, dst_ref=dst, send_sem=send_sem, recv_sem=recv_sem,
            device_id=device, device_id_type=pl.DeviceIdType.MESH,
        )

    def source_of(step):
        return field_hbm if step == 0 else later

    def field_of(step):
        return first if step == 0 else later

    def direct(step, piece):
        kind, b, bins, slot, places = DIRECT[piece]
        return send(
            source_of(step).at[pl.ds(b, bins)], got.at[step, kind, pl.ds(slot, bins)],
            send_sem.at[step, piece], got_sem.at[step, piece], {"bins": across(places)},
        )

    def shared(step, piece):
        _, slot, bins, new_slot = SHARED[piece]
        return send(
            got.at[step, 0, pl.ds(slot, bins)], got.at[step, 1, pl.ds(new_slot, bins)],
            send_sem.at[step, S0 + piece], got_sem.at[step, S0 + piece], {"bins": across(8)},
        )

    def leg(step, piece):
        kind, b, bins, _, way = FAR[piece]
        offset = 1 + 2 * far if kind else far - 1
        return send(
            source_of(step).at[pl.ds(b, bins)], relay.at[step, pl.ds(b, bins)],
            leg_send.at[step, piece], leg_recv.at[step, piece], at(offset, way * LEG),
        )

    def second_leg(step, piece):
        kind, b, bins, slot, way = FAR[piece]
        source_far = (height - way * LEG + around_z) % around_z // (sectors // 2)
        return send(
            relay.at[step, pl.ds(b, bins)], got.at[step, kind, pl.ds(slot, bins)],
            send_sem.at[step, F0 + piece], got_sem.at[step, F0 + piece], at(1 - source_far if kind else 0, way * LEG),
        )

    def arrival(step, piece):
        if piece < S0:
            return direct(step, piece)
        if piece < F0:
            return shared(step, piece - S0)
        return second_leg(step, piece - F0)

    def pass_on_far(step, pieces):
        for piece in pieces:
            leg(step, piece).wait_recv()
            second_leg(step, piece).start()

    def pass_on_shared(step):
        for piece, (before, *_) in enumerate(SHARED):
            direct(step, before).wait_recv()
            shared(step, piece).start()

    def halo_copy(step, group, side):
        if side == 0:
            src, dst, turn = BASE + columns - HALO, BASE - HALO, 1
        else:
            src, dst, turn = BASE, BASE + columns, -1
        ext = wide.at[step, pl.ds(group * GROUP, GROUP)]
        return send(
            ext.at[:, pl.ds(src, HALO)], ext.at[:, pl.ds(dst, HALO)],
            halo_send.at[step, side, group], halo_recv.at[step, side, group],
            {"lon": (sector + turn + sectors) % sectors},
        )

    def a_copy(step, turn):
        start = pl.multiple_of((spot + turn) % RING * chunk, chunk)
        return send(part.at[step, pl.ds(start, chunk)], part_in.at[step, turn], a_send.at[step, turn], a_recv.at[step, turn], {"bins": in_row(turn)})

    def b_copy(step, turn):
        return send(mid.at[step], mid_in.at[step, turn], b_send.at[step, turn], b_recv.at[step, turn], {"bins": in_column(turn)})

    def c_copy(step, turn):
        start = pl.multiple_of(spot * chunk, chunk)
        mine = total.at[step, pl.ds(start, chunk)]
        return send(mine, mine, c_send.at[step, turn], c_recv.at[step, turn], {"bins": in_row(turn)})

    def c_from(step, turn):
        start = pl.multiple_of((spot + RING - turn) % RING * chunk, chunk)
        theirs = total.at[step, pl.ds(start, chunk)]
        return send(theirs, theirs, c_send.at[step, turn], c_recv.at[step, turn], {"bins": in_row(turn)})

    def square(b, values):
        scaled = bins_ref[RATIO, b] * values
        return scaled * scaled

    def spread_a(step):
        for turn in range(1, RING):
            a_copy(step, turn).start()

    def spread_b(step):
        start = pl.multiple_of(spot * chunk, chunk)
        so_far = part[step, pl.ds(start, chunk)]
        for turn in range(1, RING):
            a_copy(step, turn).wait_recv()
            so_far += part_in[step, turn]
        mid[step] = so_far
        for turn in range(1, RING):
            b_copy(step, turn).start()

    def spread_c(step):
        start = pl.multiple_of(spot * chunk, chunk)
        so_far = mid[step]
        for turn in range(1, RING):
            b_copy(step, turn).wait_recv()
            so_far += mid_in[step, turn]
        total[step, pl.ds(start, chunk)] = so_far
        for turn in range(1, RING):
            c_copy(step, turn).start()

    def spread_end(step):
        for turn in range(1, RING):
            c_from(step, turn).wait_recv()

    def source(step, b):
        energy = field_of(step)[b]
        above = got[step, 0, b] * bins_ref[UPPER, b]
        below = got[step, 1, b] * bins_ref[LOWER, b]
        ratio = bins_ref[RATIO, b]
        wind = jnp.maximum(bins_ref[COS, b] * gain_x[...] + bins_ref[SIN, b] * gain_y[...], 0.0)
        quad = quad_gain * (energy * (above + below) - 2.0 * above * below)
        grown = energy + energy * (ratio * (wind + quad))
        top = jnp.where(open_sea[...] > 0.0, grown, energy)
        bottom = 1.0 + bins_ref[DAMP, b] * total[step] + ice[...]
        wide[step, b, pl.ds(BASE, columns)] = jnp.where(flags[...] == 0, 0.0, top / bottom)

    def halves(values):
        high = values.astype(jnp.bfloat16)
        return high, (values - high.astype(jnp.float32)).astype(jnp.bfloat16)

    def rates(fields, bins, signs, rows_out):
        parts = [halves(field) for field in fields]
        along_lat = jnp.dot(
            jnp.concatenate([jnp.concatenate(pair_of, axis=1) for pair_of in parts], axis=0),
            lat_taps[...], preferred_element_type=jnp.float32,
        )
        results = []
        for i, (field, pair_of, b) in enumerate(zip(fields, parts, bins)):
            along_lon = jnp.dot(
                lon_taps[signs[i], rows_out], jnp.concatenate(pair_of, axis=0), preferred_element_type=jnp.float32
            )
            start, end = i * ext + rows_out.start, i * ext + rows_out.start + rows_out.size
            east = (bins_ref[EAST, b] + bins_ref[WEST, b]) * rows_ref[0:1]
            results.append(
                field[rows_out.start : rows_out.start + rows_out.size]
                + along_lon * east
                + along_lat[start:end, :rows] * bins_ref[NORTH, b]
                + along_lat[start:end, rows:] * bins_ref[SOUTH, b]
            )
        return results

    def advance(step, groups_now):
        bins = [group * GROUP + j for group in groups_now for j in range(GROUP)]
        directions = [(place * here + b) // NF for b in bins]
        signs = [(d + ND // 4) // (ND // 2) % 2 for d in directions]
        every, inner = pl.ds(0, ext), pl.ds(BASE, columns)
        for j, values in enumerate(rates([wide[step, b] for b in bins], bins, signs, every)):
            one[j] = values
        for j, values in enumerate(rates([one[j] for j in range(len(bins))], bins, signs, every)):
            two[j] = 0.75 * wide[step, bins[j]] + 0.25 * values
        for j, values in enumerate(rates([two[j] for j in range(len(bins))], bins, signs, inner)):
            moved = wide[step, bins[j], inner] * (1.0 / 3.0) + (2.0 / 3.0) * values
            moved = jnp.where(flags[...] == 0, 0.0, moved)
            if step < STEPS - 1:
                later[bins[j]] = moved
                part[step + 1] += square(bins[j], moved)
            else:
                last[bins[j]] = moved

    def result_copy(group):
        some = pl.ds(group * GROUP, GROUP)
        return pltpu.make_async_copy(last.at[some], out_ref.at[some], out_sem.at[group])

    def send_group(step, group):
        for k in range(GROUPS):
            @pl.when(group == k)
            def _(k=k):
                mine = range(k * GROUP, (k + 1) * GROUP)
                for piece, (_, b, *_) in enumerate(FAR):
                    if b in mine and piece not in KEPT_FAR:
                        leg(step, piece).start()
                for piece, (_, b, *_) in enumerate(DIRECT):
                    if b in mine and piece not in KEPT_BACK:
                        direct(step, piece).start()

    inputs = [(field_hbm, first), (speed_hbm, speed), (heading_hbm, heading), (flags_hbm, flags),
              (bins_hbm.at[place], bins_ref), (rows_hbm, rows_ref)]
    inputs = [pltpu.make_async_copy(src, dst, in_sem.at[i]) for i, (src, dst) in enumerate(inputs)]
    for copy in inputs:
        copy.start()

    def band(shape, along, across_it, taps):
        offset = lax.broadcasted_iota(jnp.int32, shape, along) - lax.broadcasted_iota(jnp.int32, shape, across_it)
        matrix = jnp.zeros(shape, jnp.float32)
        for j, tap in enumerate(taps):
            matrix = jnp.where(offset == j - 3, tap, matrix)
        return matrix.astype(jnp.bfloat16)

    for sign, taps in enumerate((PLUS, MINUS)):
        lon_band, lat_band = band((ext, ext), 1, 0, taps), band((rows, rows), 0, 1, taps)
        lon_taps[sign] = jnp.concatenate([lon_band, lon_band], axis=1)
        for half in range(2):
            lat_taps[pl.ds(half * rows, rows), pl.ds(sign * rows, rows)] = lat_band
    for step in range(1, STEPS):
        part[step] = jnp.zeros((columns, rows), jnp.float32)
    for copy in inputs[4:] + inputs[:1]:
        copy.wait()
    part[0] = lax.fori_loop(0, here, lambda b, so_far: so_far + square(b, first[b]), jnp.zeros((columns, rows), jnp.float32))
    pl.semaphore_wait(barrier, len(partners))

    spread_a(0)
    for piece in range(len(FAR)):
        leg(0, piece).start()
    direct(0, 3).start()
    for copy in inputs[1:4]:
        copy.wait()
    gain = wind_gain * 0.1 * speed[...]
    gain_x[...] = gain * jnp.cos(heading[...])
    gain_y[...] = gain * jnp.sin(heading[...])
    open_sea[...] = jnp.where(flags[...] == 1, 1.0, 0.0)
    ice[...] = jnp.where(flags[...] == 2, ice_loss, 0.0)
    spread_b(0)
    for piece in (4, 5, 0, 6):
        direct(0, piece).start()
    pass_on_far(0, (0, 1, 2))
    spread_c(0)
    direct(0, 1).start()
    pass_on_far(0, (3, 4))
    pass_on_shared(0)
    direct(0, 2).start()
    spread_end(0)

    def source_group(step, group):
        for k in range(GROUPS):
            @pl.when(group == k)
            def _(k=k):
                for piece in NEEDS[step][k]:
                    arrival(step, piece).wait_recv()

        for j in range(GROUP):
            source(step, group * GROUP + j)
        for side in range(2):
            halo_copy(step, group, side).start()

    def halos_there(step, group):
        for side in range(2):
            halo_copy(step, group, side).wait_recv()

    @pl.loop(0, GROUPS + LAG)
    def _(g):
        @pl.when(g >= LAG)
        def _():
            group = g - LAG
            halos_there(0, group)
            advance(0, (group,))
            send_group(1, group)

        @pl.when(g < GROUPS)
        def _():
            source_group(0, g)

    spread_a(1)
    leg(1, 0).start()
    for piece in (4, 5, 6):
        direct(1, piece).start()
    pass_on_far(1, (1, 2))
    spread_b(1)
    pass_on_far(1, (3, 4))
    pass_on_shared(1)
    spread_c(1)
    for piece in (1, 2):
        direct(1, piece).start()
    pass_on_far(1, (0,))
    spread_end(1)


    @pl.loop(0, GROUPS // 2 + 1)
    def _(g):
        @pl.when(g < GROUPS // 2)
        def _():
            for j in range(2):
                source_group(1, (2 * g + j + 1) % GROUPS)

        @pl.when(g >= 1)
        def _():
            pair_now = [(2 * g + j - 1) % GROUPS for j in range(2)]
            for group in pair_now:
                halos_there(1, group)
            advance(1, pair_now)
            for group in pair_now:
                result_copy(group).start()

    for step in range(STEPS):
        for turn in range(1, RING):
            a_copy(step, turn).wait_send()
            b_copy(step, turn).wait_send()
            c_copy(step, turn).wait_send()
        for piece in range(PIECES):
            arrival(step, piece).wait_send()
        for piece in range(len(FAR)):
            leg(step, piece).wait_send()

        @pl.loop(0, GROUPS)
        def _(group, step=step):
            for side in range(2):
                halo_copy(step, group, side).wait_send()

    @pl.loop(0, GROUPS)
    def _(group):
        result_copy(group).wait()


def shards(spectrum, wind_speed, wind_dir, flags):
    here, columns, rows = spectrum.shape
    whole = (columns, rows)
    chunk = columns // RING
    ext = columns + 2 * BASE
    hbm = pl.BlockSpec(memory_space=pl.ANY)
    dma = pltpu.SemaphoreType.DMA

    def buffer(*shape):
        return pltpu.VMEM(shape, jnp.float32)

    return pl.pallas_call(
        kernel,
        out_shape=jax.ShapeDtypeStruct(spectrum.shape, jnp.float32),
        in_specs=[hbm] * 6,
        out_specs=hbm,
        scratch_shapes=[
            buffer(here, *whole),
            buffer(here, *whole),
            buffer(here, *whole),
            buffer(STEPS, 2, here, *whole),
            buffer(STEPS, here, *whole),
            buffer(STEPS, here, ext, rows),
            buffer(2 * GROUP, ext, rows),
            buffer(2 * GROUP, ext, rows),
            pltpu.VMEM((2, ext, 2 * ext), jnp.bfloat16),
            pltpu.VMEM((2 * rows, 2 * rows), jnp.bfloat16),
            pltpu.SMEM((16, 128), jnp.float32),
            buffer(8, rows),
            buffer(*whole),
            buffer(*whole),
            pltpu.VMEM(whole, jnp.int32),
            buffer(*whole),
            buffer(*whole),
            buffer(*whole),
            buffer(*whole),
            buffer(STEPS, *whole),
            buffer(STEPS, RING, chunk, rows),
            buffer(STEPS, chunk, rows),
            buffer(STEPS, RING, chunk, rows),
            buffer(STEPS, *whole),
        ]
        + [dma((STEPS, PIECES))] * 2
        + [dma((STEPS, len(FAR)))] * 2
        + [dma((STEPS, 2, GROUPS))] * 2
        + [dma((STEPS, RING))] * 6
        + [dma((6,)), dma((GROUPS,))],
        compiler_params=pltpu.CompilerParams(
            collective_id=0, has_side_effects=True, vmem_limit_bytes=56 * 1024 * 1024
        ),
    )(spectrum, wind_speed, wind_dir, flags, bin_table(lax.axis_size("bins"), here), row_table(rows))


def solution(mesh):
    return jax.shard_map(
        shards,
        mesh=mesh,
        in_specs=(P("bins", "lon", None), P("lon", None), P("lon", None), P("lon", None)),
        out_specs=P("bins", "lon", None),
        check_vma=False,
    )
```

```python
import math

import jax
import jax.numpy as jnp
import numpy as np
from jax import lax
from jax.experimental import pallas as pl
from jax.experimental.pallas import tpu as pltpu
from jax.sharding import PartitionSpec as P

NF = 32
ND = 36
STEPS = 2

wind_gain = 0.5
quad_gain = 0.3
break_gain = 0.3
ice_loss = 1.0
courant = 0.6

RING = 8
HALO = 9
BASE = 16
GROUP = 3
GROUPS = 6
LAG = 2
LEG = 2
PLUS = (-2.0, 15.0, -60.0, 20.0, 30.0, -3.0, 0.0)
MINUS = (0.0, 3.0, -30.0, -20.0, 60.0, -15.0, 2.0)

DIRECT = (
    (0, 0, 3, 2, -2), (0, 3, 3, 5, -2), (0, 6, 3, 8, -2), (0, 9, 3, 11, -2), (0, 12, 3, 14, -2), (0, 15, 1, 17, -2),
    (1, 16, 2, 6, 6),
)
SHARED = ((3, 12, 2, 0), (4, 14, 3, 2), (5, 17, 1, 5))
FAR = ((0, 16, 2, 0, -1), (1, 0, 3, 8, 1), (1, 3, 3, 11, -1), (1, 6, 3, 14, 1), (1, 9, 1, 17, -1))
KEPT_BACK = (1, 2, 4, 5, 6)
LATE_X = 3
KEPT_FAR = (0,)
S0, F0 = len(DIRECT), len(DIRECT) + len(SHARED)
PIECES = F0 + len(FAR)
NEEDS = (
    ((F0, 0, S0, S0 + 1), (1, S0 + 2), (2, 6, F0 + 1), (F0 + 2,), (F0 + 3,), (F0 + 4,)),
    ((F0, S0), (0, 1, S0 + 1, S0 + 2), (2, 6, F0 + 1), (F0 + 2,), (F0 + 3,), (F0 + 4,)),
)

RATIO, COS, SIN, DAMP, UPPER, LOWER, EAST, WEST, NORTH, SOUTH = range(10)


def bin_table(places, here):
    index = np.arange(places * here).reshape(places, here)
    theta = (index // NF).astype(np.float32) * np.float32(2.0 * math.pi / ND)
    theta = theta.astype(np.float64)
    level = index % NF
    ratio = 1.05 ** (level - NF // 2.0)
    east = courant * 1.1 ** (-level.astype(np.float64)) * np.cos(theta)
    north = courant * 1.1 ** (-level.astype(np.float64)) * np.sin(theta)
    table = np.zeros((places, 16, 128), np.float32)
    values = (
        ratio,
        np.cos(theta),
        np.sin(theta),
        break_gain * ratio * ratio / (NF * ND),
        level + 2 < NF,
        level >= 2,
        np.maximum(east, 0.0) / -60.0,
        np.minimum(east, 0.0) / -60.0,
        np.maximum(north, 0.0) / -60.0,
        np.minimum(north, 0.0) / -60.0,
    )
    for quantity, value in enumerate(values):
        table[:, quantity, :here] = value
    return table


def row_table(rows):
    lines = np.arange(rows)
    coslat = np.cos((lines - rows / 2 + 0.5) * (0.25 * math.pi / 180.0))
    return np.broadcast_to(1.0 / coslat, (8, rows)).astype(np.float32)


def kernel(
    field_hbm, speed_hbm, heading_hbm, flags_hbm, bins_hbm, rows_hbm, out_ref,
    first, later, last, got, relay, wide, one, two, lon_taps, lat_taps, bins_ref, rows_ref, speed, heading, flags, gain_x, gain_y, open_sea, ice,
    part, part_in, mid, mid_in, total,
    send_sem, got_sem, leg_send, leg_recv, halo_send, halo_recv,
    a_send, a_recv, b_send, b_recv, c_send, c_recv, in_sem, out_sem,
):
    here, columns, rows = field_hbm.shape
    count, sectors = lax.axis_size("bins"), lax.axis_size("lon")
    place, sector = lax.axis_index("bins"), lax.axis_index("lon")
    ext = columns + 2 * BASE
    line, spot = place // RING, place % RING
    chunk = columns // RING
    def in_row(turn):
        return line * RING + (spot + turn) % RING

    def in_column(turn):
        return (line + turn) % RING * RING + spot

    def across(offset):
        return (place + offset + count) % count

    pair, far, core = place // 2, place % 2, sector % 2
    height = far * (sectors // 2) + sector // 2
    around_z = sectors

    def at(pair_offset, climb):
        new = (height + climb + around_z) % around_z
        new_pair = (pair + pair_offset + count // 2) % (count // 2)
        return {"bins": new_pair * 2 + new // (sectors // 2), "lon": new % (sectors // 2) * 2 + core}

    for step in range(STEPS):
        for rows_of in (pl.ds(0, BASE), pl.ds(BASE + columns, BASE)):
            wide[step, :, rows_of] = jnp.zeros((here, BASE, rows), jnp.float32)

    barrier = pltpu.get_barrier_semaphore()
    partners = [{"bins": across(s * o)} for o in (2, 6, 8) for s in (1, -1)]
    partners += [at(o, s * LEG) for o in (-3, -1, 0, 1, 3) for s in (1, -1)]
    partners += [{"bins": in_row(t)} for t in range(1, RING)]
    partners += [{"bins": in_column(t)} for t in range(1, RING)]
    partners += [{"lon": (sector + s + sectors) % sectors} for s in (1, -1)]
    for partner in partners:
        pl.semaphore_signal(barrier, inc=1, device_id=partner, device_id_type=pl.DeviceIdType.MESH)

    def send(src, dst, send_sem, recv_sem, device):
        return pltpu.make_async_remote_copy(
            src_ref=src, dst_ref=dst, send_sem=send_sem, recv_sem=recv_sem,
            device_id=device, device_id_type=pl.DeviceIdType.MESH,
        )

    def source_of(step):
        return field_hbm if step == 0 else later

    def field_of(step):
        return first if step == 0 else later

    def direct(step, piece):
        kind, b, bins, slot, places = DIRECT[piece]
        return send(
            source_of(step).at[pl.ds(b, bins)], got.at[step, kind, pl.ds(slot, bins)],
            send_sem.at[step, piece], got_sem.at[step, piece], {"bins": across(places)},
        )

    def shared(step, piece):
        _, slot, bins, new_slot = SHARED[piece]
        return send(
            got.at[step, 0, pl.ds(slot, bins)], got.at[step, 1, pl.ds(new_slot, bins)],
            send_sem.at[step, S0 + piece], got_sem.at[step, S0 + piece], {"bins": across(8)},
        )

    def leg(step, piece):
        kind, b, bins, _, way = FAR[piece]
        offset = (1 + 2 * far if piece < LATE_X else 1 - far) if kind else far - 1
        return send(
            source_of(step).at[pl.ds(b, bins)], relay.at[step, pl.ds(b, bins)],
            leg_send.at[step, piece], leg_recv.at[step, piece], at(offset, way * LEG),
        )

    def second_leg(step, piece):
        kind, b, bins, slot, way = FAR[piece]
        source_far = (height - way * LEG + around_z) % around_z // (sectors // 2)
        offset = (1 - source_far if piece < LATE_X else 1 + 2 * source_far) if kind else 0
        return send(
            relay.at[step, pl.ds(b, bins)], got.at[step, kind, pl.ds(slot, bins)],
            send_sem.at[step, F0 + piece], got_sem.at[step, F0 + piece], at(offset, way * LEG),
        )

    def arrival(step, piece):
        if piece < S0:
            return direct(step, piece)
        if piece < F0:
            return shared(step, piece - S0)
        return second_leg(step, piece - F0)

    def pass_on_far(step, pieces):
        for piece in pieces:
            leg(step, piece).wait_recv()
            second_leg(step, piece).start()

    def pass_on_shared(step):
        for piece, (before, *_) in enumerate(SHARED):
            direct(step, before).wait_recv()
            shared(step, piece).start()

    def halo_copy(step, group, side):
        if side == 0:
            src, dst, turn = BASE + columns - HALO, BASE - HALO, 1
        else:
            src, dst, turn = BASE, BASE + columns, -1
        ext = wide.at[step, pl.ds(group * GROUP, GROUP)]
        return send(
            ext.at[:, pl.ds(src, HALO)], ext.at[:, pl.ds(dst, HALO)],
            halo_send.at[step, side, group], halo_recv.at[step, side, group],
            {"lon": (sector + turn + sectors) % sectors},
        )

    def a_copy(step, turn):
        start = pl.multiple_of((spot + turn) % RING * chunk, chunk)
        return send(part.at[step, pl.ds(start, chunk)], part_in.at[step, turn], a_send.at[step, turn], a_recv.at[step, turn], {"bins": in_row(turn)})

    def b_copy(step, turn):
        return send(mid.at[step], mid_in.at[step, turn], b_send.at[step, turn], b_recv.at[step, turn], {"bins": in_column(turn)})

    def c_copy(step, turn):
        start = pl.multiple_of(spot * chunk, chunk)
        mine = total.at[step, pl.ds(start, chunk)]
        return send(mine, mine, c_send.at[step, turn], c_recv.at[step, turn], {"bins": in_row(turn)})

    def c_from(step, turn):
        start = pl.multiple_of((spot + RING - turn) % RING * chunk, chunk)
        theirs = total.at[step, pl.ds(start, chunk)]
        return send(theirs, theirs, c_send.at[step, turn], c_recv.at[step, turn], {"bins": in_row(turn)})

    def square(b, values):
        scaled = bins_ref[RATIO, b] * values
        return scaled * scaled

    def spread_a(step):
        for turn in range(1, RING):
            a_copy(step, turn).start()

    def spread_b(step):
        start = pl.multiple_of(spot * chunk, chunk)
        so_far = part[step, pl.ds(start, chunk)]
        for turn in range(1, RING):
            a_copy(step, turn).wait_recv()
            so_far += part_in[step, turn]
        mid[step] = so_far
        for turn in range(1, RING):
            b_copy(step, turn).start()

    def spread_c(step):
        start = pl.multiple_of(spot * chunk, chunk)
        so_far = mid[step]
        for turn in range(1, RING):
            b_copy(step, turn).wait_recv()
            so_far += mid_in[step, turn]
        total[step, pl.ds(start, chunk)] = so_far
        for turn in range(1, RING):
            c_copy(step, turn).start()

    def spread_end(step):
        for turn in range(1, RING):
            c_from(step, turn).wait_recv()

    def source(step, b):
        energy = field_of(step)[b]
        above = got[step, 0, b] * bins_ref[UPPER, b]
        below = got[step, 1, b] * bins_ref[LOWER, b]
        ratio = bins_ref[RATIO, b]
        wind = jnp.maximum(bins_ref[COS, b] * gain_x[...] + bins_ref[SIN, b] * gain_y[...], 0.0)
        quad = quad_gain * (energy * (above + below) - 2.0 * above * below)
        grown = energy + energy * (ratio * (wind + quad))
        top = jnp.where(open_sea[...] > 0.0, grown, energy)
        bottom = 1.0 + bins_ref[DAMP, b] * total[step] + ice[...]
        wide[step, b, pl.ds(BASE, columns)] = jnp.where(flags[...] == 0, 0.0, top / bottom)

    def halves(values):
        high = values.astype(jnp.bfloat16)
        return high, (values - high.astype(jnp.float32)).astype(jnp.bfloat16)

    def rates(fields, bins, signs, rows_out):
        parts = [halves(field) for field in fields]
        along_lat = jnp.dot(
            jnp.concatenate([jnp.concatenate(pair_of, axis=1) for pair_of in parts], axis=0),
            lat_taps[...], preferred_element_type=jnp.float32,
        )
        results = []
        for i, (field, pair_of, b) in enumerate(zip(fields, parts, bins)):
            along_lon = jnp.dot(
                lon_taps[signs[i], rows_out], jnp.concatenate(pair_of, axis=0), preferred_element_type=jnp.float32
            )
            start, end = i * ext + rows_out.start, i * ext + rows_out.start + rows_out.size
            east = (bins_ref[EAST, b] + bins_ref[WEST, b]) * rows_ref[0:1]
            results.append(
                field[rows_out.start : rows_out.start + rows_out.size]
                + along_lon * east
                + along_lat[start:end, :rows] * bins_ref[NORTH, b]
                + along_lat[start:end, rows:] * bins_ref[SOUTH, b]
            )
        return results

    def advance(step, groups_now):
        bins = [group * GROUP + j for group in groups_now for j in range(GROUP)]
        directions = [(place * here + b) // NF for b in bins]
        signs = [(d + ND // 4) // (ND // 2) % 2 for d in directions]
        every, inner = pl.ds(0, ext), pl.ds(BASE, columns)
        for j, values in enumerate(rates([wide[step, b] for b in bins], bins, signs, every)):
            one[j] = values
        for j, values in enumerate(rates([one[j] for j in range(len(bins))], bins, signs, every)):
            two[j] = 0.75 * wide[step, bins[j]] + 0.25 * values
        for j, values in enumerate(rates([two[j] for j in range(len(bins))], bins, signs, inner)):
            moved = wide[step, bins[j], inner] * (1.0 / 3.0) + (2.0 / 3.0) * values
            moved = jnp.where(flags[...] == 0, 0.0, moved)
            if step < STEPS - 1:
                later[bins[j]] = moved
                part[step + 1] += square(bins[j], moved)
            else:
                last[bins[j]] = moved

    def result_copy(group):
        some = pl.ds(group * GROUP, GROUP)
        return pltpu.make_async_copy(last.at[some], out_ref.at[some], out_sem.at[group])

    def send_group(step, group):
        for k in range(GROUPS):
            @pl.when(group == k)
            def _(k=k):
                mine = range(k * GROUP, (k + 1) * GROUP)
                for piece, (_, b, *_) in enumerate(FAR):
                    if b in mine and piece not in KEPT_FAR:
                        leg(step, piece).start()
                for piece, (_, b, *_) in enumerate(DIRECT):
                    if b in mine and piece not in KEPT_BACK:
                        direct(step, piece).start()

    inputs = [(field_hbm, first), (speed_hbm, speed), (heading_hbm, heading), (flags_hbm, flags),
              (bins_hbm.at[place], bins_ref), (rows_hbm, rows_ref)]
    inputs = [pltpu.make_async_copy(src, dst, in_sem.at[i]) for i, (src, dst) in enumerate(inputs)]
    for copy in inputs:
        copy.start()

    def band(shape, along, across_it, taps):
        offset = lax.broadcasted_iota(jnp.int32, shape, along) - lax.broadcasted_iota(jnp.int32, shape, across_it)
        matrix = jnp.zeros(shape, jnp.float32)
        for j, tap in enumerate(taps):
            matrix = jnp.where(offset == j - 3, tap, matrix)
        return matrix.astype(jnp.bfloat16)

    for sign, taps in enumerate((PLUS, MINUS)):
        lon_band, lat_band = band((ext, ext), 1, 0, taps), band((rows, rows), 0, 1, taps)
        lon_taps[sign] = jnp.concatenate([lon_band, lon_band], axis=1)
        for half in range(2):
            lat_taps[pl.ds(half * rows, rows), pl.ds(sign * rows, rows)] = lat_band
    for step in range(1, STEPS):
        part[step] = jnp.zeros((columns, rows), jnp.float32)
    for copy in inputs[4:] + inputs[:1]:
        copy.wait()
    part[0] = lax.fori_loop(0, here, lambda b, so_far: so_far + square(b, first[b]), jnp.zeros((columns, rows), jnp.float32))
    pl.semaphore_wait(barrier, len(partners))

    spread_a(0)
    for piece in range(len(FAR)):
        leg(0, piece).start()
    direct(0, 3).start()
    for copy in inputs[1:4]:
        copy.wait()
    gain = wind_gain * 0.1 * speed[...]
    gain_x[...] = gain * jnp.cos(heading[...])
    gain_y[...] = gain * jnp.sin(heading[...])
    open_sea[...] = jnp.where(flags[...] == 1, 1.0, 0.0)
    ice[...] = jnp.where(flags[...] == 2, ice_loss, 0.0)
    spread_b(0)
    for piece in (4, 5, 0, 6, 1):
        direct(0, piece).start()
    pass_on_far(0, (0, 1, 2))
    spread_c(0)
    direct(0, 2).start()
    pass_on_far(0, (3, 4))
    pass_on_shared(0)
    spread_end(0)

    def source_group(step, group):
        for k in range(GROUPS):
            @pl.when(group == k)
            def _(k=k):
                for piece in NEEDS[step][k]:
                    arrival(step, piece).wait_recv()

        for j in range(GROUP):
            source(step, group * GROUP + j)
        for side in range(2):
            halo_copy(step, group, side).start()

    def halos_there(step, group):
        for side in range(2):
            halo_copy(step, group, side).wait_recv()

    @pl.loop(0, GROUPS + LAG)
    def _(g):
        @pl.when(g >= LAG)
        def _():
            group = g - LAG
            halos_there(0, group)
            advance(0, (group,))
            send_group(1, group)

        @pl.when(g < GROUPS)
        def _():
            source_group(0, g)

    spread_a(1)
    leg(1, 0).start()
    for piece in (4, 5, 6, 1):
        direct(1, piece).start()
    pass_on_far(1, (1, 2))
    spread_b(1)
    direct(1, 2).start()
    pass_on_far(1, (3, 4))
    pass_on_shared(1)
    spread_c(1)
    pass_on_far(1, (0,))
    spread_end(1)


    @pl.loop(0, GROUPS // 2 + 1)
    def _(g):
        @pl.when(g < GROUPS // 2)
        def _():
            for j in range(2):
                source_group(1, (2 * g + j + 1) % GROUPS)

        @pl.when(g >= 1)
        def _():
            pair_now = [(2 * g + j - 1) % GROUPS for j in range(2)]
            for group in pair_now:
                halos_there(1, group)
            advance(1, pair_now)
            for group in pair_now:
                result_copy(group).start()

    for step in range(STEPS):
        for turn in range(1, RING):
            a_copy(step, turn).wait_send()
            b_copy(step, turn).wait_send()
            c_copy(step, turn).wait_send()
        for piece in range(PIECES):
            arrival(step, piece).wait_send()
        for piece in range(len(FAR)):
            leg(step, piece).wait_send()

        @pl.loop(0, GROUPS)
        def _(group, step=step):
            for side in range(2):
                halo_copy(step, group, side).wait_send()

    @pl.loop(0, GROUPS)
    def _(group):
        result_copy(group).wait()


def shards(spectrum, wind_speed, wind_dir, flags):
    here, columns, rows = spectrum.shape
    whole = (columns, rows)
    chunk = columns // RING
    ext = columns + 2 * BASE
    hbm = pl.BlockSpec(memory_space=pl.ANY)
    dma = pltpu.SemaphoreType.DMA

    def buffer(*shape):
        return pltpu.VMEM(shape, jnp.float32)

    return pl.pallas_call(
        kernel,
        out_shape=jax.ShapeDtypeStruct(spectrum.shape, jnp.float32),
        in_specs=[hbm] * 6,
        out_specs=hbm,
        scratch_shapes=[
            buffer(here, *whole),
            buffer(here, *whole),
            buffer(here, *whole),
            buffer(STEPS, 2, here, *whole),
            buffer(STEPS, here, *whole),
            buffer(STEPS, here, ext, rows),
            buffer(2 * GROUP, ext, rows),
            buffer(2 * GROUP, ext, rows),
            pltpu.VMEM((2, ext, 2 * ext), jnp.bfloat16),
            pltpu.VMEM((2 * rows, 2 * rows), jnp.bfloat16),
            pltpu.SMEM((16, 128), jnp.float32),
            buffer(8, rows),
            buffer(*whole),
            buffer(*whole),
            pltpu.VMEM(whole, jnp.int32),
            buffer(*whole),
            buffer(*whole),
            buffer(*whole),
            buffer(*whole),
            buffer(STEPS, *whole),
            buffer(STEPS, RING, chunk, rows),
            buffer(STEPS, chunk, rows),
            buffer(STEPS, RING, chunk, rows),
            buffer(STEPS, *whole),
        ]
        + [dma((STEPS, PIECES))] * 2
        + [dma((STEPS, len(FAR)))] * 2
        + [dma((STEPS, 2, GROUPS))] * 2
        + [dma((STEPS, RING))] * 6
        + [dma((6,)), dma((GROUPS,))],
        compiler_params=pltpu.CompilerParams(
            collective_id=0, has_side_effects=True, vmem_limit_bytes=56 * 1024 * 1024
        ),
    )(spectrum, wind_speed, wind_dir, flags, bin_table(lax.axis_size("bins"), here), row_table(rows))


def solution(mesh):
    return jax.shard_map(
        shards,
        mesh=mesh,
        in_specs=(P("bins", "lon", None), P("lon", None), P("lon", None), P("lon", None)),
        out_specs=P("bins", "lon", None),
        check_vma=False,
    )
```
